32 devices in a mesh: dp: 4 (over y, x), seq: 8 (over z, core).
Axes of the slice: x: 2, y: 2, z: 4, core: 2. Of those that a mesh axis runs over, the one named last changes fastest.
Arguments:
- inputs: bfloat16 [8, 2048, 512], P('dp', 'seq'), may hold values from -6 to 6
- lengths: int32 [8], P('dp'), may hold values from 1 to 2048, as said below
- ln_gain: float32 [512], P(('dp', 'seq')), may hold values from 0.5 to 1.5
- ln_bias: float32 [512], P(('dp', 'seq')), may hold values from -4 to 4
- lam_log: float32 [512, 64], P(('dp', 'seq'))
- lam_im: float32 [512, 64], P(('dp', 'seq')), may hold values from -3.140625 to 3.140625
- log_dt: float32 [512], P(('dp', 'seq')), may hold values from -0.35 to 0.35
- mix_weight: float32 [512, 128], P(('dp', 'seq'))
- skip: float32 [512], P(('dp', 'seq')), may hold values from -6 to 6
- glu_weight: bfloat16 [512, 1024], P(('dp', 'seq')), may hold values from -0.25 to 0.25
- glu_bias: float32 [1024], P(('dp', 'seq')), may hold values from -4 to 4
- out_grad: bfloat16 [8, 2048, 512], P('dp', 'seq'), may hold values from -6 to 6
Outputs:
- output: bfloat16 [8, 2048, 512], P('dp', 'seq')
- input_grad: bfloat16 [8, 2048, 512], P('dp', 'seq')
- ln_gain_grad: float32 [512], P(('dp', 'seq'))
- ln_bias_grad: float32 [512], P(('dp', 'seq'))
- lam_log_grad: float32 [512, 64], P(('dp', 'seq'))
- lam_im_grad: float32 [512, 64], P(('dp', 'seq'))
- log_dt_grad: float32 [512], P(('dp', 'seq'))
- mix_weight_grad: float32 [512, 128], P(('dp', 'seq'))
- skip_grad: float32 [512], P(('dp', 'seq'))
- glu_weight_grad: float32 [512, 1024], P(('dp', 'seq'))
- glu_bias_grad: float32 [1024], P(('dp', 'seq'))
The draws below stay inside these ranges and needn't reach their ends.
Inputs may be any that keep to these rules, and one draw needn't show every extreme that they name: `lengths`: in each block of 2 consecutive sequences (those of one index of dp) one sequence has length 2048.
All inputs are finite; a program needn't handle non-finite values.
Results may differ from the reference program's by a relative error of at most 0.0056.
Values may be sent and summed in bfloat16 or wider, within the bound.
A program may use at most 320 MiB of HBM per device.

```python
import math
import jax
import jax.numpy as jnp
from jax import lax

WIDTH = 512
STATES = 64
SEQ_MB = 1
MICRO = 2
SUB = 32
LEN = 2048
BATCH = 8


def decay_rates(key, share):
    pick_key, slow_key, fast_key = jax.random.split(key, 3)
    slow = jax.random.uniform(pick_key, (WIDTH, STATES)) < share
    slow_log = jax.random.uniform(slow_key, (WIDTH, STATES), minval=jnp.log(0.1 / LEN), maxval=jnp.log(1.5 / LEN))
    fast_log = jax.random.uniform(fast_key, (WIDTH, STATES), minval=jnp.log(1.5 / LEN), maxval=jnp.log(1.0 / 25.0))
    return jnp.where(slow, slow_log, fast_log)


def draw_lam_log(key, part):
    share = 0.5
    logs = decay_rates(key, share)
    return logs.astype(jnp.float32)


def draw_mix_weight(key, part):
    share = 0.5
    logs = decay_rates(key, share)
    key = jax.random.fold_in(key, 5)
    noise = jax.random.normal(key, (WIDTH, 2 * STATES))
    rate = jnp.exp(logs)
    return (noise * jnp.sqrt(2.0 * jnp.concatenate([rate, rate], axis=-1) / STATES)).astype(jnp.float32)


def draw_lengths(key, part):
    key = jax.random.fold_in(key, 7)
    length_key, pick_key = jax.random.split(key)
    per_group = MICRO * SEQ_MB
    drawn = jax.random.randint(length_key, (BATCH,), 1, LEN + 1)
    pick = jax.random.randint(pick_key, (BATCH // per_group,), 0, per_group)
    slot = jnp.arange(BATCH, dtype=jnp.int32) % per_group
    chosen = jnp.repeat(pick, per_group)
    return jnp.where(slot == chosen, LEN, drawn).astype(jnp.int32)


def strengthened(entries, stream_key, source, target, shards_of, factor):
    def block_of(position):
        return (jnp.arange(entries.shape[position]) // (entries.shape[position] // shards_of)).reshape((-1,) + (1,) * (entries.ndim - 1 - position))

    near = jax.random.permutation(stream_key, shards_of)[block_of(target)]
    far = (block_of(target) + shards_of // 2) % shards_of
    return jnp.where((block_of(source) == near) | (block_of(source) == far), factor * entries, entries)


def steps_of(key, extent, cuts, smallest, high):
    loudness, own = 1.0, jax.random.fold_in(key, 6)
    for position, shards_of in cuts:
        heights = jnp.exp(jax.random.uniform(jax.random.fold_in(own, position), (shards_of,), jnp.float32, smallest / len(cuts), high / len(cuts)))
        loudness = loudness * jnp.repeat(heights, extent[position] // shards_of).reshape([-1 if axis == position else 1 for axis in range(len(extent))])
    return loudness


def gaussian(stream_key, shape, width, limit, cuts=(), kind=jnp.bfloat16):
    array = width * jax.random.normal(stream_key, shape, jnp.float32)
    if cuts:
        array = array * steps_of(stream_key, shape, cuts, -0.22, 0.18)
    return jnp.clip(array, -limit, limit).astype(kind)


def heavy_noise(key, shape, scale, limit, cuts, heavy, kind=jnp.bfloat16):
    values = scale * jax.random.normal(key, shape, jnp.float32)
    if cuts:
        values = values * steps_of(key, shape, cuts, -0.22, 0.18)
    return jnp.clip(strengthened(values, jax.random.fold_in(key, 3), *heavy), -limit, limit).astype(kind)


def setup_inputs(seed: int = 0) -> dict:
    keys = jax.random.split(jax.random.key(seed), 13)
    inputs = gaussian(keys[0], (BATCH, LEN, WIDTH), 1.0, 6.0, ((0, 4), (1, 8)))
    lengths = draw_lengths(jax.random.fold_in(keys[12], 71), 0)
    ln_gain = jnp.clip(1.0 + 0.1 * jax.random.normal(keys[2], (WIDTH,), jnp.float32), 0.5, 1.5)
    ln_bias = gaussian(keys[3], (WIDTH,), 0.3, 4.0, ((0, 32),), jnp.float32)
    lam_log = draw_lam_log(jax.random.fold_in(keys[12], 71), 0)
    lam_im = jnp.clip(jax.random.uniform(keys[5], (WIDTH, STATES), jnp.float32, -3.140625, 3.140625), -3.140625, 3.140625)
    log_dt = jnp.clip(jax.random.uniform(keys[6], (WIDTH,), jnp.float32, -0.35, 0.35) * steps_of(keys[6], (WIDTH,), ((0, 32),), -0.4, 0.0), -0.35, 0.35)
    mix_weight = draw_mix_weight(jax.random.fold_in(keys[12], 71), 0)
    skip = gaussian(keys[8], (WIDTH,), 0.5, 6.0, ((0, 32),), jnp.float32)
    glu_weight = gaussian(keys[9], (WIDTH, 2 * WIDTH), WIDTH ** -0.5, 0.25, ((0, 32),))
    glu_bias = gaussian(keys[10], (2 * WIDTH,), 0.3, 4.0, ((0, 32),), jnp.float32)
    out_grad = heavy_noise(keys[11], (BATCH, LEN, WIDTH), 1.0, 6.0, ((0, 4), (1, 8)), (1, 2, 8, 2.0))
    return {"inputs": inputs, "lengths": lengths, "ln_gain": ln_gain, "ln_bias": ln_bias, "lam_log": lam_log, "lam_im": lam_im, "log_dt": log_dt, "mix_weight": mix_weight, "skip": skip, "glu_weight": glu_weight, "glu_bias": glu_bias, "out_grad": out_grad}


@jax.custom_vjp
def low(v):
    return lax.optimization_barrier(v.astype(jnp.bfloat16)).astype(jnp.float32)

@jax.custom_vjp
def low_back(v):
    return v

def low_keep(v):
    return (low(v), None)

def low_pass(kept, grad):
    return (grad,)

def back_keep(v):
    return (v, None)

def back_low(kept, grad):
    return (low(grad),)
low.defvjp(low_keep, low_pass)
low_back.defvjp(back_keep, back_low)
EPS = 1e-05
HIGH = lax.Precision.HIGHEST

def halves(packed):
    count = packed.shape[-1] // 2
    return (packed[..., :count], packed[..., count:])

def cmul(first, second):
    first_re, first_im = halves(first)
    second_re, second_im = halves(second)
    return jnp.concatenate([first_re * second_re - first_im * second_im, first_re * second_im + first_im * second_re], axis=-1)

def conjugate(packed):
    real_half, imag_half = halves(packed)
    return jnp.concatenate([real_half, -imag_half], axis=-1)

def coefficients(lam_log, lam_im, log_dt, mix_weight):
    spacing = jnp.exp(log_dt)[:, None]
    rate = jnp.exp(lam_log)
    shrink = -rate * spacing
    angle = lam_im * spacing
    scale = jnp.exp(shrink)
    decay = jnp.concatenate([scale * jnp.cos(angle), scale * jnp.sin(angle)], axis=-1)
    less_re = jnp.expm1(shrink) * jnp.cos(angle) - 2.0 * jnp.sin(0.5 * angle) ** 2
    less_im = scale * jnp.sin(angle)
    modulus = rate * rate + lam_im * lam_im
    ratio = jnp.concatenate([(lam_im * less_im - rate * less_re) / modulus, -(rate * less_im + lam_im * less_re) / modulus], axis=-1)
    return (decay, cmul(mix_weight, ratio))

def power_table(lam_log, lam_im, log_dt, counts):
    spacing = jnp.exp(log_dt)[None, :, None]
    expo = counts[:, None, None]
    scale = jnp.exp(-expo * jnp.exp(lam_log)[None] * spacing)
    angle = expo * lam_im[None] * spacing
    return jnp.concatenate([scale * jnp.cos(angle), scale * jnp.sin(angle)], axis=-1)

def lag_pattern():
    index = jnp.arange(SUB, dtype=jnp.int32)
    return (index[:, None, None] - index[None, :, None] == index[None, None, :]).astype(jnp.float32)

def build_toeplitz(coeff, base):
    kernel = lax.optimization_barrier(jnp.sum(halves(cmul(coeff[None], base))[0], axis=-1))
    return jnp.einsum('kh,ijk->hij', kernel, lag_pattern(), precision=HIGH)

def layer_norm(tokens):
    mean = lax.optimization_barrier(jnp.mean(tokens, axis=-1, keepdims=True))
    centered = tokens - mean
    variance = lax.optimization_barrier(jnp.mean(centered * centered, axis=-1, keepdims=True))
    inverse = lax.rsqrt(variance + EPS)
    return (centered * inverse, inverse)

def ssm_tables(lam_log, lam_im, log_dt, mix_weight):
    decay, coeff = coefficients(lam_log, lam_im, log_dt, mix_weight)
    steps = jnp.arange(SUB, dtype=jnp.float32)
    base = power_table(lam_log, lam_im, log_dt, steps)
    upward = power_table(lam_log, lam_im, log_dt, steps + 1.0)
    downward = power_table(lam_log, lam_im, log_dt, SUB - 1.0 - steps)
    whole = power_table(lam_log, lam_im, log_dt, jnp.full((1,), SUB, jnp.float32))[0]
    toeplitz = build_toeplitz(coeff, base)
    coeff_up = conjugate(cmul(coeff[None], upward))
    return (toeplitz, coeff_up, downward, whole)

def block_step(tables, state, piece):
    toeplitz, coeff_up, downward, whole = tables
    local_part = jnp.einsum('hij,gjh->gih', toeplitz, piece, precision=HIGH)
    carried_part = jnp.einsum('ihz,ghz->gih', coeff_up, state, precision=HIGH)
    inflow = jnp.einsum('gjh,jhz->ghz', piece, downward, precision=HIGH)
    return (cmul(whole[None], state) + inflow, local_part + carried_part)

def ssm_apply(drive, tables):
    group = drive.shape[0]
    blocks = drive.reshape(group, LEN // SUB, SUB, WIDTH).transpose(1, 0, 2, 3)
    checked = jax.checkpoint(block_step)

    def advance(state, piece):
        return checked(tables, state, piece)
    start = jnp.zeros((group, WIDTH, 2 * STATES), jnp.float32)
    _, pieces = lax.scan(advance, start, blocks)
    return pieces.transpose(1, 0, 2, 3).reshape(group, LEN, WIDTH)

def forward(tokens, valid, weights):
    gain, bias, rates, turns, spacing, mixing, skipping, glu_rows, glu_shift = weights
    normed, inverse = layer_norm(tokens)
    drive = (normed * gain + bias) * valid[..., None]
    tables = ssm_tables(rates, turns, spacing, mixing)
    response = ssm_apply(drive, tables) + skipping * drive
    activated = low(jax.nn.gelu(response, approximate=False))
    pre = low_back(jnp.einsum('gth,hk->gtk', activated, glu_rows, precision=HIGH) + glu_shift)
    gate = jax.nn.sigmoid(pre[..., WIDTH:])
    return tokens + pre[..., :WIDTH] * gate * valid[..., None]

def reference(inputs, lengths, ln_gain, ln_bias, lam_log, lam_im, log_dt, mix_weight, skip, glu_weight, glu_bias, out_grad):
    group = math.gcd(BATCH, max(1, 4096 // LEN))
    count = BATCH // group
    params = (ln_gain, ln_bias, lam_log, lam_im, log_dt, mix_weight, skip, glu_weight.astype(jnp.float32), glu_bias)
    tokens = inputs.astype(jnp.float32).reshape(count, group, LEN, WIDTH)
    upstream = out_grad.astype(jnp.float32).reshape(count, group, LEN, WIDTH)
    spans = lengths.reshape(count, group)
    positions = jnp.arange(LEN, dtype=jnp.int32)

    def one_group(totals, item):
        block_tokens, block_upstream, block_spans = item
        valid = (positions[None, :] < block_spans[:, None]).astype(jnp.float32)

        def layer(token_in, weights):
            return forward(token_in, valid, weights)
        result, pull = jax.vjp(layer, block_tokens, params)
        token_grad, weight_grads = pull(block_upstream)
        totals = jax.tree.map(jnp.add, totals, weight_grads)
        return (totals, (result.astype(jnp.bfloat16), token_grad.astype(jnp.bfloat16)))
    zeros = jax.tree.map(jnp.zeros_like, params)
    totals, (results, token_grads) = lax.scan(one_group, zeros, (tokens, upstream, spans))
    return (results.reshape(BATCH, LEN, WIDTH), token_grads.reshape(BATCH, LEN, WIDTH), totals[0], totals[1], totals[2], totals[3], totals[4], totals[5], totals[6], totals[7], totals[8])
```

```python
from functools import partial

import jax
import jax.numpy as jnp
from jax import lax
from jax.sharding import PartitionSpec as P

BLOCK = 128
EPS = 1e-05
HIGH = lax.Precision.HIGHEST
BOTH = ("dp", "seq")


def halves(packed):
    count = packed.shape[-1] // 2
    return (packed[..., :count], packed[..., count:])


def cmul(first, second):
    first_re, first_im = halves(first)
    second_re, second_im = halves(second)
    return jnp.concatenate(
        [first_re * second_re - first_im * second_im, first_re * second_im + first_im * second_re],
        axis=-1,
    )


def conjugate(packed):
    real_half, imag_half = halves(packed)
    return jnp.concatenate([real_half, -imag_half], axis=-1)


def coefficients(lam_log, lam_im, log_dt, mix_weight):
    spacing = jnp.exp(log_dt)[:, None]
    rate = jnp.exp(lam_log)
    shrink = -rate * spacing
    angle = lam_im * spacing
    scale = jnp.exp(shrink)
    decay = jnp.concatenate([scale * jnp.cos(angle), scale * jnp.sin(angle)], axis=-1)
    less_re = jnp.expm1(shrink) * jnp.cos(angle) - 2.0 * jnp.sin(0.5 * angle) ** 2
    less_im = scale * jnp.sin(angle)
    modulus = rate * rate + lam_im * lam_im
    ratio = jnp.concatenate(
        [
            (lam_im * less_im - rate * less_re) / modulus,
            -(rate * less_im + lam_im * less_re) / modulus,
        ],
        axis=-1,
    )
    return (decay, cmul(mix_weight, ratio))


def powers(decay):
    real_half, imag_half = halves(decay)
    table = jnp.concatenate([jnp.ones_like(real_half), jnp.zeros_like(imag_half)], axis=-1)[:, None]
    step = decay[:, None]
    while table.shape[1] < BLOCK:
        table = jnp.concatenate([table, cmul(step, table)], axis=1)
        step = cmul(step, step)
    return (table, step[:, 0])


def link(earlier, later):
    return (cmul(earlier[0], later[0]), cmul(later[0], earlier[1]) + later[1])


def shifted(pieces, step, back):
    leads = jnp.broadcast_to(step[:, None, None], pieces.shape)
    _, reach = lax.associative_scan(link, (leads, pieces), axis=2, reverse=back)
    none = jnp.zeros_like(reach[:, :, :1])
    if back:
        return jnp.concatenate([reach[:, :, 1:], none], axis=2)
    return jnp.concatenate([none, reach[:, :, :-1]], axis=2)


def to_owner(rows):
    count, span, width = rows.shape
    groups, parts = (lax.axis_size("dp"), lax.axis_size("seq"))
    own = width // (groups * parts)
    sent = rows.reshape(count * span, width).T.reshape(-1, own, count, span)
    held = lax.all_to_all(sent, BOTH, 0, 0, tiled=True).reshape(groups, parts, own, count, span)
    held = held.transpose(2, 0, 3, 1, 4).reshape(own, groups * count, -1, BLOCK)
    return held


def to_holder(held, count, span):
    groups, parts = (lax.axis_size("dp"), lax.axis_size("seq"))
    own = held.shape[0]
    sent = held.astype(jnp.bfloat16).reshape(own, groups, count, parts, span).transpose(1, 3, 0, 2, 4)
    sent = sent.reshape(groups * parts, own, count, span)
    rows = lax.all_to_all(sent, BOTH, 0, 0, tiled=True)
    return rows.reshape(-1, count * span).T.reshape(count, span, -1).astype(jnp.float32)


def per_device(
    inputs,
    lengths,
    ln_gain,
    ln_bias,
    lam_log,
    lam_im,
    log_dt,
    mix_weight,
    skip,
    glu_weight,
    glu_bias,
    out_grad,
):
    count, span, width = inputs.shape
    offset = lax.axis_index("seq") * span
    positions = offset + jnp.arange(span, dtype=jnp.int32)
    valid = (positions[None, :] < lengths[:, None]).astype(jnp.float32)[..., None]
    rows = lax.all_gather(glu_weight, BOTH, axis=0, tiled=True)
    shift = lax.all_gather(glu_bias, BOTH, axis=0, tiled=True)
    spans = lax.all_gather(lengths, "dp", axis=0, tiled=True)
    whole_span = span * lax.axis_size("seq")
    mask = (jnp.arange(whole_span, dtype=jnp.int32)[None] < spans[:, None]).astype(jnp.float32)
    mask = mask.reshape(1, -1, whole_span // BLOCK, BLOCK)

    tokens = inputs.astype(jnp.float32)
    mean = jnp.mean(tokens, axis=-1, keepdims=True)
    centered = tokens - mean
    inverse = lax.rsqrt(jnp.mean(centered * centered, axis=-1, keepdims=True) + EPS)
    normed = centered * inverse

    (decay, coeff), coeff_pull = jax.vjp(coefficients, lam_log, lam_im, log_dt, mix_weight)
    base, whole = powers(decay)
    down = base[:, ::-1]
    real_half, imag_half = halves(coeff)
    kernel = jnp.einsum("cz,ckz->ck", conjugate(coeff), base, precision=HIGH)
    lead = cmul(coeff, decay)[:, None]
    up = conjugate(cmul(lead, base))
    back = conjugate(cmul(lead, down))
    steps = jnp.arange(BLOCK)
    lag = steps[:, None] - steps[None, :]
    toeplitz = jnp.where(lag >= 0, kernel[:, jnp.maximum(lag, 0)], 0.0)
    ramp = steps.astype(jnp.float32)[:, None]

    gain, bias, skipping = (p[:, None, None, None] for p in (ln_gain, ln_bias, skip))
    own_normed = to_owner(normed)
    drive = (own_normed * gain + bias) * mask
    entering = shifted(jnp.einsum("cbqj,cjz->cbqz", drive, down, precision=HIGH), whole, False)
    response = jnp.einsum("cij,cbqj->cbqi", toeplitz, drive, precision=HIGH)
    response += jnp.einsum("ciz,cbqz->cbqi", up, entering, precision=HIGH) + skipping * drive
    activated, gelu_pull = jax.vjp(partial(jax.nn.gelu, approximate=False), response)
    activated = to_holder(activated, count, span).astype(jnp.bfloat16).reshape(-1, width)
    pre = jnp.dot(activated, rows, preferred_element_type=jnp.float32) + shift
    gate = jax.nn.sigmoid(pre[:, width:])
    flat_valid = valid.reshape(-1, 1)
    result = (tokens + (pre[:, :width] * gate * flat_valid).reshape(tokens.shape)).astype(jnp.bfloat16)
    upstream = out_grad.astype(jnp.float32)
    gated = upstream.reshape(-1, width) * flat_valid
    pre_grad = jnp.concatenate(
        [gated * gate, gated * pre[:, :width] * gate * (1.0 - gate)], axis=-1
    ).astype(jnp.bfloat16)
    rows_grad = lax.dot_general(
        activated, pre_grad, (((0,), (0,)), ((), ())), preferred_element_type=jnp.float32
    )
    shift_grad = jnp.sum(pre_grad.astype(jnp.float32), axis=0)
    act_grad = lax.dot_general(
        pre_grad, rows, (((1,), (1,)), ((), ())), preferred_element_type=jnp.float32
    )
    response_grad = gelu_pull(to_owner(act_grad.reshape(tokens.shape)))[0]

    skip_grad = jnp.sum(response_grad * drive, axis=(1, 2, 3))
    outflow = jnp.einsum("cbqt,ctz->cbqz", response_grad, base, precision=HIGH)
    leaving = shifted(outflow, whole, True)
    drive_grad = jnp.einsum("cij,cbqi->cbqj", toeplitz, response_grad, precision=HIGH)
    drive_grad += jnp.einsum("cjz,cbqz->cbqj", back, leaving, precision=HIGH) + skipping * response_grad
    norm_grad = drive_grad * mask
    gain_grad = jnp.sum(norm_grad * own_normed, axis=(1, 2, 3))
    bias_grad = jnp.sum(norm_grad, axis=(1, 2, 3))
    scaled = to_holder(norm_grad * gain, count, span)
    token_grad = upstream + inverse * (
        scaled
        - jnp.mean(scaled, axis=-1, keepdims=True)
        - normed * jnp.mean(scaled * normed, axis=-1, keepdims=True)
    )

    cross = jnp.einsum("cbqj,cbqi->cij", drive, response_grad, precision=HIGH)
    lags = jnp.stack([jnp.trace(cross, offset=-k, axis1=1, axis2=2) for k in range(BLOCK)], axis=-1)
    second = jnp.einsum("cbqj,cjz->cbqz", drive, down * ramp[::-1], precision=HIGH)
    third = jnp.einsum("cbqt,ctz->cbqz", response_grad, base * (ramp + 1.0), precision=HIGH)
    total = partial(jnp.sum, axis=(1, 2))
    moment = cmul(decay, total(cmul(entering, outflow))) + jnp.einsum("ck,ckz->cz", lags, base, precision=HIGH)
    before = jnp.concatenate([jnp.zeros_like(base[:, :1]), base[:, :-1]], axis=1) * ramp
    paired = BLOCK * cmul(whole, total(cmul(leaving, entering)))
    paired += total(cmul(leaving, second) + cmul(entering, third))
    paired = cmul(coeff, paired + jnp.einsum("ck,ckz->cz", lags, before, precision=HIGH))
    rate_grad, turn_grad, spacing_grad, mixing_grad = coeff_pull((conjugate(paired), conjugate(moment)))

    scatter = partial(lax.psum_scatter, axis_name=BOTH, scatter_dimension=0, tiled=True)
    return (
        result,
        token_grad.astype(jnp.bfloat16),
        gain_grad,
        bias_grad,
        rate_grad,
        turn_grad,
        spacing_grad,
        mixing_grad,
        skip_grad,
        scatter(rows_grad),
        scatter(shift_grad),
    )


def solution(mesh):
    tokens, vector, matrix = (P("dp", "seq", None), P(BOTH), P(BOTH, None))
    return jax.shard_map(
        per_device,
        mesh=mesh,
        in_specs=(
            tokens, P("dp"), vector, vector, matrix, matrix, vector, matrix, vector, matrix, vector, tokens,
        ),
        out_specs=(
            tokens, tokens, vector, vector, matrix, matrix, vector, matrix, vector, matrix, vector,
        ),
        check_vma=False,
    )
```

```python
import math
from functools import partial

import jax
import jax.numpy as jnp
from jax import lax
from jax.experimental import pallas as pl
from jax.experimental.pallas import tpu as pltpu
from jax.sharding import PartitionSpec as P

BLOCK = 128
EPS = 1e-05
HIGH = lax.Precision.HIGHEST
BOTH = ("dp", "seq")


def halves(packed):
    count = packed.shape[-1] // 2
    return (packed[..., :count], packed[..., count:])


def cmul(first, second):
    first_re, first_im = halves(first)
    second_re, second_im = halves(second)
    return jnp.concatenate(
        [first_re * second_re - first_im * second_im, first_re * second_im + first_im * second_re],
        axis=-1,
    )


def conjugate(packed):
    real_half, imag_half = halves(packed)
    return jnp.concatenate([real_half, -imag_half], axis=-1)


def coefficients(lam_log, lam_im, log_dt, mix_weight):
    spacing = jnp.exp(log_dt)[:, None]
    rate = jnp.exp(lam_log)
    shrink = -rate * spacing
    angle = lam_im * spacing
    scale = jnp.exp(shrink)
    decay = jnp.concatenate([scale * jnp.cos(angle), scale * jnp.sin(angle)], axis=-1)
    less_re = jnp.expm1(shrink) * jnp.cos(angle) - 2.0 * jnp.sin(0.5 * angle) ** 2
    less_im = scale * jnp.sin(angle)
    modulus = rate * rate + lam_im * lam_im
    ratio = jnp.concatenate(
        [
            (lam_im * less_im - rate * less_re) / modulus,
            -(rate * less_im + lam_im * less_re) / modulus,
        ],
        axis=-1,
    )
    return (decay, cmul(mix_weight, ratio))


def powers(decay):
    real_half, imag_half = halves(decay)
    table = jnp.concatenate([jnp.ones_like(real_half), jnp.zeros_like(imag_half)], axis=-1)[:, None]
    step = decay[:, None]
    while table.shape[1] < BLOCK:
        table = jnp.concatenate([table, cmul(step, table)], axis=1)
        step = cmul(step, step)
    return (table, step[:, 0])


def link(earlier, later):
    return (cmul(earlier[0], later[0]), cmul(later[0], earlier[1]) + later[1])


def shifted(pieces, step, back):
    leads = jnp.broadcast_to(step[:, None, None], pieces.shape)
    _, reach = lax.associative_scan(link, (leads, pieces), axis=2, reverse=back)
    none = jnp.zeros_like(reach[:, :, :1])
    if back:
        return jnp.concatenate([reach[:, :, 1:], none], axis=2)
    return jnp.concatenate([none, reach[:, :, :-1]], axis=2)


def to_owner(rows):
    count, span, width = rows.shape
    groups, parts = (lax.axis_size("dp"), lax.axis_size("seq"))
    own = width // (groups * parts)
    sent = rows.reshape(count * span, width).T.reshape(-1, own, count, span)
    held = lax.all_to_all(sent, BOTH, 0, 0, tiled=True).reshape(groups, parts, own, count, span)
    held = held.transpose(2, 0, 3, 1, 4).reshape(own, groups * count, -1, BLOCK)
    return held


def to_holder(held, count, span):
    groups, parts = (lax.axis_size("dp"), lax.axis_size("seq"))
    own = held.shape[0]
    sent = held.astype(jnp.bfloat16).reshape(own, groups, count, parts, span).transpose(1, 3, 0, 2, 4)
    sent = sent.reshape(groups * parts, own, count, span)
    rows = lax.all_to_all(sent, BOTH, 0, 0, tiled=True)
    return rows.reshape(-1, count * span).T.reshape(count, span, -1).astype(jnp.float32)


def per_device(
    inputs,
    lengths,
    ln_gain,
    ln_bias,
    lam_log,
    lam_im,
    log_dt,
    mix_weight,
    skip,
    glu_weight,
    glu_bias,
    out_grad,
):
    count, span, width = inputs.shape
    offset = lax.axis_index("seq") * span
    positions = offset + jnp.arange(span, dtype=jnp.int32)
    valid = (positions[None, :] < lengths[:, None]).astype(jnp.float32)[..., None]
    rows = lax.all_gather(glu_weight, BOTH, axis=0, tiled=True)
    shift = lax.all_gather(glu_bias, BOTH, axis=0, tiled=True)
    spans = lax.all_gather(lengths, "dp", axis=0, tiled=True)
    whole_span = span * lax.axis_size("seq")
    mask = (jnp.arange(whole_span, dtype=jnp.int32)[None] < spans[:, None]).astype(jnp.float32)
    mask = mask.reshape(1, -1, whole_span // BLOCK, BLOCK)

    tokens = inputs.astype(jnp.float32)
    mean = jnp.mean(tokens, axis=-1, keepdims=True)
    centered = tokens - mean
    inverse = lax.rsqrt(jnp.mean(centered * centered, axis=-1, keepdims=True) + EPS)
    normed = centered * inverse

    (decay, coeff), coeff_pull = jax.vjp(coefficients, lam_log, lam_im, log_dt, mix_weight)
    base, whole = powers(decay)
    down = base[:, ::-1]
    real_half, imag_half = halves(coeff)
    kernel = jnp.einsum("cz,ckz->ck", conjugate(coeff), base, precision=HIGH)
    lead = cmul(coeff, decay)[:, None]
    up = conjugate(cmul(lead, base))
    back = conjugate(cmul(lead, down))
    steps = jnp.arange(BLOCK)
    lag = steps[:, None] - steps[None, :]
    toeplitz = jnp.where(lag >= 0, kernel[:, jnp.maximum(lag, 0)], 0.0)
    ramp = steps.astype(jnp.float32)[:, None]

    gain, bias, skipping = (p[:, None, None, None] for p in (ln_gain, ln_bias, skip))
    own_normed = to_owner(normed)
    drive = (own_normed * gain + bias) * mask
    entering = shifted(jnp.einsum("cbqj,cjz->cbqz", drive, down, precision=HIGH), whole, False)
    response = jnp.einsum("cij,cbqj->cbqi", toeplitz, drive, precision=HIGH)
    response += jnp.einsum("ciz,cbqz->cbqi", up, entering, precision=HIGH) + skipping * drive
    activated, gelu_pull = jax.vjp(partial(jax.nn.gelu, approximate=False), response)
    activated = to_holder(activated, count, span).astype(jnp.bfloat16).reshape(-1, width)
    pre = jnp.dot(activated, rows, preferred_element_type=jnp.float32) + shift
    gate = jax.nn.sigmoid(pre[:, width:])
    flat_valid = valid.reshape(-1, 1)
    result = (tokens + (pre[:, :width] * gate * flat_valid).reshape(tokens.shape)).astype(jnp.bfloat16)
    upstream = out_grad.astype(jnp.float32)
    gated = upstream.reshape(-1, width) * flat_valid
    pre_grad = jnp.concatenate(
        [gated * gate, gated * pre[:, :width] * gate * (1.0 - gate)], axis=-1
    ).astype(jnp.bfloat16)
    rows_grad = lax.dot_general(
        activated, pre_grad, (((0,), (0,)), ((), ())), preferred_element_type=jnp.float32
    )
    shift_grad = jnp.sum(pre_grad.astype(jnp.float32), axis=0)
    act_grad = lax.dot_general(
        pre_grad, rows, (((1,), (1,)), ((), ())), preferred_element_type=jnp.float32
    )
    response_grad = gelu_pull(to_owner(act_grad.reshape(tokens.shape)))[0]

    skip_grad = jnp.sum(response_grad * drive, axis=(1, 2, 3))
    outflow = jnp.einsum("cbqt,ctz->cbqz", response_grad, base, precision=HIGH)
    leaving = shifted(outflow, whole, True)
    drive_grad = jnp.einsum("cij,cbqi->cbqj", toeplitz, response_grad, precision=HIGH)
    drive_grad += jnp.einsum("cjz,cbqz->cbqj", back, leaving, precision=HIGH) + skipping * response_grad
    norm_grad = drive_grad * mask
    gain_grad = jnp.sum(norm_grad * own_normed, axis=(1, 2, 3))
    bias_grad = jnp.sum(norm_grad, axis=(1, 2, 3))
    scaled = to_holder(norm_grad * gain, count, span)
    token_grad = upstream + inverse * (
        scaled
        - jnp.mean(scaled, axis=-1, keepdims=True)
        - normed * jnp.mean(scaled * normed, axis=-1, keepdims=True)
    )

    cross = jnp.einsum("cbqj,cbqi->cij", drive, response_grad, precision=HIGH)
    lags = jnp.stack([jnp.trace(cross, offset=-k, axis1=1, axis2=2) for k in range(BLOCK)], axis=-1)
    second = jnp.einsum("cbqj,cjz->cbqz", drive, down * ramp[::-1], precision=HIGH)
    third = jnp.einsum("cbqt,ctz->cbqz", response_grad, base * (ramp + 1.0), precision=HIGH)
    total = partial(jnp.sum, axis=(1, 2))
    moment = cmul(decay, total(cmul(entering, outflow))) + jnp.einsum("ck,ckz->cz", lags, base, precision=HIGH)
    before = jnp.concatenate([jnp.zeros_like(base[:, :1]), base[:, :-1]], axis=1) * ramp
    paired = BLOCK * cmul(whole, total(cmul(leaving, entering)))
    paired += total(cmul(leaving, second) + cmul(entering, third))
    paired = cmul(coeff, paired + jnp.einsum("ck,ckz->cz", lags, before, precision=HIGH))
    rate_grad, turn_grad, spacing_grad, mixing_grad = coeff_pull((conjugate(paired), conjugate(moment)))

    scatter = partial(lax.psum_scatter, axis_name=BOTH, scatter_dimension=0, tiled=True)
    return (
        result,
        token_grad.astype(jnp.bfloat16),
        gain_grad,
        bias_grad,
        rate_grad,
        turn_grad,
        spacing_grad,
        mixing_grad,
        skip_grad,
        scatter(rows_grad),
        scatter(shift_grad),
    )


MESH = pl.DeviceIdType.MESH
F32, BF16, I16 = (jnp.float32, jnp.bfloat16, jnp.int16)
STEPS = 32700.0
GROUP = 4


def low_half(shape):
    return lax.broadcasted_iota(jnp.int32, shape, len(shape) - 1) < shape[-1] // 2


def swap(packed):
    return pltpu.roll(packed, packed.shape[-1] // 2, packed.ndim - 1)


def spread(packed):
    other, low = (swap(packed), low_half(packed.shape))
    return (jnp.where(low, packed, other), jnp.where(low, -other, packed))


def times(packed, factor):
    return packed * factor[0] + swap(packed) * factor[1]


def two(value):
    high = value.astype(BF16)
    return (high, (value - high.astype(F32)).astype(BF16))


def rows_of(value):
    return jnp.concatenate(two(value), axis=0)


def lanes_of(value):
    return jnp.concatenate(two(value), axis=1)


def dot(left, right, dims=((1,), (0,))):
    return lax.dot_general(left, right, (dims, ((), ())), preferred_element_type=F32)


def fold_rows(value):
    count = value.shape[0] // 2
    return value[:count] + value[count:]


def fold_lanes(value):
    count = value.shape[1] // 2
    return value[:, :count] + value[:, count:]


def small_expm1(value):
    near = jnp.abs(value) < 0.5
    small = jnp.where(near, value, 0.0)
    series = jnp.ones_like(small)
    for order in range(10, 1, -1):
        series = 1.0 + small * (1.0 / order) * series
    return jnp.where(near, small * series, jnp.exp(value) - 1.0)


def coefficient_parts(lam_log, lam_im, log_dt, mix_re, mix_im):
    spacing, rate = (jnp.exp(log_dt), jnp.exp(lam_log))
    shrink, angle = (-rate * spacing, lam_im * spacing)
    scale = jnp.exp(shrink)
    cosine, sine, half = (jnp.cos(angle), jnp.sin(angle), jnp.sin(0.5 * angle))
    less_re = small_expm1(shrink) * cosine - 2.0 * half * half
    less_im = scale * sine
    modulus = rate * rate + lam_im * lam_im
    ratio_re = (lam_im * less_im - rate * less_re) / modulus
    ratio_im = -(rate * less_im + lam_im * less_re) / modulus
    return (
        scale * cosine,
        less_im,
        mix_re * ratio_re - mix_im * ratio_im,
        mix_re * ratio_im + mix_im * ratio_re,
    )


def whole_kernel(
    size,
    inputs, lengths, ln_gain, ln_bias, lam_log, lam_im, log_dt, mix_weight, skip, glu_weight, glu_bias, out_grad,
    result, token_grad, gain_grad, bias_grad, rate_grad, turn_grad, spacing_grad, mixing_grad, skip_grad,
    rows_grad, shift_grad,
    s,
):
    groups, parts, own, width, span, count = size
    devices, blocks, pairs = (groups * parts, span // BLOCK, parts // 2)
    tiles = width // BLOCK
    dp, seq = (lax.axis_index("dp"), lax.axis_index("seq"))
    core, pair = (lax.rem(seq, 2), seq // 2)
    me = dp * parts + seq
    share = 2 * own
    per_tile = BLOCK // share

    def place(target):
        return (target // parts, lax.rem(target, parts))

    def send(source, target, send_sem, recv_sem, device):
        pltpu.make_async_remote_copy(
            src_ref=source, dst_ref=target, send_sem=send_sem, recv_sem=recv_sem,
            device_id=device, device_id_type=MESH,
        ).start()

    def wait_sent(ref, sem):
        pltpu.make_async_copy(ref, ref, sem).wait()

    def scatter(out, into, sems):
        def one(k, carry):
            target = lax.rem(me + k, devices)
            send(out.at[target], into.at[me], sems.at[0], sems.at[1], place(target))
            return carry

        lax.fori_loop(1, devices, one, 0)

    def spread_out(out, into, sems):
        def one(k, carry):
            target = lax.rem(me + k, devices)
            send(out, into.at[me], sems.at[0], sems.at[1], place(target))
            return carry

        lax.fori_loop(1, devices, one, 0)

    def arrived(ref, sems):
        wait_sent(ref.at[pl.ds(0, devices - 1)], sems.at[1])

    def left(ref, sems):
        wait_sent(ref.at[pl.ds(0, devices - 1)], sems.at[0])

    barrier = pltpu.get_barrier_semaphore()

    def greet(k, carry):
        pl.semaphore_signal(barrier, inc=1, device_id=place(lax.rem(me + k, devices)), device_id_type=MESH)
        return carry

    lax.fori_loop(1, devices, greet, 0)

    lane = lax.broadcasted_iota(jnp.int32, (1, span), 1) + seq * span
    quantum = math.sqrt(width) / STEPS

    def norm(m):
        tokens = inputs[m].T
        s.tokens[m] = tokens
        total = jnp.zeros((1, span), F32)
        for j in range(tiles):
            total += jnp.sum(tokens[j * BLOCK : (j + 1) * BLOCK].astype(F32), axis=0, keepdims=True)
        mean = total * (1.0 / width)
        total = jnp.zeros((1, span), F32)
        for j in range(tiles):
            off = tokens[j * BLOCK : (j + 1) * BLOCK].astype(F32) - mean
            total += jnp.sum(off * off, axis=0, keepdims=True)
        inverse = lax.rsqrt(total * (1.0 / width) + EPS)
        valid = (lane < lengths[m]).astype(F32)
        s.inverse[m : m + 1] = inverse
        s.valid[m : m + 1] = valid
        for j in range(tiles):
            normed = (tokens[j * BLOCK : (j + 1) * BLOCK].astype(F32) - mean) * inverse
            s.normed[m, j * BLOCK : (j + 1) * BLOCK] = normed
            coded = jnp.round(normed * valid * (1.0 / quantum)).astype(I16)
            s.x_out[m, j * BLOCK // own : (j + 1) * BLOCK // own] = coded.reshape(-1, own, span)
        s.x_in[m, pl.ds(me, 1)] = s.x_out[m, pl.ds(me, 1)]

    norm(0)

    row_lane = lax.broadcasted_iota(jnp.int32, (1, BLOCK), 1)
    start = lax.rem(me, per_tile) * share
    row = jnp.zeros((1, BLOCK), F32)
    for k in range(share):
        row = jnp.where(row_lane == start + k, glu_bias[k], row)
    after = lax.rem(start + share, BLOCK)
    for m in range(count):
        row = jnp.where(row_lane == after + m, lengths[m].astype(F32), row)
    s.note_out[0] = row
    s.note_in[pl.ds(me, 1)] = row[None]
    s.weight[pl.ds(dp, 1), pl.ds(pair, 1), pl.ds(core, 1)] = glu_weight[...][None, None, None]

    pl.semaphore_wait(barrier, devices - 1)
    spread_out(s.note_out.at[0], s.note_in, s.note_sem)
    scatter(s.x_out.at[0], s.x_in.at[0], s.x_sem.at[0])

    def weight_hop(hop):
        if hop == 0:
            for k in range(1, pairs):
                there = lax.rem(pair + k, pairs)
                send(glu_weight, s.weight.at[dp, pair, core], s.weight_sem.at[0], s.weight_sem.at[1],
                     (dp, there * 2 + core))
        elif hop == 1:
            for k in range(1, groups):
                mine = s.weight.at[dp, :, core]
                send(mine, mine, s.weight_sem.at[2], s.weight_sem.at[3], (lax.rem(dp + k, groups), seq))
        else:
            mine = s.weight.at[:, :, core]
            send(mine, mine, s.weight_sem.at[4], s.weight_sem.at[5], (dp, pair * 2 + 1 - core))

    def weight_wait(hop):
        if hop == 0:
            ref = s.weight.at[0, pl.ds(0, pairs - 1), 0]
        elif hop == 1:
            ref = s.weight.at[pl.ds(0, groups - 1), :, 0]
        else:
            ref = s.weight.at[:, :, 0]
        wait_sent(ref, s.weight_sem.at[2 * hop])
        wait_sent(ref, s.weight_sem.at[2 * hop + 1])

    weight_hop(0)
    for m in range(1, count):
        norm(m)
        scatter(s.x_out.at[m], s.x_in.at[m], s.x_sem.at[m])

    log_step = jnp.zeros(lam_log.shape, F32)
    channel = lax.broadcasted_iota(jnp.int32, lam_log.shape, 0)
    for c in range(own):
        log_step = jnp.where(channel == c, log_dt[c], log_step)
    states = lam_log.shape[1]
    mix_re, mix_im = (mix_weight[:, :states], mix_weight[:, states:])
    (decay_re, decay_im, coeff_re, coeff_im), pull = jax.vjp(
        coefficient_parts, lam_log[...], lam_im[...], log_step, mix_re, mix_im
    )
    decay = jnp.concatenate([decay_re, decay_im], axis=1)
    coeff = jnp.concatenate([coeff_re, coeff_im], axis=1)
    power = decay
    factors = []
    for bit in range(s.power_both.shape[0]):
        factors.append(spread(power))
        s.power_both[bit], s.power_cross[bit] = factors[-1]
        power = times(power, factors[-1])
    sign = jnp.where(low_half(coeff.shape), 1.0, -1.0)
    lead = spread(times(coeff, factors[0]))
    s.lead[0], s.lead[1] = (lead[0] * sign, lead[1] * sign)
    s.coeff[...] = coeff * sign

    def power_of(bit, c):
        return (s.power_both[bit, pl.ds(c, 1), :], s.power_cross[bit, pl.ds(c, 1), :])

    square = (BLOCK, BLOCK)
    row_id = lax.broadcasted_iota(jnp.int32, square, 0)
    lane_id = lax.broadcasted_iota(jnp.int32, square, 1)
    ramp = row_id.astype(F32)

    def tables(c):
        eight = row_id[:8]
        unit = low_half((8, BLOCK)).astype(F32)
        base, down = (unit, unit)
        for bit in range(3):
            step = power_of(bit, c)
            base = jnp.where((eight >> bit) & 1 == 1, times(base, step), base)
            down = jnp.where(((7 - eight) >> bit) & 1 == 1, times(down, step), down)
        for bit in range(3, 7):
            step = power_of(bit, c)
            base = jnp.concatenate([base, times(base, step)], axis=0)
            down = jnp.concatenate([times(down, step), down], axis=0)
        lead = (s.lead[0, pl.ds(c, 1), :], s.lead[1, pl.ds(c, 1), :])
        s.base[c] = lanes_of(base)
        s.down[c] = lanes_of(down)
        s.base_ramp[c] = lanes_of(base * (ramp + 1.0))
        s.down_ramp[c] = lanes_of(down * (BLOCK - 1.0 - ramp))
        s.up[c] = rows_of(times(base, lead))
        s.back[c] = rows_of(times(down, lead))
        kernel = lax.dot_general(
            jnp.broadcast_to(s.coeff[pl.ds(c, 1), :], (8, BLOCK)), base, (((1,), (1,)), ((), ())),
            preferred_element_type=F32, precision=HIGH,
        )
        slanted = pltpu.roll(jnp.broadcast_to(kernel[:1], square), 0, 1, stride=1, stride_axis=0)
        s.toeplitz[c] = rows_of(jnp.where(lane_id >= row_id, slanted, 0.0))

    def over_channels(body):
        def some(g, carry):
            for u in range(GROUP):
                body(g * GROUP + u)
            return carry

        lax.fori_loop(0, own // GROUP, some, 0)

    over_channels(tables)

    source_seq = lax.rem(lax.broadcasted_iota(jnp.int32, (devices, BLOCK), 0), parts)
    source_lane = lax.broadcasted_iota(jnp.int32, (devices, BLOCK), 1)
    device_bit = 7 + blocks.bit_length() - 1

    def rows_in(ref, m):
        for q in range(blocks):
            piece = ref[m, :, :, q * BLOCK : (q + 1) * BLOCK]
            s.stage[q] = piece.astype(F32).reshape(devices * own, BLOCK)

    def rows_out(ref, m):
        for q in range(blocks):
            ref[m, :, :, q * BLOCK : (q + 1) * BLOCK] = (
                s.stage[q].astype(BF16).reshape(devices, own, BLOCK)
            )

    def gather_channel(c):
        return [s.stage[q, pl.ds(c, devices, stride=own), :] for q in range(blocks)]

    def put_channel(c, value):
        for q in range(blocks):
            s.stage[q, pl.ds(c, devices, stride=own), :] = value[q * devices : (q + 1) * devices]

    def pieces(value):
        return [value[q * devices : (q + 1) * devices] for q in range(blocks)]

    def states_before(flows, c):
        block_step = power_of(7, c)
        total = flows[0]
        for flow in flows[1:]:
            total = times(total, block_step) + flow
        reach = 1
        while reach < parts:
            moved = times(pltpu.roll(total, reach, 0), power_of(device_bit + reach.bit_length() - 1, c))
            total = total + jnp.where(source_seq >= reach, moved, 0.0)
            reach *= 2
        state = jnp.where(source_seq >= 1, pltpu.roll(total, 1, 0), 0.0)
        listing = [state]
        for flow in flows[:-1]:
            state = times(state, block_step) + flow
            listing.append(state)
        return jnp.concatenate(listing, axis=0)

    def states_after(flows, c):
        block_step = power_of(7, c)
        total = flows[-1]
        for flow in flows[-2::-1]:
            total = times(total, block_step) + flow
        reach = 1
        while reach < parts:
            moved = times(
                pltpu.roll(total, devices - reach, 0), power_of(device_bit + reach.bit_length() - 1, c)
            )
            total = total + jnp.where(source_seq < parts - reach, moved, 0.0)
            reach *= 2
        state = jnp.where(source_seq < parts - 1, pltpu.roll(total, devices - 1, 0), 0.0)
        listing = [state]
        for flow in flows[:0:-1]:
            state = times(state, block_step) + flow
            listing.append(state)
        return jnp.concatenate(listing[::-1], axis=0)

    def read_notes():
        arrived(s.note_in, s.note_sem)
        left(s.note_in, s.note_sem)
        notes = s.note_in[...].reshape(devices, BLOCK)
        origin = lax.rem(lax.broadcasted_iota(jnp.int32, (devices, BLOCK), 0), per_tile) * share
        behind = lax.rem(origin + share, BLOCK)
        for m in range(count):
            length = jnp.sum(jnp.where(source_lane == behind + m, notes, 0.0), axis=1, keepdims=True)
            for q in range(blocks):
                position = source_seq * span + source_lane + q * BLOCK
                s.mask[m, q * devices : (q + 1) * devices] = (position.astype(F32) < length).astype(F32)
        biased = jnp.where((source_lane >= origin) & (source_lane < origin + share), notes, 0.0)
        tile_rows = jnp.sum(biased.reshape(devices // per_tile, per_tile, BLOCK), axis=1)
        s.shift[...] = tile_rows.T

    def forward(m):
        arrived(s.x_in.at[m], s.x_sem.at[m])
        rows_in(s.x_in, m)

        def body(c):
            own_normed = jnp.concatenate(gather_channel(c), axis=0) * quantum
            drive = (own_normed * ln_gain[c] + ln_bias[c]) * s.mask[m]
            coded = rows_of(drive)
            inflow = fold_lanes(fold_rows(dot(coded, s.down[c])))
            entering = states_before(pieces(inflow), c)
            response = fold_rows(dot(jnp.concatenate([coded, coded], axis=1), s.toeplitz[c]))
            response += fold_lanes(fold_rows(dot(rows_of(entering), s.up[c], ((1,), (1,)))))
            response += skip[c] * drive
            share_below = 0.5 * (1.0 + lax.erf(response * math.sqrt(0.5)))
            density = jnp.exp(-0.5 * response * response) * (1.0 / math.sqrt(2.0 * math.pi))
            s.own_normed[m, c] = own_normed
            s.drive[m, c] = drive
            s.entering[m, c] = entering
            s.slope[m, c] = share_below + response * density
            put_channel(c, response * share_below)

        over_channels(body)
        rows_out(s.a_out, m)
        s.a_in[m, pl.ds(me, 1)] = s.a_out[m, pl.ds(me, 1)]
        scatter(s.a_out.at[m], s.a_in.at[m], s.a_sem.at[m])

    read_notes()
    forward(0)
    weight_wait(0)
    weight_hop(1)
    for m in range(1, count):
        forward(m)
    weight_wait(1)
    weight_hop(2)
    for m in range(count):
        s.upstream[m] = out_grad[m].T
    weight_wait(2)
    for j in range(tiles):
        rows = slice(j * BLOCK, (j + 1) * BLOCK)
        per = BLOCK // own
        flat = s.weight[...].reshape(devices, own, 2 * width)[j * per : (j + 1) * per]
        flat = flat.reshape(BLOCK, 2 * width)
        s.flat[rows] = flat
        s.flipped[:, rows] = flat.T

    def project(m):
        arrived(s.a_in.at[m], s.a_sem.at[m])
        activated = s.a_in[m].reshape(width, span)
        valid = s.valid[m : m + 1]
        for j in range(tiles):
            rows = slice(j * BLOCK, (j + 1) * BLOCK)
            gates = slice(width + j * BLOCK, width + (j + 1) * BLOCK)
            value = dot(s.flipped[rows], activated) + s.shift[:, j : j + 1]
            gate = jax.nn.sigmoid(dot(s.flipped[gates], activated) + s.shift[:, tiles + j : tiles + j + 1])
            gated = s.upstream[m, rows].astype(F32) * valid
            s.pre_grad[rows] = (gated * gate).astype(BF16)
            s.pre_grad[gates] = (gated * value * gate * (1.0 - gate)).astype(BF16)
            s.result[m, rows] = (s.tokens[m, rows].astype(F32) + value * gate * valid).astype(BF16)
        largest = jnp.zeros((1, 1), F32)
        for j in range(tiles):
            rows = slice(j * BLOCK, (j + 1) * BLOCK)
            piece = dot(s.flat[rows], s.pre_grad[...])
            s.act_grad[rows] = piece
            largest = jnp.maximum(largest, jnp.max(jnp.abs(piece), axis=(0, 1), keepdims=True))
        largest = jnp.maximum(largest, 1e-30)
        s.scale_out[m] = jnp.broadcast_to(largest * (1.0 / STEPS), (1, BLOCK))
        s.scale_in[m, pl.ds(me, 1)] = s.scale_out[m][None]
        spread_out(s.scale_out.at[m], s.scale_in.at[m], s.scale_sem.at[m])
        factor = STEPS / largest
        for j in range(tiles):
            rows = slice(j * BLOCK, (j + 1) * BLOCK)
            coded = jnp.round(s.act_grad[rows] * factor).astype(I16)
            s.g_out[m, j * BLOCK // own : (j + 1) * BLOCK // own] = coded.reshape(-1, own, span)
        s.g_in[m, pl.ds(me, 1)] = s.g_out[m, pl.ds(me, 1)]
        scatter(s.g_out.at[m], s.g_in.at[m], s.g_sem.at[m])
        ones = jnp.ones((span, BLOCK), BF16)
        for j in range(groups):
            per = width // groups
            rows = slice(j * per, (j + 1) * per)
            piece = dot(activated[rows], s.pre_grad[...], ((1,), (1,))).reshape(pairs, 2, own, 2 * width)
            sums = dot(s.pre_grad[2 * j * per : 2 * (j + 1) * per], ones).reshape(pairs, 2, 2, own, BLOCK)
            lane3 = lax.broadcasted_iota(jnp.int32, (pairs, 2, own, BLOCK), 3)
            sums = jnp.where(lane3 == 0, sums[:, :, 0], jnp.where(lane3 == 1, sums[:, :, 1], 0.0))
            if m == 0:
                s.total[j, :, :, :, : 2 * width] = piece
                s.total[j, :, :, :, 2 * width :] = sums
            else:
                s.total[j, :, :, :, : 2 * width] += piece
                s.total[j, :, :, :, 2 * width :] += sums

    for m in range(count):
        project(m)

    def sum_hop(hop):
        if hop == 0:
            send(s.total.at[:, :, 1 - core], s.sum_core, s.sum_sem.at[0], s.sum_sem.at[1],
                 (dp, pair * 2 + 1 - core))
        elif hop == 1:
            wait_sent(s.sum_core, s.sum_sem.at[0])
            wait_sent(s.sum_core, s.sum_sem.at[1])
            for j in range(groups):
                part = s.total[j, :, pl.ds(core, 1)].reshape(pairs, own, -1) + s.sum_core[j]
                s.sum_core[j] = part
                s.sum_dp_out[j] = part.astype(BF16)
            for k in range(1, groups):
                there = lax.rem(dp + k, groups)
                send(s.sum_dp_out.at[there], s.sum_dp_in.at[dp], s.sum_sem.at[2], s.sum_sem.at[3], (there, seq))
        elif hop == 2:
            ref = s.sum_dp_in.at[pl.ds(0, groups - 1)]
            wait_sent(ref, s.sum_sem.at[2])
            wait_sent(ref, s.sum_sem.at[3])
            part = s.sum_core[dp]
            for k in range(1, groups):
                part += s.sum_dp_in[lax.rem(dp + k, groups)].astype(F32)
            s.sum_core[0] = part
            s.sum_z_out[...] = part.astype(BF16)
            for k in range(1, pairs):
                there = lax.rem(pair + k, pairs)
                send(s.sum_z_out.at[there], s.sum_z_in.at[pair], s.sum_sem.at[4], s.sum_sem.at[5],
                     (dp, there * 2 + core))
        else:
            ref = s.sum_z_in.at[pl.ds(0, pairs - 1)]
            wait_sent(ref, s.sum_sem.at[4])
            wait_sent(ref, s.sum_sem.at[5])
            part = s.sum_core[0, pl.ds(pair, 1)].reshape(own, -1)
            for k in range(1, pairs):
                part += s.sum_z_in[lax.rem(pair + k, pairs)].astype(F32)
            rows_grad[...] = part[:, : 2 * width]
            columns = part[:, 2 * width :].T
            shift_grad[...] = jnp.concatenate([columns[:1], columns[1:2]], axis=1)

    sum_hop(0)

    def add_row(ref, m, c, value):
        line = jnp.sum(value, axis=0, keepdims=True)
        if m == 0:
            ref[pl.ds(c, 1), :] = line
        else:
            ref[pl.ds(c, 1), :] += line

    def backward(m):
        arrived(s.g_in.at[m], s.g_sem.at[m])
        arrived(s.scale_in.at[m], s.scale_sem.at[m])
        rows_in(s.g_in, m)
        s.scales[...] = s.scale_in[m].reshape(devices, BLOCK)

        def body(c):
            grad = jnp.concatenate([piece * s.scales[...] for piece in gather_channel(c)], axis=0)
            grad = grad * s.slope[m, c]
            coded = rows_of(grad)
            outflow = fold_lanes(fold_rows(dot(coded, s.base[c])))
            leaving = states_after(pieces(outflow), c)
            drive_grad = fold_lanes(fold_rows(dot(coded, s.toeplitz[c], ((1,), (1,)))))
            drive_grad += fold_lanes(fold_rows(dot(rows_of(leaving), s.back[c], ((1,), (1,)))))
            drive_grad += skip[c] * grad
            norm_grad = drive_grad * s.mask[m]
            s.grad[m, c] = grad
            s.outflow[m, c] = outflow
            s.leaving[m, c] = leaving
            add_row(s.gain_rows, m, c, norm_grad * s.own_normed[m, c])
            add_row(s.bias_rows, m, c, norm_grad)
            add_row(s.skip_rows, m, c, grad * s.drive[m, c])
            put_channel(c, norm_grad * ln_gain[c])

        over_channels(body)
        rows_out(s.d_out, m)
        s.d_in[m, pl.ds(me, 1)] = s.d_out[m, pl.ds(me, 1)]
        scatter(s.d_out.at[m], s.d_in.at[m], s.d_sem.at[m])

    backward(0)
    sum_hop(1)
    for m in range(1, count):
        backward(m)
    sum_hop(2)

    def pair_sum(first, second):
        straight = jnp.sum(first * second, axis=0, keepdims=True)
        crossed = jnp.sum(first * swap(second), axis=0, keepdims=True)
        return jnp.where(low_half(straight.shape), straight - swap(straight), crossed + swap(crossed))

    def parameters(c):
        moment, ends, sides = (jnp.zeros((1, BLOCK), F32) for _ in range(3))
        lefts, rights = ([], [])
        for m in range(count):
            drive, grad = (two(s.drive[m, c]), two(s.grad[m, c]))
            entering, leaving = (s.entering[m, c], s.leaving[m, c])
            second = fold_lanes(fold_rows(dot(jnp.concatenate(drive, axis=0), s.down_ramp[c])))
            third = fold_lanes(fold_rows(dot(jnp.concatenate(grad, axis=0), s.base_ramp[c])))
            moment += pair_sum(entering, s.outflow[m, c])
            ends += pair_sum(leaving, entering)
            sides += pair_sum(leaving, second) + pair_sum(entering, third)
            lefts += [drive[0], drive[0], drive[1]]
            rights += [grad[0], grad[1], grad[0]]
        cross = dot(jnp.concatenate(lefts, axis=0), jnp.concatenate(rights, axis=0), ((0,), (0,)))
        cross = jnp.where(lane_id >= row_id, cross, 0.0)
        for bit in range(7):
            moved = pltpu.roll(cross, BLOCK - (1 << bit), 1)
            cross = jnp.where((row_id >> bit) & 1 == 1, moved, cross)
        lags = jnp.sum(cross, axis=0, keepdims=True)
        later = jnp.where(row_lane < BLOCK - 1, pltpu.roll(lags, BLOCK - 1, 1), 0.0)
        near = fold_lanes(fold_rows(dot(rows_of(jnp.broadcast_to(lags, (8, BLOCK))), s.base[c])))
        nearer = fold_lanes(fold_rows(dot(rows_of(jnp.broadcast_to(later, (8, BLOCK))), s.base_ramp[c])))
        s.moment[pl.ds(c, 1), :] = times(moment, power_of(0, c)) + near[:1]
        s.paired[pl.ds(c, 1), :] = times(ends, power_of(7, c)) * float(BLOCK) + sides + nearer[:1]

    over_channels(parameters)
    moment = s.moment[...]
    paired = times(s.paired[...], spread(coeff))
    grads = pull(
        (paired[:, :states], -paired[:, states:], moment[:, :states], -moment[:, states:])
    )
    rate_grad[...], turn_grad[...] = grads[:2]
    mixing_grad[...] = jnp.concatenate(grads[3:], axis=1)
    fill = jnp.zeros((own, BLOCK - states), F32)
    s.step_rows[...] = jnp.concatenate([grads[2], fill], axis=1)
    ones = jnp.ones((8, BLOCK), F32)
    for rows, out in (
        (s.step_rows, spacing_grad),
        (s.gain_rows, gain_grad),
        (s.bias_rows, bias_grad),
        (s.skip_rows, skip_grad),
    ):
        line = lax.dot_general(ones, rows[...], (((1,), (1,)), ((), ())), preferred_element_type=F32, precision=HIGH)
        out[...] = line[:1]
    for m in range(count):
        result[m] = s.result[m].T
    sum_hop(3)

    for m in range(count):
        arrived(s.d_in.at[m], s.d_sem.at[m])
        inverse = s.inverse[m : m + 1]
        plain = jnp.zeros((1, span), F32)
        along = jnp.zeros((1, span), F32)
        for j in range(tiles):
            scaled = s.d_in[m, j * BLOCK // own : (j + 1) * BLOCK // own].reshape(BLOCK, span).astype(F32)
            plain += jnp.sum(scaled, axis=0, keepdims=True)
            along += jnp.sum(scaled * s.normed[m, j * BLOCK : (j + 1) * BLOCK], axis=0, keepdims=True)
        plain, along = (plain * (1.0 / width), along * (1.0 / width))
        for j in range(tiles):
            rows = slice(j * BLOCK, (j + 1) * BLOCK)
            scaled = s.d_in[m, j * BLOCK // own : (j + 1) * BLOCK // own].reshape(BLOCK, span).astype(F32)
            piece = s.upstream[m, rows].astype(F32) + inverse * (scaled - plain - s.normed[m, rows] * along)
            token_grad[m, :, rows] = piece.astype(BF16).T

    for m in range(count):
        left(s.x_out.at[m], s.x_sem.at[m])
        left(s.a_out.at[m], s.a_sem.at[m])
        left(s.g_out.at[m], s.g_sem.at[m])
        left(s.scale_in.at[m], s.scale_sem.at[m])
        left(s.d_out.at[m], s.d_sem.at[m])


class Scratch:
    def __init__(self, names, refs):
        for name, ref in zip(names, refs, strict=True):
            setattr(self, name, ref)


def scratch_of(size):
    groups, parts, own, width, span, count = size
    devices, blocks, pairs = (groups * parts, span // BLOCK, parts // 2)
    rows = blocks * devices
    bits = 7 + (blocks * parts).bit_length()
    wide = 2 * width + BLOCK
    vmem, sems = (pltpu.VMEM, pltpu.SemaphoreType.DMA)
    chunks = (count, devices, own, span)
    held = vmem((count, own, rows, BLOCK), F32)
    table, stacked = (vmem((own, BLOCK, 2 * BLOCK), BF16), vmem((own, 2 * BLOCK, BLOCK), BF16))
    lines = vmem((own, BLOCK), F32)
    return {
        "tokens": vmem((count, width, span), BF16),
        "upstream": vmem((count, width, span), BF16),
        "result": vmem((count, width, span), BF16),
        "normed": vmem((count, width, span), F32),
        "inverse": vmem((count, span), F32),
        "valid": vmem((count, span), F32),
        "x_out": vmem(chunks, I16), "x_in": vmem(chunks, I16), "x_sem": sems((count, 2)),
        "a_out": vmem(chunks, BF16), "a_in": vmem(chunks, BF16), "a_sem": sems((count, 2)),
        "g_out": vmem(chunks, I16), "g_in": vmem(chunks, I16), "g_sem": sems((count, 2)),
        "d_out": vmem(chunks, BF16), "d_in": vmem(chunks, BF16), "d_sem": sems((count, 2)),
        "note_out": vmem((1, 1, BLOCK), F32), "note_in": vmem((devices, 1, BLOCK), F32), "note_sem": sems((2,)),
        "scale_out": vmem((count, 1, BLOCK), F32), "scale_in": vmem((count, devices, 1, BLOCK), F32),
        "scale_sem": sems((count, 2)),
        "scales": vmem((devices, BLOCK), F32),
        "weight": vmem((groups, pairs, 2, own, 2 * width), BF16), "weight_sem": sems((6,)),
        "flat": vmem((width, 2 * width), BF16),
        "flipped": vmem((2 * width, width), BF16),
        "shift": vmem((BLOCK, 2 * width // BLOCK), F32),
        "pre_grad": vmem((2 * width, span), BF16),
        "act_grad": vmem((width, span), F32),
        "total": vmem((groups, pairs, 2, own, wide), F32),
        "sum_core": vmem((groups, pairs, own, wide), F32),
        "sum_dp_out": vmem((groups, pairs, own, wide), BF16),
        "sum_dp_in": vmem((groups, pairs, own, wide), BF16),
        "sum_z_out": vmem((pairs, own, wide), BF16),
        "sum_z_in": vmem((pairs, own, wide), BF16),
        "sum_sem": sems((6,)),
        "power_both": vmem((bits, own, BLOCK), F32),
        "power_cross": vmem((bits, own, BLOCK), F32),
        "lead": vmem((2, own, BLOCK), F32),
        "coeff": lines,
        "base": table, "down": table, "base_ramp": table, "down_ramp": table,
        "up": stacked, "back": stacked, "toeplitz": stacked,
        "stage": vmem((blocks, devices * own, BLOCK), F32),
        "mask": vmem((count, rows, BLOCK), F32),
        "own_normed": held, "drive": held, "entering": held, "slope": held,
        "grad": held, "outflow": held, "leaving": held,
        "gain_rows": lines, "bias_rows": lines, "skip_rows": lines, "step_rows": lines,
        "moment": lines, "paired": lines,
    }


def in_one_kernel(groups, parts, *args):
    inputs, lengths, ln_gain, ln_bias, lam_log, lam_im, log_dt, mix_weight, skip, glu_weight, glu_bias, out_grad = args
    count, span, width = inputs.shape
    own = ln_gain.shape[0]
    size = (groups, parts, own, width, span, count)
    scratch = scratch_of(size)

    def kernel(*refs):
        arguments, results, kept = (refs[:12], refs[12:23], refs[23:])
        whole_kernel(size, *arguments, *results, Scratch(scratch, kept))

    vmem, smem = (pl.BlockSpec(memory_space=pltpu.VMEM), pl.BlockSpec(memory_space=pltpu.SMEM))
    line = jax.ShapeDtypeStruct((1, own), F32)
    outs = pl.pallas_call(
        kernel,
        out_shape=(
            jax.ShapeDtypeStruct(inputs.shape, BF16),
            jax.ShapeDtypeStruct(inputs.shape, BF16),
            line,
            line,
            jax.ShapeDtypeStruct(lam_log.shape, F32),
            jax.ShapeDtypeStruct(lam_im.shape, F32),
            line,
            jax.ShapeDtypeStruct(mix_weight.shape, F32),
            line,
            jax.ShapeDtypeStruct(glu_weight.shape, F32),
            jax.ShapeDtypeStruct((1, 2 * own), F32),
        ),
        in_specs=[vmem, smem, smem, smem, vmem, vmem, smem, vmem, smem, vmem, smem, vmem],
        out_specs=[vmem] * 11,
        scratch_shapes=list(scratch.values()),
        compiler_params=pltpu.CompilerParams(
            collective_id=0, has_side_effects=True, vmem_limit_bytes=60 * 1024 * 1024
        ),
    )(*args)
    return tuple(out.reshape(-1) if out.shape[0] == 1 else out for out in outs)


def solution(mesh):
    tokens, vector, matrix = (P("dp", "seq", None), P(BOTH), P(BOTH, None))
    groups, parts = (mesh.shape["dp"], mesh.shape["seq"])

    def step(*args):
        own = args[2].shape[0]
        if own % 16 == 0 and parts % 2 == 0:
            return in_one_kernel(groups, parts, *args)
        return per_device(*args)

    return jax.shard_map(
        step,
        mesh=mesh,
        in_specs=(
            tokens, P("dp"), vector, vector, matrix, matrix, vector, matrix, vector, matrix, vector, tokens,
        ),
        out_specs=(
            tokens, tokens, vector, vector, matrix, matrix, vector, matrix, vector, matrix, vector,
        ),
        check_vma=False,
    )
```

```python
import math
from functools import partial

import jax
import jax.numpy as jnp
from jax import lax
from jax.experimental import pallas as pl
from jax.experimental.pallas import tpu as pltpu
from jax.sharding import PartitionSpec as P

BLOCK = 128
EPS = 1e-05
HIGH = lax.Precision.HIGHEST
BOTH = ("dp", "seq")


def halves(packed):
    count = packed.shape[-1] // 2
    return (packed[..., :count], packed[..., count:])


def cmul(first, second):
    first_re, first_im = halves(first)
    second_re, second_im = halves(second)
    return jnp.concatenate(
        [first_re * second_re - first_im * second_im, first_re * second_im + first_im * second_re],
        axis=-1,
    )


def conjugate(packed):
    real_half, imag_half = halves(packed)
    return jnp.concatenate([real_half, -imag_half], axis=-1)


def coefficients(lam_log, lam_im, log_dt, mix_weight):
    spacing = jnp.exp(log_dt)[:, None]
    rate = jnp.exp(lam_log)
    shrink = -rate * spacing
    angle = lam_im * spacing
    scale = jnp.exp(shrink)
    decay = jnp.concatenate([scale * jnp.cos(angle), scale * jnp.sin(angle)], axis=-1)
    less_re = jnp.expm1(shrink) * jnp.cos(angle) - 2.0 * jnp.sin(0.5 * angle) ** 2
    less_im = scale * jnp.sin(angle)
    modulus = rate * rate + lam_im * lam_im
    ratio = jnp.concatenate(
        [
            (lam_im * less_im - rate * less_re) / modulus,
            -(rate * less_im + lam_im * less_re) / modulus,
        ],
        axis=-1,
    )
    return (decay, cmul(mix_weight, ratio))


def powers(decay):
    real_half, imag_half = halves(decay)
    table = jnp.concatenate([jnp.ones_like(real_half), jnp.zeros_like(imag_half)], axis=-1)[:, None]
    step = decay[:, None]
    while table.shape[1] < BLOCK:
        table = jnp.concatenate([table, cmul(step, table)], axis=1)
        step = cmul(step, step)
    return (table, step[:, 0])


def link(earlier, later):
    return (cmul(earlier[0], later[0]), cmul(later[0], earlier[1]) + later[1])


def shifted(pieces, step, back):
    leads = jnp.broadcast_to(step[:, None, None], pieces.shape)
    _, reach = lax.associative_scan(link, (leads, pieces), axis=2, reverse=back)
    none = jnp.zeros_like(reach[:, :, :1])
    if back:
        return jnp.concatenate([reach[:, :, 1:], none], axis=2)
    return jnp.concatenate([none, reach[:, :, :-1]], axis=2)


def to_owner(rows):
    count, span, width = rows.shape
    groups, parts = (lax.axis_size("dp"), lax.axis_size("seq"))
    own = width // (groups * parts)
    sent = rows.reshape(count * span, width).T.reshape(-1, own, count, span)
    held = lax.all_to_all(sent, BOTH, 0, 0, tiled=True).reshape(groups, parts, own, count, span)
    held = held.transpose(2, 0, 3, 1, 4).reshape(own, groups * count, -1, BLOCK)
    return held


def to_holder(held, count, span):
    groups, parts = (lax.axis_size("dp"), lax.axis_size("seq"))
    own = held.shape[0]
    sent = held.astype(jnp.bfloat16).reshape(own, groups, count, parts, span).transpose(1, 3, 0, 2, 4)
    sent = sent.reshape(groups * parts, own, count, span)
    rows = lax.all_to_all(sent, BOTH, 0, 0, tiled=True)
    return rows.reshape(-1, count * span).T.reshape(count, span, -1).astype(jnp.float32)


def per_device(
    inputs,
    lengths,
    ln_gain,
    ln_bias,
    lam_log,
    lam_im,
    log_dt,
    mix_weight,
    skip,
    glu_weight,
    glu_bias,
    out_grad,
):
    count, span, width = inputs.shape
    offset = lax.axis_index("seq") * span
    positions = offset + jnp.arange(span, dtype=jnp.int32)
    valid = (positions[None, :] < lengths[:, None]).astype(jnp.float32)[..., None]
    rows = lax.all_gather(glu_weight, BOTH, axis=0, tiled=True)
    shift = lax.all_gather(glu_bias, BOTH, axis=0, tiled=True)
    spans = lax.all_gather(lengths, "dp", axis=0, tiled=True)
    whole_span = span * lax.axis_size("seq")
    mask = (jnp.arange(whole_span, dtype=jnp.int32)[None] < spans[:, None]).astype(jnp.float32)
    mask = mask.reshape(1, -1, whole_span // BLOCK, BLOCK)

    tokens = inputs.astype(jnp.float32)
    mean = jnp.mean(tokens, axis=-1, keepdims=True)
    centered = tokens - mean
    inverse = lax.rsqrt(jnp.mean(centered * centered, axis=-1, keepdims=True) + EPS)
    normed = centered * inverse

    (decay, coeff), coeff_pull = jax.vjp(coefficients, lam_log, lam_im, log_dt, mix_weight)
    base, whole = powers(decay)
    down = base[:, ::-1]
    real_half, imag_half = halves(coeff)
    kernel = jnp.einsum("cz,ckz->ck", conjugate(coeff), base, precision=HIGH)
    lead = cmul(coeff, decay)[:, None]
    up = conjugate(cmul(lead, base))
    back = conjugate(cmul(lead, down))
    steps = jnp.arange(BLOCK)
    lag = steps[:, None] - steps[None, :]
    toeplitz = jnp.where(lag >= 0, kernel[:, jnp.maximum(lag, 0)], 0.0)
    ramp = steps.astype(jnp.float32)[:, None]

    gain, bias, skipping = (p[:, None, None, None] for p in (ln_gain, ln_bias, skip))
    own_normed = to_owner(normed)
    drive = (own_normed * gain + bias) * mask
    entering = shifted(jnp.einsum("cbqj,cjz->cbqz", drive, down, precision=HIGH), whole, False)
    response = jnp.einsum("cij,cbqj->cbqi", toeplitz, drive, precision=HIGH)
    response += jnp.einsum("ciz,cbqz->cbqi", up, entering, precision=HIGH) + skipping * drive
    activated, gelu_pull = jax.vjp(partial(jax.nn.gelu, approximate=False), response)
    activated = to_holder(activated, count, span).astype(jnp.bfloat16).reshape(-1, width)
    pre = jnp.dot(activated, rows, preferred_element_type=jnp.float32) + shift
    gate = jax.nn.sigmoid(pre[:, width:])
    flat_valid = valid.reshape(-1, 1)
    result = (tokens + (pre[:, :width] * gate * flat_valid).reshape(tokens.shape)).astype(jnp.bfloat16)
    upstream = out_grad.astype(jnp.float32)
    gated = upstream.reshape(-1, width) * flat_valid
    pre_grad = jnp.concatenate(
        [gated * gate, gated * pre[:, :width] * gate * (1.0 - gate)], axis=-1
    ).astype(jnp.bfloat16)
    rows_grad = lax.dot_general(
        activated, pre_grad, (((0,), (0,)), ((), ())), preferred_element_type=jnp.float32
    )
    shift_grad = jnp.sum(pre_grad.astype(jnp.float32), axis=0)
    act_grad = lax.dot_general(
        pre_grad, rows, (((1,), (1,)), ((), ())), preferred_element_type=jnp.float32
    )
    response_grad = gelu_pull(to_owner(act_grad.reshape(tokens.shape)))[0]

    skip_grad = jnp.sum(response_grad * drive, axis=(1, 2, 3))
    outflow = jnp.einsum("cbqt,ctz->cbqz", response_grad, base, precision=HIGH)
    leaving = shifted(outflow, whole, True)
    drive_grad = jnp.einsum("cij,cbqi->cbqj", toeplitz, response_grad, precision=HIGH)
    drive_grad += jnp.einsum("cjz,cbqz->cbqj", back, leaving, precision=HIGH) + skipping * response_grad
    norm_grad = drive_grad * mask
    gain_grad = jnp.sum(norm_grad * own_normed, axis=(1, 2, 3))
    bias_grad = jnp.sum(norm_grad, axis=(1, 2, 3))
    scaled = to_holder(norm_grad * gain, count, span)
    token_grad = upstream + inverse * (
        scaled
        - jnp.mean(scaled, axis=-1, keepdims=True)
        - normed * jnp.mean(scaled * normed, axis=-1, keepdims=True)
    )

    cross = jnp.einsum("cbqj,cbqi->cij", drive, response_grad, precision=HIGH)
    lags = jnp.stack([jnp.trace(cross, offset=-k, axis1=1, axis2=2) for k in range(BLOCK)], axis=-1)
    second = jnp.einsum("cbqj,cjz->cbqz", drive, down * ramp[::-1], precision=HIGH)
    third = jnp.einsum("cbqt,ctz->cbqz", response_grad, base * (ramp + 1.0), precision=HIGH)
    total = partial(jnp.sum, axis=(1, 2))
    moment = cmul(decay, total(cmul(entering, outflow))) + jnp.einsum("ck,ckz->cz", lags, base, precision=HIGH)
    before = jnp.concatenate([jnp.zeros_like(base[:, :1]), base[:, :-1]], axis=1) * ramp
    paired = BLOCK * cmul(whole, total(cmul(leaving, entering)))
    paired += total(cmul(leaving, second) + cmul(entering, third))
    paired = cmul(coeff, paired + jnp.einsum("ck,ckz->cz", lags, before, precision=HIGH))
    rate_grad, turn_grad, spacing_grad, mixing_grad = coeff_pull((conjugate(paired), conjugate(moment)))

    scatter = partial(lax.psum_scatter, axis_name=BOTH, scatter_dimension=0, tiled=True)
    return (
        result,
        token_grad.astype(jnp.bfloat16),
        gain_grad,
        bias_grad,
        rate_grad,
        turn_grad,
        spacing_grad,
        mixing_grad,
        skip_grad,
        scatter(rows_grad),
        scatter(shift_grad),
    )


MESH = pl.DeviceIdType.MESH
F32, BF16, I16 = (jnp.float32, jnp.bfloat16, jnp.int16)
STEPS = 32700.0
GROUP = 4
HALVES = 2


def two(value):
    high = value.astype(BF16)
    return (high, (value - high.astype(F32)).astype(BF16))


def dot(left, right, dims=((1,), (0,))):
    return lax.dot_general(left, right, (dims, ((), ())), preferred_element_type=F32)


TURNED = ((1,), (1,))
SIDEWAYS = ((0,), (0,))


def product(left, table, dims=((1,), (0,))):
    return dot(left[0], table[0], dims) + dot(left[1], table[0], dims) + dot(left[0], table[1], dims)


def times(value, factor):
    return (value[0] * factor[0] - value[1] * factor[1], value[0] * factor[1] + value[1] * factor[0])


def plus(first, second):
    return (first[0] + second[0], first[1] + second[1])


def choose(condition, first, second):
    return (jnp.where(condition, first[0], second[0]), jnp.where(condition, first[1], second[1]))


def split(value):
    return (value[:, :BLOCK], value[:, BLOCK:])


def beside(*parts):
    return jnp.concatenate(parts, axis=1)


def over(*parts):
    return jnp.concatenate(parts, axis=0)


def total_rows(value):
    return jnp.sum(value, axis=0, keepdims=True)


def small_expm1(value):
    near = jnp.abs(value) < 0.5
    small = jnp.where(near, value, 0.0)
    series = jnp.ones_like(small)
    for order in range(10, 1, -1):
        series = 1.0 + small * (1.0 / order) * series
    return jnp.where(near, small * series, jnp.exp(value) - 1.0)


def coefficient_parts(lam_log, lam_im, log_dt, mix_re, mix_im):
    spacing, rate = (jnp.exp(log_dt), jnp.exp(lam_log))
    shrink, angle = (-rate * spacing, lam_im * spacing)
    scale = jnp.exp(shrink)
    cosine, sine, half = (jnp.cos(angle), jnp.sin(angle), jnp.sin(0.5 * angle))
    less_re = small_expm1(shrink) * cosine - 2.0 * half * half
    less_im = scale * sine
    modulus = rate * rate + lam_im * lam_im
    ratio = (
        (lam_im * less_im - rate * less_re) / modulus,
        -(rate * less_im + lam_im * less_re) / modulus,
    )
    return (scale * cosine, less_im) + times((mix_re, mix_im), ratio)


def whole_kernel(
    size,
    inputs, lengths, ln_gain, ln_bias, lam_log, lam_im, log_dt, mix_weight, skip, glu_weight, glu_bias, out_grad,
    result, token_grad, gain_grad, bias_grad, rate_grad, turn_grad, spacing_grad, mixing_grad, skip_grad,
    rows_grad, shift_grad,
    s,
):
    groups, parts, own, width, span, count = size
    local, blocks, zs = (parts // HALVES, span // BLOCK, parts // 2)
    members = groups * local
    tiles, couples, states = (width // BLOCK, own // 2, lam_log.shape[1])
    wide = 2 * width
    dp, seq = (lax.axis_index("dp"), lax.axis_index("seq"))
    core, z = (lax.rem(seq, 2), seq // 2)
    half, here = (seq // local, lax.rem(seq, local))
    other = 1 - half
    me = dp * local + here
    partner = (dp, other * local + here)

    def place(member):
        return (member // local, half * local + lax.rem(member, local))

    def send(source, target, sems, device):
        pltpu.make_async_remote_copy(
            src_ref=source, dst_ref=target, send_sem=sems.at[0], recv_sem=sems.at[1],
            device_id=device, device_id_type=MESH,
        ).start()

    def wait_for(ref, sem):
        pltpu.make_async_copy(ref, ref, sem).wait()

    def to_owners(out, into, sems):
        def one(k, carry):
            member = lax.rem(me + k, members)
            send(out.at[member // local, lax.rem(member, local)], into.at[me], sems, place(member))
            return carry

        lax.fori_loop(1, members, one, 0)

    def to_holders(out, into, sems):
        def one(k, carry):
            member = lax.rem(me + k, members)
            send(out.at[member], into.at[dp, here], sems, place(member))
            return carry

        lax.fori_loop(1, members, one, 0)

    def to_all(out, into, sems):
        def one(k, carry):
            send(out, into.at[me], sems, place(lax.rem(me + k, members)))
            return carry

        lax.fori_loop(1, members, one, 0)

    def many(ref):
        return ref.at[pl.ds(0, members - 1)]

    barrier = pltpu.get_barrier_semaphore()

    def greet(k, carry):
        member = place(lax.rem(me + k, members))
        pl.semaphore_signal(barrier, inc=1, device_id=member, device_id_type=MESH)
        return carry

    lax.fori_loop(1, members, greet, 0)
    for k in range(zs // HALVES):
        there = other * local + 2 * k + core
        pl.semaphore_signal(barrier, inc=1, device_id=(dp, there), device_id_type=MESH)

    lane = lax.broadcasted_iota(jnp.int32, (1, span), 1) + seq * span
    quantum = math.sqrt(width) / STEPS

    def chunk_rows(j):
        per = BLOCK // own
        for i in range(per):
            shard = j * per + i
            yield slice(i * own, (i + 1) * own), shard // parts, shard % parts // local, shard % local

    def norm(m):
        tokens = inputs[m].T
        s.tokens[m] = tokens
        total = jnp.zeros((1, span), F32)
        for j in range(tiles):
            total += total_rows(tokens[j * BLOCK : (j + 1) * BLOCK].astype(F32))
        mean = total * (1.0 / width)
        total = jnp.zeros((1, span), F32)
        for j in range(tiles):
            off = tokens[j * BLOCK : (j + 1) * BLOCK].astype(F32) - mean
            total += total_rows(off * off)
        inverse = lax.rsqrt(total * (1.0 / width) + EPS)
        valid = (lane < lengths[m]).astype(F32)
        s.inverse[m : m + 1] = inverse
        s.valid[m : m + 1] = valid
        for j in range(tiles):
            normed = (tokens[j * BLOCK : (j + 1) * BLOCK].astype(F32) - mean) * inverse
            s.normed[m, j * BLOCK : (j + 1) * BLOCK] = normed
            coded = jnp.round(normed * valid * (1.0 / quantum)).astype(I16)
            for rows, a, k, p in chunk_rows(j):
                s.x_out[k, m, a, p] = coded[rows]
        for k in range(HALVES):
            s.x_in[k, m, pl.ds(me, 1)] = s.x_out[k, m, dp, pl.ds(here, 1)]

    for m in range(count):
        norm(m)

    row_lane = lax.broadcasted_iota(jnp.int32, (1, BLOCK), 1)
    row = jnp.zeros((1, BLOCK), F32)
    for m in range(count):
        row = jnp.where(row_lane == m, lengths[m].astype(F32), row)
    s.note_out[0] = row
    s.note_in[pl.ds(me, 1)] = row[None]

    own_row = lax.broadcasted_iota(jnp.int32, (own, BLOCK), 0)
    own_lane = lax.broadcasted_iota(jnp.int32, (own, BLOCK), 1)
    scalars = jnp.zeros((own, BLOCK), F32)
    shifts = jnp.zeros((own, BLOCK), F32)
    for c in range(own):
        for i, ref in enumerate((log_dt, ln_gain, ln_bias, skip)):
            scalars = jnp.where((own_row == c) & (own_lane == i), ref[c], scalars)
        for i in range(2):
            shifts = jnp.where((own_row == c) & (own_lane % 2 == i), glu_bias[i * own + c], shifts)
    s.params[pl.ds(half, 1), :, :states] = lam_log[...][None]
    s.params[pl.ds(half, 1), :, states : 2 * states] = lam_im[...][None]
    s.params[pl.ds(half, 1), :, BLOCK : 2 * BLOCK] = mix_weight[...][None]
    s.params[pl.ds(half, 1), :, 2 * BLOCK :] = scalars[None]
    high = shifts.astype(BF16)
    rest = shifts - high.astype(F32)
    middle = rest.astype(BF16)
    lowest = (rest - middle.astype(F32)).astype(BF16)
    thirds = jnp.where(own_lane < 2, high, jnp.where(own_lane < 4, middle, lowest))
    s.weight_out[:, :wide] = glu_weight[...]
    s.weight_out[:, wide:] = thirds
    s.weight[pl.ds(dp, 1), pl.ds(z, 1), pl.ds(core, 1)] = s.weight_out[...][None, None, None]

    def weight_hop(hop):
        sems = s.weight_sem.at[hop]
        if hop == 0:
            for k in range(1, zs):
                there = lax.rem(z + k, zs)
                send(s.weight_out, s.weight.at[dp, z, core], sems, (dp, there * 2 + core))
        elif hop == 1:
            for k in range(1, groups):
                mine = s.weight.at[dp, :, core]
                send(mine, mine, sems, (lax.rem(dp + k, groups), seq))
        else:
            mine = s.weight.at[:, :, core]
            send(mine, mine, sems, (dp, z * 2 + 1 - core))

    def weight_wait(hop):
        if hop == 0:
            ref = s.weight.at[0, pl.ds(0, zs - 1), 0]
        elif hop == 1:
            ref = s.weight.at[pl.ds(0, groups - 1), :, 0]
        else:
            ref = s.weight.at[:, :, 0]
        wait_for(ref, s.weight_sem.at[hop, 0])
        wait_for(ref, s.weight_sem.at[hop, 1])

    pl.semaphore_wait(barrier, members - 1 + zs // HALVES)
    send(s.params.at[half], s.params.at[half], s.params_sem, partner)
    to_all(s.note_out.at[0], s.note_in, s.note_sem)
    for k in range(HALVES):
        for m in range(count):
            to_owners(s.x_out.at[k, m], s.x_in.at[k, m], s.x_sem.at[k, m])
    weight_hop(0)

    wait_for(s.params.at[0], s.params_sem.at[0])
    wait_for(s.params.at[0], s.params_sem.at[1])
    pair_low = lax.broadcasted_iota(jnp.int32, (couples, BLOCK), 1) < states

    def coupled(value):
        s.turn[...] = value
        even = s.turn[pl.ds(0, couples, stride=2), :]
        odd = s.turn[pl.ds(1, couples, stride=2), :]
        return jnp.where(pair_low, even, pltpu.roll(odd, states, 1))

    def raw_params(k):
        packed = [s.params[k, :, i * BLOCK : (i + 1) * BLOCK] for i in range(3)]
        lam, mix, rest = packed
        log_step = jnp.broadcast_to(rest[:, :1], (own, BLOCK))
        return tuple(
            coupled(value)
            for value in (lam, pltpu.roll(lam, states, 1), log_step, mix, pltpu.roll(mix, states, 1))
        )

    for k in range(HALVES):
        rest = s.params[k, :, 2 * BLOCK :]
        for i in range(1, 4):
            s.scalars[i - 1, k * own : (k + 1) * own] = jnp.broadcast_to(rest[:, i : i + 1], (own, BLOCK))
        parts_k = coefficient_parts(*raw_params(k))
        rows = slice(k * couples, (k + 1) * couples)
        decay, coeff = (parts_k[:2], parts_k[2:])
        s.coeff[0, rows], s.coeff[1, rows] = coeff
        s.lead[0, rows], s.lead[1, rows] = times(coeff, decay)
        power = decay
        for bit in range(s.power.shape[0]):
            s.power[bit, 0, rows], s.power[bit, 1, rows] = power
            power = times(power, power)

    def power_of(bit, p):
        return (s.power[bit, 0, pl.ds(p, 1), :], s.power[bit, 1, pl.ds(p, 1), :])

    square = (BLOCK, BLOCK)
    row_id = lax.broadcasted_iota(jnp.int32, square, 0)
    lane_id = lax.broadcasted_iota(jnp.int32, square, 1)
    ramp = row_id.astype(F32)
    first_states = lax.rem(lax.broadcasted_iota(jnp.int32, (BLOCK, 2 * BLOCK), 1), BLOCK) < states

    def stacked(value):
        none = jnp.zeros_like(value)
        return over(jnp.where(first_states, value, none), jnp.where(first_states, none, value))

    def put_table(ref, p, value):
        for i, part in enumerate(two(beside(*value))):
            ref[p, i] = stacked(part)

    def tables(p):
        eight = row_id[:8]
        unit = (jnp.ones((8, BLOCK), F32), jnp.zeros((8, BLOCK), F32))
        base, down = (unit, unit)
        for bit in range(3):
            step = power_of(bit, p)
            base = choose((eight >> bit) & 1 == 1, times(base, step), base)
            down = choose(((7 - eight) >> bit) & 1 == 1, times(down, step), down)
        for bit in range(3, 7):
            step = power_of(bit, p)
            more, most = (times(base, step), times(down, step))
            base = (over(base[0], more[0]), over(base[1], more[1]))
            down = (over(most[0], down[0]), over(most[1], down[1]))
        lead = (s.lead[0, pl.ds(p, 1), :], s.lead[1, pl.ds(p, 1), :])
        up, back = (times(base, lead), times(down, lead))
        put_table(s.base, p, base)
        put_table(s.down, p, down)
        put_table(s.up, p, (up[0], -up[1]))
        put_table(s.back, p, (back[0], -back[1]))
        for ref, value, slope in (
            (s.base_ramp, base, ramp + 1.0),
            (s.down_ramp, down, BLOCK - 1.0 - ramp),
        ):
            ref[p] = stacked(beside(value[0] * slope, value[1] * slope).astype(BF16))
        weights = beside(s.coeff[0, pl.ds(p, 1), :], -s.coeff[1, pl.ds(p, 1), :])
        weights = jnp.broadcast_to(weights, (8, 2 * BLOCK))
        pick = lax.rem(lax.broadcasted_iota(jnp.int32, (8, 2 * BLOCK), 1), BLOCK) < states
        pick = pick == (lax.broadcasted_iota(jnp.int32, (8, 2 * BLOCK), 0) == 0)
        kernel = lax.dot_general(
            jnp.where(pick, weights, 0.0), beside(*base), (TURNED, ((), ())),
            preferred_element_type=F32, precision=HIGH,
        )
        for i in range(2):
            slanted = jnp.broadcast_to(kernel[i : i + 1], square)
            slanted = pltpu.roll(slanted, 0, 1, stride=1, stride_axis=0)
            side = slice(i * BLOCK, (i + 1) * BLOCK)
            off = slice((1 - i) * BLOCK, (2 - i) * BLOCK)
            for part, value in enumerate(two(jnp.where(lane_id >= row_id, slanted, 0.0))):
                s.toeplitz[p, part, side, side] = value
                s.toeplitz[p, part, side, off] = jnp.zeros(square, BF16)

    def over_couples(k, body, group=GROUP):
        def some(g, carry):
            for u in range(group):
                body(k * couples + g * group + u, g * group + u)
            return carry

        lax.fori_loop(0, couples // group, some, 0)

    for k in range(HALVES):
        over_couples(k, lambda p, c: tables(p), 2)

    half_rows = count * members
    full_rows = blocks * half_rows
    place_of = lax.rem(lax.broadcasted_iota(jnp.int32, (half_rows, BLOCK), 0), local)
    place_lane = lax.broadcasted_iota(jnp.int32, (half_rows, BLOCK), 1)
    step_bit = 7 + blocks.bit_length() - 1

    def rows_in(ref, k):
        for m in range(count):
            for q in range(blocks):
                piece = ref[k, m, :, :, q * BLOCK : (q + 1) * BLOCK]
                s.stage_in[q, m] = piece.astype(F32).reshape(members * own, BLOCK)

    def rows_out(ref, k):
        for m in range(count):
            for q in range(blocks):
                ref[k, m, :, :, q * BLOCK : (q + 1) * BLOCK] = (
                    s.stage_out[q, m].astype(BF16).reshape(members, own, BLOCK)
                )

    def gather_couple(c):
        sides = []
        for i in range(2):
            sides.append(
                over(
                    *(
                        s.stage_in[q, m, pl.ds(2 * c + i, members, stride=own), :]
                        for q in range(blocks)
                        for m in range(count)
                    )
                )
            )
        return beside(*sides)

    def put_couple(c, value):
        for i, side in enumerate(split(value)):
            for q in range(blocks):
                for m in range(count):
                    first = (q * count + m) * members
                    s.stage_out[q, m, pl.ds(2 * c + i, members, stride=own), :] = side[first : first + members]

    def scalar_rows(i, p):
        return beside(s.scalars[i, pl.ds(2 * p, 1), :], s.scalars[i, pl.ds(2 * p + 1, 1), :])

    def by_block(value):
        return [split(value[q * half_rows : (q + 1) * half_rows]) for q in range(blocks)]

    def scan(flows, p, upward):
        block_step = power_of(7, p)
        flows = flows if upward else flows[::-1]
        total = flows[0]
        for flow in flows[1:]:
            total = plus(times(total, block_step), flow)

        def moved(value, reach):
            shift = reach if upward else half_rows - reach
            inside = place_of >= reach if upward else place_of < local - reach
            return tuple(jnp.where(inside, pltpu.roll(part, shift, 0), 0.0) for part in value)

        reach = 1
        while reach < local:
            total = plus(total, times(moved(total, reach), power_of(step_bit + reach.bit_length() - 1, p)))
            reach *= 2
        return moved(total, 1), total

    def carried(state, ref, p, upward):
        for j in range(local):
            for i in range(2):
                s.widen[p, i, pl.ds(j, count * groups, stride=local), :] = ref[p, i]
        carry = (s.widen[p, 0], s.widen[p, 1])
        distance = place_of if upward else local - 1 - place_of
        for bit in range(local.bit_length() - 1):
            further = times(carry, power_of(step_bit + bit, p))
            carry = choose((distance >> bit) & 1 == 1, further, carry)
        return plus(state, carry)

    def through(state, flows, p, upward):
        block_step = power_of(7, p)
        listing = [state]
        flows = flows if upward else flows[::-1]
        for flow in flows[:-1]:
            state = plus(times(state, block_step), flow)
            listing.append(state)
        listing = listing if upward else listing[::-1]
        return over(*(beside(*state) for state in listing))

    def read_notes():
        wait_for(many(s.note_in), s.note_sem.at[1])
        notes = s.note_in[...].reshape(members, BLOCK)
        member_lane = lax.broadcasted_iota(jnp.int32, (members, BLOCK), 1)
        member_place = lax.rem(lax.broadcasted_iota(jnp.int32, (members, BLOCK), 0), local)
        start = (half * local + member_place) * span + member_lane
        for m in range(count):
            length = jnp.sum(jnp.where(member_lane == m, notes, 0.0), axis=1, keepdims=True)
            for q in range(blocks):
                first = (q * count + m) * members
                within = ((start + q * BLOCK).astype(F32) < length).astype(F32)
                s.mask[first : first + members] = beside(within, within)

    def pick_last(p, total, out, first):
        for i in range(2):
            s.widen[p, i] = total[i]
            out[p, i] = s.widen[p, i, pl.ds(first, count * groups, stride=local), :]

    def forward_first(k):
        for m in range(count):
            wait_for(many(s.x_in.at[k, m]), s.x_sem.at[k, m, 1])
        rows_in(s.x_in, k)

        def inflow(p, c):
            own_normed = gather_couple(c) * quantum
            drive = (own_normed * scalar_rows(0, p) + scalar_rows(1, p)) * s.mask[...]
            s.own_normed[p] = own_normed
            s.drive[p] = drive
            s.inflow[p] = product(two(drive), s.down[p])

        over_couples(k, inflow)

        def scanned(p, c):
            state, total = scan(by_block(s.inflow[p]), p, True)
            s.entering[p, :half_rows] = beside(*state)
            pick_last(p, total, s.carry_out, local - 1)

        over_couples(k, scanned)
        rows = pl.ds(k * couples, couples)

        @pl.when(half == 0)
        def _():
            send(s.carry_out.at[rows], s.carry_in.at[rows], s.carry_sem.at[k], partner)

    def forward_second(k):
        rows = pl.ds(k * couples, couples)

        @pl.when(half == 0)
        def _():
            s.carry_in[rows] = jnp.zeros((couples, 2, count * groups, BLOCK), F32)

        @pl.when(half == 1)
        def _():
            wait_for(s.carry_in.at[rows], s.carry_sem.at[k, 1])

        def complete(p, c):
            state = carried(split(s.entering[p, :half_rows]), s.carry_in, p, True)
            s.entering[p] = through(state, by_block(s.inflow[p]), p, True)

        over_couples(k, complete)

        def respond(p, c):
            drive = s.drive[p]
            response = product(two(drive), s.toeplitz[p])
            response += product(two(s.entering[p]), s.up[p], TURNED)
            response += scalar_rows(2, p) * drive
            share_below = 0.5 * (1.0 + lax.erf(response * math.sqrt(0.5)))
            density = jnp.exp(-0.5 * response * response) * (1.0 / math.sqrt(2.0 * math.pi))
            s.slope[p] = share_below + response * density
            put_couple(c, response * share_below)

        over_couples(k, respond)
        rows_out(s.a_out, k)
        for m in range(count):
            s.a_in[m, dp, k, pl.ds(here, 1)] = s.a_out[k, m, pl.ds(me, 1)]
            to_holders(s.a_out.at[k, m], s.a_in.at[m, :, k], s.a_sem.at[k, m])

    read_notes()
    for k in range(HALVES):
        forward_first(k)
        if k == 0:
            weight_wait(0)
            weight_hop(1)
    for k in range(HALVES):
        forward_second(k)
        if k == 0:
            weight_wait(1)
            weight_hop(2)

    for m in range(count):
        s.upstream[m] = out_grad[m].T
    weight_wait(2)
    for j in range(tiles):
        rows = slice(j * BLOCK, (j + 1) * BLOCK)
        per = BLOCK // own
        flat = s.weight[...].reshape(-1, own, wide + BLOCK)[j * per : (j + 1) * per].reshape(BLOCK, -1)
        s.flat[rows] = flat[:, :wide]
        s.flipped[:, rows] = flat[:, :wide].T
        shifts = flat[:, wide:].astype(F32)
        shifts = shifts + pltpu.roll(shifts, BLOCK - 2, 1) + pltpu.roll(shifts, BLOCK - 4, 1)
        for i in range(2):
            column = jnp.broadcast_to(shifts[:, i : i + 1], (BLOCK, BLOCK)).reshape(per, own, BLOCK)
            for n in range(per):
                first = ((j * per + n) * 2 + i) * own
                s.shift[first : first + own] = column[n]

    def project(m):
        for k in range(HALVES):
            ref = s.a_out.at[k, m, pl.ds(0, members - 1)]
            wait_for(ref, s.a_sem.at[k, m, 1])
        activated = s.a_in[m].reshape(width, span)
        valid = s.valid[m : m + 1]
        for j in range(tiles):
            rows = slice(j * BLOCK, (j + 1) * BLOCK)
            gates = slice(width + j * BLOCK, width + (j + 1) * BLOCK)
            value = dot(s.flipped[rows], activated) + beside(*[s.shift[rows]] * blocks)
            gate = jax.nn.sigmoid(dot(s.flipped[gates], activated) + beside(*[s.shift[gates]] * blocks))
            gated = s.upstream[m, rows].astype(F32) * valid
            s.pre_grad[rows] = (gated * gate).astype(BF16)
            s.pre_grad[gates] = (gated * value * gate * (1.0 - gate)).astype(BF16)
            s.result[m, rows] = (s.tokens[m, rows].astype(F32) + value * gate * valid).astype(BF16)
        largest = jnp.zeros((1, 1), F32)
        for j in range(tiles):
            rows = slice(j * BLOCK, (j + 1) * BLOCK)
            piece = dot(s.flat[rows], s.pre_grad[...])
            s.act_grad[rows] = piece
            largest = jnp.maximum(largest, jnp.max(jnp.abs(piece), axis=(0, 1), keepdims=True))
        largest = jnp.maximum(largest, 1e-30)
        s.scale_out[m] = jnp.broadcast_to(largest * (1.0 / STEPS), (1, BLOCK))
        s.scale_in[m, pl.ds(me, 1)] = s.scale_out[m][None]
        to_all(s.scale_out.at[m], s.scale_in.at[m], s.scale_sem.at[m])
        factor = STEPS / largest
        for j in range(tiles):
            coded = jnp.round(s.act_grad[j * BLOCK : (j + 1) * BLOCK] * factor).astype(I16)
            for rows, a, k, p in chunk_rows(j):
                s.g_out[k, m, a, p] = coded[rows]
        for k in range(HALVES):
            s.g_in[k, m, pl.ds(me, 1)] = s.g_out[k, m, dp, pl.ds(here, 1)]
            to_owners(s.g_out.at[k, m], s.g_in.at[k, m], s.g_sem.at[k, m])
        ones = jnp.ones((span, BLOCK), BF16)
        for j in range(groups):
            per = width // groups
            rows = slice(j * per, (j + 1) * per)
            piece = dot(activated[rows], s.pre_grad[...], TURNED).reshape(zs, 2, own, wide)
            sums = dot(s.pre_grad[2 * j * per : 2 * (j + 1) * per], ones).reshape(zs, 2, 2, own, BLOCK)
            lane4 = lax.broadcasted_iota(jnp.int32, (zs, 2, own, BLOCK), 3)
            sums = jnp.where(lane4 == 0, sums[:, :, 0], jnp.where(lane4 == 1, sums[:, :, 1], 0.0))
            if m == 0:
                s.total[j, :, :, :, :wide] = piece
                s.total[j, :, :, :, wide:] = sums
            else:
                s.total[j, :, :, :, :wide] += piece
                s.total[j, :, :, :, wide:] += sums

    for m in range(count):
        project(m)

    def sum_hop(hop):
        sems = s.sum_sem
        if hop == 0:
            send(s.total.at[:, :, 1 - core], s.sum_core, sems.at[0], (dp, z * 2 + 1 - core))
        elif hop == 1:
            wait_for(s.sum_core, sems.at[0, 0])
            wait_for(s.sum_core, sems.at[0, 1])
            for j in range(groups):
                part = s.total[j, :, pl.ds(core, 1)].reshape(zs, own, -1) + s.sum_core[j]
                s.sum_core[j] = part
                s.sum_dp_out[j] = part.astype(BF16)
            for k in range(1, groups):
                there = lax.rem(dp + k, groups)
                send(s.sum_dp_out.at[there], s.sum_dp_in.at[dp], sems.at[1], (there, seq))
        elif hop == 2:
            ref = s.sum_dp_in.at[pl.ds(0, groups - 1)]
            wait_for(ref, sems.at[1, 0])
            wait_for(ref, sems.at[1, 1])
            part = s.sum_core[dp]
            for k in range(1, groups):
                part += s.sum_dp_in[lax.rem(dp + k, groups)].astype(F32)
            s.sum_core[0] = part
            s.sum_z_out[...] = part.astype(BF16)
            for k in range(1, zs):
                there = lax.rem(z + k, zs)
                send(s.sum_z_out.at[there], s.sum_z_in.at[z], sems.at[2], (dp, there * 2 + core))
        else:
            ref = s.sum_z_in.at[pl.ds(0, zs - 1)]
            wait_for(ref, sems.at[2, 0])
            wait_for(ref, sems.at[2, 1])
            part = s.sum_core[0, pl.ds(z, 1)].reshape(own, -1)
            for k in range(1, zs):
                part += s.sum_z_in[lax.rem(z + k, zs)].astype(F32)
            rows_grad[...] = part[:, :wide]
            columns = part[:, wide:].T
            shift_grad[...] = beside(columns[:1], columns[1:2])

    sum_hop(0)

    def backward_first(k):
        for m in range(count):
            wait_for(many(s.g_in.at[k, m]), s.g_sem.at[k, m, 1])
            if k == 0:
                wait_for(many(s.scale_in.at[m]), s.scale_sem.at[m, 1])
                scale = s.scale_in[m].reshape(members, BLOCK)
                for q in range(blocks):
                    first = (q * count + m) * members
                    s.scales[first : first + members] = beside(scale, scale)
        rows_in(s.g_in, k)

        def outflow(p, c):
            grad = gather_couple(c) * s.scales[...] * s.slope[p]
            s.grad[p] = grad
            s.outflow[p] = product(two(grad), s.base[p])

        over_couples(k, outflow)

        def scanned(p, c):
            state, total = scan(by_block(s.outflow[p]), p, False)
            s.leaving[p, full_rows - half_rows :] = beside(*state)
            pick_last(p, total, s.back_out, 0)

        over_couples(k, scanned)
        rows = pl.ds(k * couples, couples)

        @pl.when(half == 1)
        def _():
            send(s.back_out.at[rows], s.back_in.at[rows], s.back_sem.at[k], partner)

    def backward_second(k):
        rows = pl.ds(k * couples, couples)

        @pl.when(half == 1)
        def _():
            s.back_in[rows] = jnp.zeros((couples, 2, count * groups, BLOCK), F32)

        @pl.when(half == 0)
        def _():
            wait_for(s.back_in.at[rows], s.back_sem.at[k, 1])

        def complete(p, c):
            state = carried(split(s.leaving[p, full_rows - half_rows :]), s.back_in, p, False)
            s.leaving[p] = through(state, by_block(s.outflow[p]), p, False)

        over_couples(k, complete)

        def respond(p, c):
            grad = s.grad[p]
            drive_grad = product(two(grad), s.toeplitz[p], TURNED)
            drive_grad += product(two(s.leaving[p]), s.back[p], TURNED)
            drive_grad += scalar_rows(2, p) * grad
            norm_grad = drive_grad * s.mask[...]
            for i, value in enumerate((norm_grad * s.own_normed[p], norm_grad, grad * s.drive[p])):
                for side, line in enumerate(split(total_rows(value))):
                    s.part[k, pl.ds(4 * couples + i * own + 2 * c + side, 1), :] = line
            put_couple(c, norm_grad * scalar_rows(0, p))

        over_couples(k, respond)
        rows_out(s.d_out, k)
        for m in range(count):
            s.d_in[m, dp, k, pl.ds(here, 1)] = s.d_out[k, m, pl.ds(me, 1)]
            to_holders(s.d_out.at[k, m], s.d_in.at[m, :, k], s.d_sem.at[k, m])

    for k in range(HALVES):
        backward_first(k)
        if k == 0:
            sum_hop(1)
    for k in range(HALVES):
        backward_second(k)
    sum_hop(2)

    def sum_of_products(first, second):
        (a, b), (c, d) = (split(first), split(second))
        return (total_rows(a * c - b * d), total_rows(a * d + b * c))

    def correlate(p, c):
        drive, grad = (two(s.drive[p]), two(s.grad[p]))
        entering, leaving = (s.entering[p], s.leaving[p])
        second = dot(drive[0], s.down_ramp[p]) + dot(drive[1], s.down_ramp[p])
        third = dot(grad[0], s.base_ramp[p]) + dot(grad[1], s.base_ramp[p])
        moment = times(sum_of_products(entering, s.outflow[p]), power_of(0, p))
        paired = times(sum_of_products(leaving, entering), power_of(7, p))
        paired = (paired[0] * float(BLOCK), paired[1] * float(BLOCK))
        paired = plus(paired, plus(sum_of_products(leaving, second), sum_of_products(entering, third)))
        for i, line in enumerate(moment + paired):
            s.sums[i, pl.ds(p, 1), :] = line
        for side in range(2):
            lanes = slice(side * BLOCK, (side + 1) * BLOCK)
            left = over(drive[0][:, lanes], drive[1][:, lanes], drive[0][:, lanes])
            right = over(grad[0][:, lanes], grad[0][:, lanes], grad[1][:, lanes])
            cross = jnp.where(lane_id >= row_id, dot(left, right, SIDEWAYS), 0.0)
            lags = cross[:8]
            for i in range(1, BLOCK // 8):
                lags = lags + pltpu.roll(cross[8 * i : 8 * i + 8], BLOCK - 8 * i, 1)
            for bit in range(3):
                moved = pltpu.roll(lags, BLOCK - (1 << bit), 1)
                lags = jnp.where((row_id[:8] >> bit) & 1 == 1, moved, lags)
            s.lags[side, pl.ds(p, 1), :] = total_rows(lags)

    for k in range(HALVES):
        over_couples(k, correlate)

    def near(p, c):
        lags = [s.lags[side, pl.ds(p, 1), :] for side in range(2)]
        later = [jnp.where(row_lane < BLOCK - 1, pltpu.roll(line, BLOCK - 1, 1), 0.0) for line in lags]
        lags, later = (two(jnp.broadcast_to(beside(*lines), (8, 2 * BLOCK))) for lines in (lags, later))
        moment = product(lags, s.base[p])
        paired = dot(later[0], s.base_ramp[p]) + dot(later[1], s.base_ramp[p])
        for i, line in enumerate(split(moment[:1]) + split(paired[:1])):
            s.sums[i, pl.ds(p, 1), :] += line

    for k in range(HALVES):
        over_couples(k, near)
        for i in range(4):
            s.part[k, i * couples : (i + 1) * couples] = s.sums[i, k * couples : (k + 1) * couples]
    send(s.part.at[other], s.part_in, s.part_sem, partner)
    for m in range(count):
        result[m] = s.result[m].T
    sum_hop(3)

    def norm_backward(m):
        for k in range(HALVES):
            wait_for(s.d_out.at[k, m, pl.ds(0, members - 1)], s.d_sem.at[k, m, 1])
        inverse = s.inverse[m : m + 1]
        scaled = s.d_in[m].reshape(width, span)
        plain = jnp.zeros((1, span), F32)
        along = jnp.zeros((1, span), F32)
        for j in range(tiles):
            rows = slice(j * BLOCK, (j + 1) * BLOCK)
            piece = scaled[rows].astype(F32)
            plain += total_rows(piece)
            along += total_rows(piece * s.normed[m, rows])
        plain, along = (plain * (1.0 / width), along * (1.0 / width))
        for j in range(tiles):
            rows = slice(j * BLOCK, (j + 1) * BLOCK)
            piece = scaled[rows].astype(F32) - plain - s.normed[m, rows] * along
            piece = s.upstream[m, rows].astype(F32) + inverse * piece
            token_grad[m, :, rows] = piece.astype(BF16).T

    norm_backward(0)

    wait_for(s.part_in, s.part_sem.at[0])
    wait_for(s.part_in, s.part_sem.at[1])
    mine = s.part[half] + s.part_in[...]
    moment, paired = (
        tuple(mine[i * couples : (i + 1) * couples] for i in pick) for pick in ((0, 1), (2, 3))
    )
    parts_own, pull = jax.vjp(coefficient_parts, *raw_params(half))
    paired = times(paired, parts_own[2:])
    grads = pull((paired[0], -paired[1], moment[0], -moment[1]))

    def uncoupled(value):
        s.turn[pl.ds(0, couples, stride=2), :] = value
        s.turn[pl.ds(1, couples, stride=2), :] = pltpu.roll(value, states, 1)
        return s.turn[...]

    rate_grad[...] = uncoupled(grads[0])[:, :states]
    turn_grad[...] = uncoupled(grads[1])[:, :states]
    mix_low = own_lane < states
    mix_re = uncoupled(grads[3])
    mixing_grad[...] = jnp.where(mix_low, mix_re, pltpu.roll(uncoupled(grads[4]), states, 1))
    lines = [jnp.where(mix_low, uncoupled(grads[2]), 0.0)]
    lines += [mine[4 * couples + i * own : 4 * couples + (i + 1) * own] for i in range(3)]
    ones = jnp.ones((8, BLOCK), F32)
    for rows, out in zip(lines, (spacing_grad, gain_grad, bias_grad, skip_grad), strict=True):
        line = lax.dot_general(ones, rows, (TURNED, ((), ())), preferred_element_type=F32, precision=HIGH)
        out[...] = line[:1]

    for m in range(1, count):
        norm_backward(m)

    wait_for(many(s.note_in), s.note_sem.at[0])
    for m in range(count):
        wait_for(many(s.scale_in.at[m]), s.scale_sem.at[m, 0])
        for k in range(HALVES):
            wait_for(many(s.x_in.at[k, m]), s.x_sem.at[k, m, 0])
            wait_for(many(s.a_out.at[k, m]), s.a_sem.at[k, m, 0])
            wait_for(many(s.g_in.at[k, m]), s.g_sem.at[k, m, 0])
            wait_for(many(s.d_out.at[k, m]), s.d_sem.at[k, m, 0])
    for k in range(HALVES):
        rows = pl.ds(k * couples, couples)

        @pl.when(half == 0)
        def _():
            wait_for(s.carry_out.at[rows], s.carry_sem.at[k, 0])

        @pl.when(half == 1)
        def _():
            wait_for(s.back_out.at[rows], s.back_sem.at[k, 0])


class Scratch:
    def __init__(self, names, refs):
        for name, ref in zip(names, refs, strict=True):
            setattr(self, name, ref)


def scratch_of(size, states):
    groups, parts, own, width, span, count = size
    local, blocks, zs = (parts // HALVES, span // BLOCK, parts // 2)
    members, couples = (groups * local, own // 2)
    every = HALVES * couples
    rows = blocks * count * members
    bits = 7 + (blocks * local).bit_length()
    wide = 2 * width + BLOCK
    vmem, sems = (pltpu.VMEM, pltpu.SemaphoreType.DMA)
    by_holder = (HALVES, count, groups, local, own, span)
    by_owner = (HALVES, count, members, own, span)
    filed = (count, groups, HALVES, local, own, span)
    chunk_sems = sems((HALVES, count, 2))
    held = vmem((every, rows, 2 * BLOCK), F32)
    table, plain = (vmem((every, 2, 2 * BLOCK, 2 * BLOCK), BF16), vmem((every, 2 * BLOCK, 2 * BLOCK), BF16))
    carry = vmem((every, 2, count * groups, BLOCK), F32)
    part_rows = 4 * couples + 3 * own
    return {
        "tokens": vmem((count, width, span), BF16),
        "upstream": vmem((count, width, span), BF16),
        "result": vmem((count, width, span), BF16),
        "normed": vmem((count, width, span), F32),
        "inverse": vmem((count, span), F32),
        "valid": vmem((count, span), F32),
        "x_out": vmem(by_holder, I16), "x_in": vmem(by_owner, I16), "x_sem": chunk_sems,
        "a_out": vmem(by_owner, BF16), "a_in": vmem(filed, BF16), "a_sem": chunk_sems,
        "g_out": vmem(by_holder, I16), "g_in": vmem(by_owner, I16), "g_sem": chunk_sems,
        "d_out": vmem(by_owner, BF16), "d_in": vmem(filed, BF16), "d_sem": chunk_sems,
        "note_out": vmem((1, 1, BLOCK), F32), "note_in": vmem((members, 1, BLOCK), F32), "note_sem": sems((2,)),
        "scale_out": vmem((count, 1, BLOCK), F32), "scale_in": vmem((count, members, 1, BLOCK), F32),
        "scale_sem": sems((count, 2)),
        "scales": vmem((rows, 2 * BLOCK), F32),
        "params": vmem((HALVES, own, 3 * BLOCK), F32), "params_sem": sems((2,)),
        "weight_out": vmem((own, wide), BF16),
        "weight": vmem((groups, zs, 2, own, wide), BF16), "weight_sem": sems((3, 2)),
        "flat": vmem((width, 2 * width), BF16),
        "flipped": vmem((2 * width, width), BF16),
        "shift": vmem((2 * width, BLOCK), F32),
        "pre_grad": vmem((2 * width, span), BF16),
        "act_grad": vmem((width, span), F32),
        "total": vmem((groups, zs, 2, own, wide), F32),
        "sum_core": vmem((groups, zs, own, wide), F32),
        "sum_dp_out": vmem((groups, zs, own, wide), BF16),
        "sum_dp_in": vmem((groups, zs, own, wide), BF16),
        "sum_z_out": vmem((zs, own, wide), BF16),
        "sum_z_in": vmem((zs, own, wide), BF16),
        "sum_sem": sems((3, 2)),
        "turn": vmem((own, BLOCK), F32),
        "scalars": vmem((3, HALVES * own, BLOCK), F32),
        "power": vmem((bits, 2, every, BLOCK), F32),
        "lead": vmem((2, every, BLOCK), F32),
        "coeff": vmem((2, every, BLOCK), F32),
        "base": table, "down": table, "up": table, "back": table, "toeplitz": table,
        "base_ramp": plain, "down_ramp": plain,
        "stage_in": vmem((blocks, count, members * own, BLOCK), F32),
        "stage_out": vmem((blocks, count, members * own, BLOCK), F32),
        "mask": vmem((rows, 2 * BLOCK), F32),
        "own_normed": held, "drive": held, "entering": held, "slope": held, "inflow": held,
        "grad": held, "outflow": held, "leaving": held,
        "widen": vmem((every, 2, count * members, BLOCK), F32),
        "carry_out": carry, "carry_in": carry, "carry_sem": sems((HALVES, 2)),
        "back_out": carry, "back_in": carry, "back_sem": sems((HALVES, 2)),
        "sums": vmem((4, every, BLOCK), F32),
        "lags": vmem((2, every, BLOCK), F32),
        "part": vmem((HALVES, part_rows, BLOCK), F32), "part_in": vmem((part_rows, BLOCK), F32),
        "part_sem": sems((2,)),
    }


def handed_over(values):
    def kernel(*refs):
        for given, out in zip(refs[: len(values)], refs[len(values) :], strict=True):
            out[...] = given[...].reshape(out.shape)

    shapes = [(value.size,) if value.shape[0] == 1 else value.shape for value in values]
    return pl.pallas_call(
        kernel,
        out_shape=[jax.ShapeDtypeStruct(shape, value.dtype) for shape, value in zip(shapes, values, strict=True)],
        in_specs=[pl.BlockSpec(memory_space=pltpu.VMEM)] * len(values),
        out_specs=[pl.BlockSpec(memory_space=pltpu.VMEM)] * len(values),
    )(*values)


def in_one_kernel(groups, parts, *args):
    inputs, lengths, ln_gain, ln_bias, lam_log, lam_im, log_dt, mix_weight, skip, glu_weight, glu_bias, out_grad = args
    count, span, width = inputs.shape
    own = ln_gain.shape[0]
    size = (groups, parts, own, width, span, count)
    scratch = scratch_of(size, lam_log.shape[1])

    def kernel(*refs):
        arguments, results, kept = (refs[:12], refs[12:23], refs[23:])
        whole_kernel(size, *arguments, *results, Scratch(scratch, kept))

    vmem, smem = (pl.BlockSpec(memory_space=pltpu.VMEM), pl.BlockSpec(memory_space=pltpu.SMEM))
    line = jax.ShapeDtypeStruct((1, own), F32)
    outs = pl.pallas_call(
        kernel,
        out_shape=(
            jax.ShapeDtypeStruct(inputs.shape, BF16),
            jax.ShapeDtypeStruct(inputs.shape, BF16),
            line,
            line,
            jax.ShapeDtypeStruct(lam_log.shape, F32),
            jax.ShapeDtypeStruct(lam_im.shape, F32),
            line,
            jax.ShapeDtypeStruct(mix_weight.shape, F32),
            line,
            jax.ShapeDtypeStruct(glu_weight.shape, F32),
            jax.ShapeDtypeStruct((1, 2 * own), F32),
        ),
        in_specs=[vmem, smem, smem, smem, vmem, vmem, smem, vmem, smem, vmem, smem, vmem],
        out_specs=[vmem] * 11,
        scratch_shapes=list(scratch.values()),
        compiler_params=pltpu.CompilerParams(
            collective_id=0, has_side_effects=True, vmem_limit_bytes=62 * 1024 * 1024
        ),
    )(*args)
    return tuple(handed_over(outs))


def solution(mesh):
    tokens, vector, matrix = (P("dp", "seq", None), P(BOTH), P(BOTH, None))
    groups, parts = (mesh.shape["dp"], mesh.shape["seq"])

    def step(*args):
        own = args[2].shape[0]
        if own % 16 == 0 and parts % 4 == 0:
            return in_one_kernel(groups, parts, *args)
        return per_device(*args)

    return jax.shard_map(
        step,
        mesh=mesh,
        in_specs=(
            tokens, P("dp"), vector, vector, matrix, matrix, vector, matrix, vector, matrix, vector, tokens,
        ),
        out_specs=(
            tokens, tokens, vector, vector, matrix, matrix, vector, matrix, vector, matrix, vector,
        ),
        check_vma=False,
    )
```

```python
import math
from functools import partial

import jax
import jax.numpy as jnp
from jax import lax
from jax.experimental import pallas as pl
from jax.experimental.pallas import tpu as pltpu
from jax.sharding import PartitionSpec as P

BLOCK = 128
EPS = 1e-05
HIGH = lax.Precision.HIGHEST
BOTH = ("dp", "seq")


def halves(packed):
    count = packed.shape[-1] // 2
    return (packed[..., :count], packed[..., count:])


def cmul(first, second):
    first_re, first_im = halves(first)
    second_re, second_im = halves(second)
    return jnp.concatenate(
        [first_re * second_re - first_im * second_im, first_re * second_im + first_im * second_re],
        axis=-1,
    )


def conjugate(packed):
    real_half, imag_half = halves(packed)
    return jnp.concatenate([real_half, -imag_half], axis=-1)


def coefficients(lam_log, lam_im, log_dt, mix_weight):
    spacing = jnp.exp(log_dt)[:, None]
    rate = jnp.exp(lam_log)
    shrink = -rate * spacing
    angle = lam_im * spacing
    scale = jnp.exp(shrink)
    decay = jnp.concatenate([scale * jnp.cos(angle), scale * jnp.sin(angle)], axis=-1)
    less_re = jnp.expm1(shrink) * jnp.cos(angle) - 2.0 * jnp.sin(0.5 * angle) ** 2
    less_im = scale * jnp.sin(angle)
    modulus = rate * rate + lam_im * lam_im
    ratio = jnp.concatenate(
        [
            (lam_im * less_im - rate * less_re) / modulus,
            -(rate * less_im + lam_im * less_re) / modulus,
        ],
        axis=-1,
    )
    return (decay, cmul(mix_weight, ratio))


def powers(decay):
    real_half, imag_half = halves(decay)
    table = jnp.concatenate([jnp.ones_like(real_half), jnp.zeros_like(imag_half)], axis=-1)[:, None]
    step = decay[:, None]
    while table.shape[1] < BLOCK:
        table = jnp.concatenate([table, cmul(step, table)], axis=1)
        step = cmul(step, step)
    return (table, step[:, 0])


def link(earlier, later):
    return (cmul(earlier[0], later[0]), cmul(later[0], earlier[1]) + later[1])


def shifted(pieces, step, back):
    leads = jnp.broadcast_to(step[:, None, None], pieces.shape)
    _, reach = lax.associative_scan(link, (leads, pieces), axis=2, reverse=back)
    none = jnp.zeros_like(reach[:, :, :1])
    if back:
        return jnp.concatenate([reach[:, :, 1:], none], axis=2)
    return jnp.concatenate([none, reach[:, :, :-1]], axis=2)


def to_owner(rows):
    count, span, width = rows.shape
    groups, parts = (lax.axis_size("dp"), lax.axis_size("seq"))
    own = width // (groups * parts)
    sent = rows.reshape(count * span, width).T.reshape(-1, own, count, span)
    held = lax.all_to_all(sent, BOTH, 0, 0, tiled=True).reshape(groups, parts, own, count, span)
    held = held.transpose(2, 0, 3, 1, 4).reshape(own, groups * count, -1, BLOCK)
    return held


def to_holder(held, count, span):
    groups, parts = (lax.axis_size("dp"), lax.axis_size("seq"))
    own = held.shape[0]
    sent = held.astype(jnp.bfloat16).reshape(own, groups, count, parts, span).transpose(1, 3, 0, 2, 4)
    sent = sent.reshape(groups * parts, own, count, span)
    rows = lax.all_to_all(sent, BOTH, 0, 0, tiled=True)
    return rows.reshape(-1, count * span).T.reshape(count, span, -1).astype(jnp.float32)


def per_device(
    inputs,
    lengths,
    ln_gain,
    ln_bias,
    lam_log,
    lam_im,
    log_dt,
    mix_weight,
    skip,
    glu_weight,
    glu_bias,
    out_grad,
):
    count, span, width = inputs.shape
    offset = lax.axis_index("seq") * span
    positions = offset + jnp.arange(span, dtype=jnp.int32)
    valid = (positions[None, :] < lengths[:, None]).astype(jnp.float32)[..., None]
    rows = lax.all_gather(glu_weight, BOTH, axis=0, tiled=True)
    shift = lax.all_gather(glu_bias, BOTH, axis=0, tiled=True)
    spans = lax.all_gather(lengths, "dp", axis=0, tiled=True)
    whole_span = span * lax.axis_size("seq")
    mask = (jnp.arange(whole_span, dtype=jnp.int32)[None] < spans[:, None]).astype(jnp.float32)
    mask = mask.reshape(1, -1, whole_span // BLOCK, BLOCK)

    tokens = inputs.astype(jnp.float32)
    mean = jnp.mean(tokens, axis=-1, keepdims=True)
    centered = tokens - mean
    inverse = lax.rsqrt(jnp.mean(centered * centered, axis=-1, keepdims=True) + EPS)
    normed = centered * inverse

    (decay, coeff), coeff_pull = jax.vjp(coefficients, lam_log, lam_im, log_dt, mix_weight)
    base, whole = powers(decay)
    down = base[:, ::-1]
    real_half, imag_half = halves(coeff)
    kernel = jnp.einsum("cz,ckz->ck", conjugate(coeff), base, precision=HIGH)
    lead = cmul(coeff, decay)[:, None]
    up = conjugate(cmul(lead, base))
    back = conjugate(cmul(lead, down))
    steps = jnp.arange(BLOCK)
    lag = steps[:, None] - steps[None, :]
    toeplitz = jnp.where(lag >= 0, kernel[:, jnp.maximum(lag, 0)], 0.0)
    ramp = steps.astype(jnp.float32)[:, None]

    gain, bias, skipping = (p[:, None, None, None] for p in (ln_gain, ln_bias, skip))
    own_normed = to_owner(normed)
    drive = (own_normed * gain + bias) * mask
    entering = shifted(jnp.einsum("cbqj,cjz->cbqz", drive, down, precision=HIGH), whole, False)
    response = jnp.einsum("cij,cbqj->cbqi", toeplitz, drive, precision=HIGH)
    response += jnp.einsum("ciz,cbqz->cbqi", up, entering, precision=HIGH) + skipping * drive
    activated, gelu_pull = jax.vjp(partial(jax.nn.gelu, approximate=False), response)
    activated = to_holder(activated, count, span).astype(jnp.bfloat16).reshape(-1, width)
    pre = jnp.dot(activated, rows, preferred_element_type=jnp.float32) + shift
    gate = jax.nn.sigmoid(pre[:, width:])
    flat_valid = valid.reshape(-1, 1)
    result = (tokens + (pre[:, :width] * gate * flat_valid).reshape(tokens.shape)).astype(jnp.bfloat16)
    upstream = out_grad.astype(jnp.float32)
    gated = upstream.reshape(-1, width) * flat_valid
    pre_grad = jnp.concatenate(
        [gated * gate, gated * pre[:, :width] * gate * (1.0 - gate)], axis=-1
    ).astype(jnp.bfloat16)
    rows_grad = lax.dot_general(
        activated, pre_grad, (((0,), (0,)), ((), ())), preferred_element_type=jnp.float32
    )
    shift_grad = jnp.sum(pre_grad.astype(jnp.float32), axis=0)
    act_grad = lax.dot_general(
        pre_grad, rows, (((1,), (1,)), ((), ())), preferred_element_type=jnp.float32
    )
    response_grad = gelu_pull(to_owner(act_grad.reshape(tokens.shape)))[0]

    skip_grad = jnp.sum(response_grad * drive, axis=(1, 2, 3))
    outflow = jnp.einsum("cbqt,ctz->cbqz", response_grad, base, precision=HIGH)
    leaving = shifted(outflow, whole, True)
    drive_grad = jnp.einsum("cij,cbqi->cbqj", toeplitz, response_grad, precision=HIGH)
    drive_grad += jnp.einsum("cjz,cbqz->cbqj", back, leaving, precision=HIGH) + skipping * response_grad
    norm_grad = drive_grad * mask
    gain_grad = jnp.sum(norm_grad * own_normed, axis=(1, 2, 3))
    bias_grad = jnp.sum(norm_grad, axis=(1, 2, 3))
    scaled = to_holder(norm_grad * gain, count, span)
    token_grad = upstream + inverse * (
        scaled
        - jnp.mean(scaled, axis=-1, keepdims=True)
        - normed * jnp.mean(scaled * normed, axis=-1, keepdims=True)
    )

    cross = jnp.einsum("cbqj,cbqi->cij", drive, response_grad, precision=HIGH)
    lags = jnp.stack([jnp.trace(cross, offset=-k, axis1=1, axis2=2) for k in range(BLOCK)], axis=-1)
    second = jnp.einsum("cbqj,cjz->cbqz", drive, down * ramp[::-1], precision=HIGH)
    third = jnp.einsum("cbqt,ctz->cbqz", response_grad, base * (ramp + 1.0), precision=HIGH)
    total = partial(jnp.sum, axis=(1, 2))
    moment = cmul(decay, total(cmul(entering, outflow))) + jnp.einsum("ck,ckz->cz", lags, base, precision=HIGH)
    before = jnp.concatenate([jnp.zeros_like(base[:, :1]), base[:, :-1]], axis=1) * ramp
    paired = BLOCK * cmul(whole, total(cmul(leaving, entering)))
    paired += total(cmul(leaving, second) + cmul(entering, third))
    paired = cmul(coeff, paired + jnp.einsum("ck,ckz->cz", lags, before, precision=HIGH))
    rate_grad, turn_grad, spacing_grad, mixing_grad = coeff_pull((conjugate(paired), conjugate(moment)))

    scatter = partial(lax.psum_scatter, axis_name=BOTH, scatter_dimension=0, tiled=True)
    return (
        result,
        token_grad.astype(jnp.bfloat16),
        gain_grad,
        bias_grad,
        rate_grad,
        turn_grad,
        spacing_grad,
        mixing_grad,
        skip_grad,
        scatter(rows_grad),
        scatter(shift_grad),
    )


MESH = pl.DeviceIdType.MESH
F32, BF16, I16 = (jnp.float32, jnp.bfloat16, jnp.int16)
STEPS = 32700.0
GROUP = 4
HALVES = 2


def two(value):
    high = value.astype(BF16)
    return (high, (value - high.astype(F32)).astype(BF16))


def dot(left, right, dims=((1,), (0,))):
    return lax.dot_general(left, right, (dims, ((), ())), preferred_element_type=F32)


TURNED = ((1,), (1,))
SIDEWAYS = ((0,), (0,))


def product(left, table, dims=((1,), (0,))):
    return folded(over(*left), table[0], dims) + dot(left[0], table[1], dims)


def folded(rows, table, dims=((1,), (0,))):
    value = dot(rows, table, dims)
    half = value.shape[0] // 2
    return value[:half] + value[half:]


def times(value, factor):
    return (value[0] * factor[0] - value[1] * factor[1], value[0] * factor[1] + value[1] * factor[0])


def plus(first, second):
    return (first[0] + second[0], first[1] + second[1])


def choose(condition, first, second):
    return (jnp.where(condition, first[0], second[0]), jnp.where(condition, first[1], second[1]))


def split(value):
    return (value[:, :BLOCK], value[:, BLOCK:])


def beside(*parts):
    return jnp.concatenate(parts, axis=1)


def over(*parts):
    return jnp.concatenate(parts, axis=0)


def total_rows(value):
    return jnp.sum(value, axis=0, keepdims=True)


def small_expm1(value):
    near = jnp.abs(value) < 0.5
    small = jnp.where(near, value, 0.0)
    series = jnp.ones_like(small)
    for order in range(10, 1, -1):
        series = 1.0 + small * (1.0 / order) * series
    return jnp.where(near, small * series, jnp.exp(value) - 1.0)


def coefficient_parts(lam_log, lam_im, log_dt, mix_re, mix_im):
    spacing, rate = (jnp.exp(log_dt), jnp.exp(lam_log))
    shrink, angle = (-rate * spacing, lam_im * spacing)
    scale = jnp.exp(shrink)
    cosine, sine, half = (jnp.cos(angle), jnp.sin(angle), jnp.sin(0.5 * angle))
    less_re = small_expm1(shrink) * cosine - 2.0 * half * half
    less_im = scale * sine
    modulus = rate * rate + lam_im * lam_im
    ratio = (
        (lam_im * less_im - rate * less_re) / modulus,
        -(rate * less_im + lam_im * less_re) / modulus,
    )
    return (scale * cosine, less_im) + times((mix_re, mix_im), ratio)


def whole_kernel(
    size,
    inputs, lengths, ln_gain, ln_bias, lam_log, lam_im, log_dt, mix_weight, skip, glu_weight, glu_bias, out_grad,
    result, token_grad, gain_grad, bias_grad, rate_grad, turn_grad, spacing_grad, mixing_grad, skip_grad,
    rows_grad, shift_grad,
    s,
):
    groups, parts, own, width, span, count = size
    local, blocks, zs = (parts // HALVES, span // BLOCK, parts // 2)
    members = groups * local
    tiles, couples, states = (width // BLOCK, own // 2, lam_log.shape[1])
    wide = 2 * width
    dp, seq = (lax.axis_index("dp"), lax.axis_index("seq"))
    core, z = (lax.rem(seq, 2), seq // 2)
    half, here = (seq // local, lax.rem(seq, local))
    other = 1 - half
    me = dp * local + here
    partner = (dp, other * local + here)

    def place(member):
        return (member // local, half * local + lax.rem(member, local))

    def send(source, target, sems, device):
        pltpu.make_async_remote_copy(
            src_ref=source, dst_ref=target, send_sem=sems.at[0], recv_sem=sems.at[1],
            device_id=device, device_id_type=MESH,
        ).start()

    def wait_for(ref, sem):
        pltpu.make_async_copy(ref, ref, sem).wait()

    def to_owners(out, into, sems):
        for k in range(1, members):
            member = lax.rem(me + k, members)
            send(out.at[member // local, lax.rem(member, local)], into.at[me], sems, place(member))

    def to_holders(out, into, sems):
        for k in range(1, members):
            member = lax.rem(me + k, members)
            send(out.at[member], into.at[dp, here], sems, place(member))

    def to_all(out, into, sems):
        for k in range(1, members):
            send(out, into.at[me], sems, place(lax.rem(me + k, members)))

    def many(ref):
        return ref.at[pl.ds(0, members - 1)]

    barrier = pltpu.get_barrier_semaphore()

    def greet(k, carry):
        member = place(lax.rem(me + k, members))
        pl.semaphore_signal(barrier, inc=1, device_id=member, device_id_type=MESH)
        return carry

    lax.fori_loop(1, members, greet, 0)
    for k in range(zs // HALVES):
        there = other * local + 2 * k + core
        pl.semaphore_signal(barrier, inc=1, device_id=(dp, there), device_id_type=MESH)

    lane = lax.broadcasted_iota(jnp.int32, (1, span), 1) + seq * span
    quantum = math.sqrt(width) / STEPS

    def chunk_rows(j):
        per = BLOCK // own
        for i in range(per):
            shard = j * per + i
            yield slice(i * own, (i + 1) * own), shard // parts, shard % parts // local, shard % local

    def norm(m):
        tokens = inputs[m].T
        s.tokens[m] = tokens
        total = jnp.zeros((1, span), F32)
        for j in range(tiles):
            total += total_rows(tokens[j * BLOCK : (j + 1) * BLOCK].astype(F32))
        mean = total * (1.0 / width)
        total = jnp.zeros((1, span), F32)
        for j in range(tiles):
            off = tokens[j * BLOCK : (j + 1) * BLOCK].astype(F32) - mean
            total += total_rows(off * off)
        inverse = lax.rsqrt(total * (1.0 / width) + EPS)
        valid = (lane < lengths[m]).astype(F32)
        s.inverse[m : m + 1] = inverse
        s.valid[m : m + 1] = valid
        for j in range(tiles):
            normed = (tokens[j * BLOCK : (j + 1) * BLOCK].astype(F32) - mean) * inverse
            s.normed[m, j * BLOCK : (j + 1) * BLOCK] = normed
            coded = jnp.round(normed * valid * (1.0 / quantum)).astype(I16)
            for rows, a, k, p in chunk_rows(j):
                s.x_out[k, m, a, p] = coded[rows]
        for k in range(HALVES):
            s.x_in[k, m, pl.ds(me, 1)] = s.x_out[k, m, dp, pl.ds(here, 1)]

    row_lane = lax.broadcasted_iota(jnp.int32, (1, BLOCK), 1)
    row = jnp.zeros((1, BLOCK), F32)
    for m in range(count):
        row = jnp.where(row_lane == m, lengths[m].astype(F32), row)
    s.note_out[0] = row
    s.note_in[pl.ds(me, 1)] = row[None]

    own_row = lax.broadcasted_iota(jnp.int32, (own, BLOCK), 0)
    own_lane = lax.broadcasted_iota(jnp.int32, (own, BLOCK), 1)
    scalars = jnp.zeros((own, BLOCK), F32)
    shifts = jnp.zeros((own, BLOCK), F32)
    for c in range(own):
        for i, ref in enumerate((log_dt, ln_gain, ln_bias, skip)):
            scalars = jnp.where((own_row == c) & (own_lane == i), ref[c], scalars)
        for i in range(2):
            shifts = jnp.where((own_row == c) & (own_lane % 2 == i), glu_bias[i * own + c], shifts)
    s.params[pl.ds(half, 1), :, :states] = lam_log[...][None]
    s.params[pl.ds(half, 1), :, states : 2 * states] = lam_im[...][None]
    s.params[pl.ds(half, 1), :, BLOCK : 2 * BLOCK] = mix_weight[...][None]
    s.params[pl.ds(half, 1), :, 2 * BLOCK :] = scalars[None]
    high = shifts.astype(BF16)
    rest = shifts - high.astype(F32)
    middle = rest.astype(BF16)
    lowest = (rest - middle.astype(F32)).astype(BF16)
    thirds = jnp.where(own_lane < 2, high, jnp.where(own_lane < 4, middle, lowest))
    s.weight_out[:, :wide] = glu_weight[...]
    s.weight_out[:, wide:] = thirds
    s.weight[pl.ds(dp, 1), pl.ds(z, 1), pl.ds(core, 1)] = s.weight_out[...][None, None, None]

    def weight_hop(hop):
        sems = s.weight_sem.at[hop]
        if hop == 0:
            for k in range(1, zs):
                there = lax.rem(z + k, zs)
                send(s.weight_out, s.weight.at[dp, z, core], sems, (dp, there * 2 + core))
        elif hop == 1:
            for k in range(1, groups):
                mine = s.weight.at[dp, :, core]
                send(mine, mine, sems, (lax.rem(dp + k, groups), seq))
        else:
            mine = s.weight.at[:, :, core]
            send(mine, mine, sems, (dp, z * 2 + 1 - core))

    def weight_wait(hop):
        if hop == 0:
            ref = s.weight.at[0, pl.ds(0, zs - 1), 0]
        elif hop == 1:
            ref = s.weight.at[pl.ds(0, groups - 1), :, 0]
        else:
            ref = s.weight.at[:, :, 0]
        wait_for(ref, s.weight_sem.at[hop, 0])
        wait_for(ref, s.weight_sem.at[hop, 1])

    pl.semaphore_wait(barrier, members - 1 + zs // HALVES)
    send(s.params.at[half], s.params.at[half], s.params_sem, partner)
    to_all(s.note_out.at[0], s.note_in, s.note_sem)
    weight_hop(0)
    for m in range(count):
        norm(m)
        for k in range(HALVES):
            to_owners(s.x_out.at[k, m], s.x_in.at[k, m], s.x_sem.at[k, m])

    wait_for(s.params.at[0], s.params_sem.at[0])
    wait_for(s.params.at[0], s.params_sem.at[1])
    pair_low = lax.broadcasted_iota(jnp.int32, (couples, BLOCK), 1) < states

    def coupled(value):
        s.turn[...] = value
        even = s.turn[pl.ds(0, couples, stride=2), :]
        odd = s.turn[pl.ds(1, couples, stride=2), :]
        return jnp.where(pair_low, even, pltpu.roll(odd, states, 1))

    def raw_params(k):
        packed = [s.params[k, :, i * BLOCK : (i + 1) * BLOCK] for i in range(3)]
        lam, mix, rest = packed
        log_step = jnp.broadcast_to(rest[:, :1], (own, BLOCK))
        return tuple(
            coupled(value)
            for value in (lam, pltpu.roll(lam, states, 1), log_step, mix, pltpu.roll(mix, states, 1))
        )

    for k in range(HALVES):
        rest = s.params[k, :, 2 * BLOCK :]
        for i in range(1, 4):
            s.scalars[i - 1, k * own : (k + 1) * own] = jnp.broadcast_to(rest[:, i : i + 1], (own, BLOCK))
        rows = slice(k * couples, (k + 1) * couples)
        for i, value in enumerate(raw_params(k)):
            s.raw[i, rows] = value
        parts_k = coefficient_parts(*(s.raw[i, rows] for i in range(5)))
        decay, coeff = (parts_k[:2], parts_k[2:])
        s.coeff[0, rows], s.coeff[1, rows] = coeff
        s.lead[0, rows], s.lead[1, rows] = times(coeff, decay)
        power = decay
        for bit in range(s.power.shape[0]):
            s.power[bit, 0, rows], s.power[bit, 1, rows] = power
            power = times(power, power)

    def power_of(bit, p):
        return (s.power[bit, 0, pl.ds(p, 1), :], s.power[bit, 1, pl.ds(p, 1), :])

    square = (BLOCK, BLOCK)
    row_id = lax.broadcasted_iota(jnp.int32, square, 0)
    lane_id = lax.broadcasted_iota(jnp.int32, square, 1)
    ramp = row_id.astype(F32)
    first_states = lax.rem(lax.broadcasted_iota(jnp.int32, (BLOCK, 2 * BLOCK), 1), BLOCK) < states

    def stacked(value):
        none = jnp.zeros_like(value)
        return over(jnp.where(first_states, value, none), jnp.where(first_states, none, value))

    def put_table(ref, p, value):
        for i, part in enumerate(two(beside(*value))):
            ref[p, i] = stacked(part)

    def tables_first(p):
        eight = row_id[:8]
        unit = (jnp.ones((8, BLOCK), F32), jnp.zeros((8, BLOCK), F32))
        base, down = (unit, unit)
        for bit in range(3):
            step = power_of(bit, p)
            base = choose((eight >> bit) & 1 == 1, times(base, step), base)
            down = choose(((7 - eight) >> bit) & 1 == 1, times(down, step), down)
        for bit in range(3, 7):
            step = power_of(bit, p)
            more, most = (times(base, step), times(down, step))
            base = (over(base[0], more[0]), over(base[1], more[1]))
            down = (over(most[0], down[0]), over(most[1], down[1]))
        s.base_kept[p] = beside(*base)
        s.down_kept[p] = beside(*down)
        put_table(s.down, p, down)

    def tables_middle(p):
        base = split(s.base_kept[p])
        up = times(base, (s.lead[0, pl.ds(p, 1), :], s.lead[1, pl.ds(p, 1), :]))
        put_table(s.up, p, (up[0], -up[1]))
        weights = beside(s.coeff[0, pl.ds(p, 1), :], -s.coeff[1, pl.ds(p, 1), :])
        weights = jnp.broadcast_to(weights, (8, 2 * BLOCK))
        pick = lax.rem(lax.broadcasted_iota(jnp.int32, (8, 2 * BLOCK), 1), BLOCK) < states
        pick = pick == (lax.broadcasted_iota(jnp.int32, (8, 2 * BLOCK), 0) == 0)
        kernel = lax.dot_general(
            jnp.where(pick, weights, 0.0), beside(*base), (TURNED, ((), ())),
            preferred_element_type=F32, precision=HIGH,
        )
        for i in range(2):
            slanted = jnp.broadcast_to(kernel[i : i + 1], square)
            slanted = pltpu.roll(slanted, 0, 1, stride=1, stride_axis=0)
            side = slice(i * BLOCK, (i + 1) * BLOCK)
            off = slice((1 - i) * BLOCK, (2 - i) * BLOCK)
            for part, value in enumerate(two(jnp.where(lane_id >= row_id, slanted, 0.0))):
                s.toeplitz[p, part, side, side] = value
                s.toeplitz[p, part, side, off] = jnp.zeros(square, BF16)

    def tables_second(p):
        base, down = (split(s.base_kept[p]), split(s.down_kept[p]))
        back = times(down, (s.lead[0, pl.ds(p, 1), :], s.lead[1, pl.ds(p, 1), :]))
        put_table(s.base, p, base)
        put_table(s.back, p, (back[0], -back[1]))
        for ref, value, slope in (
            (s.base_ramp, base, ramp + 1.0),
            (s.down_ramp, down, BLOCK - 1.0 - ramp),
        ):
            ref[p] = stacked(beside(value[0] * slope, value[1] * slope).astype(BF16))

    def over_couples(k, body, group=GROUP):
        def some(g, carry):
            for u in range(group):
                body(k * couples + g * group + u, g * group + u)
            return carry

        lax.fori_loop(0, couples // group, some, 0)

    for k in range(HALVES):
        over_couples(k, lambda p, c: tables_first(p))

    half_rows = count * members
    full_rows = blocks * half_rows
    place_of = lax.rem(lax.broadcasted_iota(jnp.int32, (half_rows, BLOCK), 0), local)
    place_lane = lax.broadcasted_iota(jnp.int32, (half_rows, BLOCK), 1)
    step_bit = 7 + blocks.bit_length() - 1

    def rows_in(ref, k):
        for m in range(count):
            for q in range(blocks):
                piece = ref[k, m, :, :, q * BLOCK : (q + 1) * BLOCK]
                s.stage_in[q, m] = piece.astype(F32).reshape(members * own, BLOCK)

    def rows_out(ref, k):
        for m in range(count):
            for q in range(blocks):
                ref[k, m, :, :, q * BLOCK : (q + 1) * BLOCK] = (
                    s.stage_out[q, m].astype(BF16).reshape(members, own, BLOCK)
                )

    def gather_couple(c):
        sides = []
        for i in range(2):
            sides.append(
                over(
                    *(
                        s.stage_in[q, m, pl.ds(2 * c + i, members, stride=own), :]
                        for q in range(blocks)
                        for m in range(count)
                    )
                )
            )
        return beside(*sides)

    def put_couple(c, value):
        for i, side in enumerate(split(value)):
            for q in range(blocks):
                for m in range(count):
                    first = (q * count + m) * members
                    s.stage_out[q, m, pl.ds(2 * c + i, members, stride=own), :] = side[first : first + members]

    def scalar_rows(i, p):
        return beside(s.scalars[i, pl.ds(2 * p, 1), :], s.scalars[i, pl.ds(2 * p + 1, 1), :])

    def by_block(value):
        return [split(value[q * half_rows : (q + 1) * half_rows]) for q in range(blocks)]

    def scan(flows, p, upward):
        block_step = power_of(7, p)
        flows = flows if upward else flows[::-1]
        total = flows[0]
        for flow in flows[1:]:
            total = plus(times(total, block_step), flow)

        def moved(value, reach):
            shift = reach if upward else half_rows - reach
            inside = place_of >= reach if upward else place_of < local - reach
            return tuple(jnp.where(inside, pltpu.roll(part, shift, 0), 0.0) for part in value)

        reach = 1
        while reach < local:
            total = plus(total, times(moved(total, reach), power_of(step_bit + reach.bit_length() - 1, p)))
            reach *= 2
        return moved(total, 1), total

    def carried(state, ref, scales, p, c, k, upward):
        scale = jnp.sum(jnp.where(carry_lane == c, scales[k], 0.0), axis=1, keepdims=True)
        lines = ref[p].astype(F32)
        lines = (lines[: count * groups] * scale, lines[count * groups :] * scale)
        for j in range(local):
            for i in range(2):
                s.widen[p, i, pl.ds(j, count * groups, stride=local), :] = lines[i]
        carry = (s.widen[p, 0], s.widen[p, 1])
        distance = place_of if upward else local - 1 - place_of
        for bit in range(local.bit_length() - 1):
            further = times(carry, power_of(step_bit + bit, p))
            carry = choose((distance >> bit) & 1 == 1, further, carry)
        return plus(state, carry)

    def through(state, flows, p, upward):
        block_step = power_of(7, p)
        listing = [state]
        flows = flows if upward else flows[::-1]
        for flow in flows[:-1]:
            state = plus(times(state, block_step), flow)
            listing.append(state)
        listing = listing if upward else listing[::-1]
        return over(*(beside(*state) for state in listing))

    def read_notes():
        wait_for(many(s.note_in), s.note_sem.at[1])
        notes = s.note_in[...].reshape(members, BLOCK)
        member_lane = lax.broadcasted_iota(jnp.int32, (members, BLOCK), 1)
        member_place = lax.rem(lax.broadcasted_iota(jnp.int32, (members, BLOCK), 0), local)
        start = (half * local + member_place) * span + member_lane
        for m in range(count):
            length = jnp.sum(jnp.where(member_lane == m, notes, 0.0), axis=1, keepdims=True)
            for q in range(blocks):
                first = (q * count + m) * members
                within = ((start + q * BLOCK).astype(F32) < length).astype(F32)
                s.mask[first : first + members] = beside(within, within)

    carry_lane = lax.broadcasted_iota(jnp.int32, (count * groups, BLOCK), 1)

    def pick_last(p, c, k, total, out, scales, first):
        lines = []
        for i in range(2):
            s.widen[p, i] = total[i]
            lines.append(s.widen[p, i, pl.ds(first, count * groups, stride=local), :])
        top = jnp.max(jnp.maximum(jnp.abs(lines[0]), jnp.abs(lines[1])), axis=1, keepdims=True)
        top = jnp.maximum(top, 1e-30)
        factor = STEPS / top
        out[p] = jnp.round(over(lines[0] * factor, lines[1] * factor)).astype(I16)
        scales[k] = jnp.where(carry_lane == c, top * (1.0 / STEPS), scales[k])

    def forward_first(k):
        for m in range(count):
            wait_for(many(s.x_in.at[k, m]), s.x_sem.at[k, m, 1])
        rows_in(s.x_in, k)

        def inflow(p, c):
            own_normed = gather_couple(c) * quantum
            drive = (own_normed * scalar_rows(0, p) + scalar_rows(1, p)) * s.mask[...]
            s.own_normed[p] = own_normed
            s.drive[p] = drive
            s.inflow[p] = product(two(drive), s.down[p])

        over_couples(k, inflow)

        s.carry_scale_out[k] = jnp.zeros((count * groups, BLOCK), F32)

        def scanned(p, c):
            state, total = scan(by_block(s.inflow[p]), p, True)
            s.entering[p, :half_rows] = beside(*state)
            pick_last(p, c, k, total, s.carry_out, s.carry_scale_out, local - 1)

        over_couples(k, scanned)
        rows = pl.ds(k * couples, couples)

        @pl.when(half == 0)
        def _():
            send(s.carry_out.at[rows], s.carry_in.at[rows], s.carry_sem.at[k, 0], partner)
            send(s.carry_scale_out.at[k], s.carry_scale_in.at[k], s.carry_sem.at[k, 1], partner)

    def forward_local(k):
        def nearby(p, c):
            drive = s.drive[p]
            s.response[p] = product(two(drive), s.toeplitz[p]) + scalar_rows(2, p) * drive

        over_couples(k, nearby)

    def share_below(response):
        return 0.5 * (1.0 + lax.erf(response * math.sqrt(0.5)))

    def slopes(p, c):
        response = s.response[p]
        density = jnp.exp(-0.5 * response * response) * (1.0 / math.sqrt(2.0 * math.pi))
        s.slope[p] = share_below(response) + response * density

    def forward_second(k):
        rows = pl.ds(k * couples, couples)

        @pl.when(half == 0)
        def _():
            s.carry_in[rows] = jnp.zeros((couples, 2 * count * groups, BLOCK), I16)
            s.carry_scale_in[k] = jnp.zeros((count * groups, BLOCK), F32)

        @pl.when(half == 1)
        def _():
            wait_for(s.carry_in.at[rows], s.carry_sem.at[k, 0, 1])
            wait_for(s.carry_scale_in.at[k], s.carry_sem.at[k, 1, 1])

        def complete(p, c):
            state = carried(
                split(s.entering[p, :half_rows]), s.carry_in, s.carry_scale_in, p, c, k, True
            )
            s.entering[p] = through(state, by_block(s.inflow[p]), p, True)

        over_couples(k, complete)

        def respond(p, c):
            response = s.response[p] + product(two(s.entering[p]), s.up[p], TURNED)
            s.response[p] = response
            put_couple(c, response * share_below(response))

        over_couples(k, respond)
        rows_out(s.a_out, k)
        for m in range(count):
            s.a_in[m, dp, k, pl.ds(here, 1)] = s.a_out[k, m, pl.ds(me, 1)]
            to_holders(s.a_out.at[k, m], s.a_in.at[m, :, k], s.a_sem.at[k, m])

    read_notes()
    over_couples(0, lambda p, c: tables_middle(p))
    weight_wait(0)
    weight_hop(1)
    over_couples(1, lambda p, c: tables_middle(p))
    for k in range(HALVES):
        forward_first(k)
    for k in range(HALVES):
        forward_local(k)
    for k in range(HALVES):
        forward_second(k)
        if k == 0:
            weight_wait(1)
            weight_hop(2)
    for k in range(HALVES):
        over_couples(k, lambda p, c: tables_second(p))

    for m in range(count):
        s.upstream[m] = out_grad[m].T
    weight_wait(2)
    for j in range(tiles):
        rows = slice(j * BLOCK, (j + 1) * BLOCK)
        per = BLOCK // own
        flat = s.weight[...].reshape(-1, own, wide + BLOCK)[j * per : (j + 1) * per].reshape(BLOCK, -1)
        s.flat[rows] = flat[:, :wide]
        s.flipped[:, rows] = flat[:, :wide].T
        shifts = flat[:, wide:].astype(F32)
        shifts = shifts + pltpu.roll(shifts, BLOCK - 2, 1) + pltpu.roll(shifts, BLOCK - 4, 1)
        for i in range(2):
            column = jnp.broadcast_to(shifts[:, i : i + 1], (BLOCK, BLOCK)).reshape(per, own, BLOCK)
            for n in range(per):
                first = ((j * per + n) * 2 + i) * own
                s.shift[first : first + own] = column[n]

    def project(m):
        for k in range(HALVES):
            ref = s.a_out.at[k, m, pl.ds(0, members - 1)]
            wait_for(ref, s.a_sem.at[k, m, 1])
        activated = s.a_in[m].reshape(width, span)
        valid = s.valid[m : m + 1]
        lanes = slice(m * span, (m + 1) * span)
        s.pre[...] = dot(s.flipped[...], activated)
        for j in range(tiles):
            rows = slice(j * BLOCK, (j + 1) * BLOCK)
            gates = slice(width + j * BLOCK, width + (j + 1) * BLOCK)
            value = s.pre[rows] + beside(*[s.shift[rows]] * blocks)
            gate = jax.nn.sigmoid(s.pre[gates] + beside(*[s.shift[gates]] * blocks))
            gated = s.upstream[m, rows].astype(F32) * valid
            s.pre_grad[rows, lanes] = (gated * gate).astype(BF16)
            s.pre_grad[gates, lanes] = (gated * value * gate * (1.0 - gate)).astype(BF16)
            s.result[m, rows] = (s.tokens[m, rows].astype(F32) + value * gate * valid).astype(BF16)
        s.act_grad[...] = dot(s.flat[...], s.pre_grad[:, lanes])
        largest = jnp.zeros((1, 1), F32)
        for j in range(tiles):
            piece = s.act_grad[j * BLOCK : (j + 1) * BLOCK]
            largest = jnp.maximum(largest, jnp.max(jnp.abs(piece), axis=(0, 1), keepdims=True))
        largest = jnp.maximum(largest, 1e-30)
        s.scale_out[m] = jnp.broadcast_to(largest * (1.0 / STEPS), (1, BLOCK))
        s.scale_in[m, pl.ds(me, 1)] = s.scale_out[m][None]
        to_all(s.scale_out.at[m], s.scale_in.at[m], s.scale_sem.at[m])
        factor = STEPS / largest
        for j in range(tiles):
            coded = jnp.round(s.act_grad[j * BLOCK : (j + 1) * BLOCK] * factor).astype(I16)
            for rows, a, k, p in chunk_rows(j):
                s.g_out[k, m, a, p] = coded[rows]
        for k in range(HALVES):
            s.g_in[k, m, pl.ds(me, 1)] = s.g_out[k, m, dp, pl.ds(here, 1)]
            to_owners(s.g_out.at[k, m], s.g_in.at[k, m], s.g_sem.at[k, m])
    def weight_gradient():
        ones = jnp.ones((count * span, BLOCK), BF16)
        per = width // groups
        lane4 = lax.broadcasted_iota(jnp.int32, (zs, 2, own, BLOCK), 3)
        for j in range(groups):
            activated = beside(*(s.a_in[m, j].reshape(per, span) for m in range(count)))
            piece = dot(activated, s.pre_grad[...], TURNED).reshape(zs, 2, own, wide)
            sums = dot(s.pre_grad[2 * j * per : 2 * (j + 1) * per], ones).reshape(zs, 2, 2, own, BLOCK)
            sums = jnp.where(lane4 == 0, sums[:, :, 0], jnp.where(lane4 == 1, sums[:, :, 1], 0.0))
            s.total[j, :, :, :, :wide] = piece
            s.total[j, :, :, :, wide:] = sums

    for m in range(count):
        project(m)
    weight_gradient()

    def sum_hop(hop):
        sems = s.sum_sem
        if hop == 0:
            send(s.total.at[:, :, 1 - core], s.sum_core, sems.at[0], (dp, z * 2 + 1 - core))
        elif hop == "ready":
            wait_for(s.sum_core, sems.at[0, 0])
            wait_for(s.sum_core, sems.at[0, 1])
            for j in range(groups):
                part = s.total[j, :, pl.ds(core, 1)].reshape(zs, own, -1) + s.sum_core[j]
                s.sum_core[j] = part
                s.sum_dp_out[j] = part.astype(BF16)
        elif hop == 1:
            for k in range(1, groups):
                there = lax.rem(dp + k, groups)
                send(s.sum_dp_out.at[there], s.sum_dp_in.at[dp], sems.at[1], (there, seq))
        elif hop == 2:
            ref = s.sum_dp_in.at[pl.ds(0, groups - 1)]
            wait_for(ref, sems.at[1, 0])
            wait_for(ref, sems.at[1, 1])
            part = s.sum_core[dp]
            for k in range(1, groups):
                part += s.sum_dp_in[lax.rem(dp + k, groups)].astype(F32)
            s.sum_core[0] = part
            s.sum_z_out[...] = part.astype(BF16)
            for k in range(1, zs):
                there = lax.rem(z + k, zs)
                send(s.sum_z_out.at[there], s.sum_z_in.at[z], sems.at[2], (dp, there * 2 + core))
        else:
            ref = s.sum_z_in.at[pl.ds(0, zs - 1)]
            wait_for(ref, sems.at[2, 0])
            wait_for(ref, sems.at[2, 1])
            part = s.sum_core[0, pl.ds(z, 1)].reshape(own, -1)
            for k in range(1, zs):
                part += s.sum_z_in[lax.rem(z + k, zs)].astype(F32)
            rows_grad[...] = part[:, :wide]
            columns = part[:, wide:].T
            shift_grad[...] = beside(columns[:1], columns[1:2])

    sum_hop(0)
    for k in range(HALVES):
        over_couples(k, slopes)
    sum_hop("ready")

    def backward_first(k):
        for m in range(count):
            wait_for(many(s.g_in.at[k, m]), s.g_sem.at[k, m, 1])
            if k == 0:
                wait_for(many(s.scale_in.at[m]), s.scale_sem.at[m, 1])
                scale = s.scale_in[m].reshape(members, BLOCK)
                for q in range(blocks):
                    first = (q * count + m) * members
                    s.scales[first : first + members] = beside(scale, scale)
        if k == 0:
            sum_hop(1)
        rows_in(s.g_in, k)

        def outflow(p, c):
            grad = gather_couple(c) * s.scales[...] * s.slope[p]
            s.grad[p] = grad
            s.outflow[p] = product(two(grad), s.base[p])

        over_couples(k, outflow)

        s.back_scale_out[k] = jnp.zeros((count * groups, BLOCK), F32)

        def scanned(p, c):
            state, total = scan(by_block(s.outflow[p]), p, False)
            s.leaving[p, full_rows - half_rows :] = beside(*state)
            pick_last(p, c, k, total, s.back_out, s.back_scale_out, 0)

        over_couples(k, scanned)
        rows = pl.ds(k * couples, couples)

        @pl.when(half == 1)
        def _():
            send(s.back_out.at[rows], s.back_in.at[rows], s.back_sem.at[k, 0], partner)
            send(s.back_scale_out.at[k], s.back_scale_in.at[k], s.back_sem.at[k, 1], partner)

    def backward_local(k):
        def nearby(p, c):
            grad = s.grad[p]
            s.response[p] = product(two(grad), s.toeplitz[p], TURNED) + scalar_rows(2, p) * grad

        over_couples(k, nearby)

    def backward_second(k):
        rows = pl.ds(k * couples, couples)

        @pl.when(half == 1)
        def _():
            s.back_in[rows] = jnp.zeros((couples, 2 * count * groups, BLOCK), I16)
            s.back_scale_in[k] = jnp.zeros((count * groups, BLOCK), F32)

        @pl.when(half == 0)
        def _():
            wait_for(s.back_in.at[rows], s.back_sem.at[k, 0, 1])
            wait_for(s.back_scale_in.at[k], s.back_sem.at[k, 1, 1])

        def complete(p, c):
            state = carried(
                split(s.leaving[p, full_rows - half_rows :]), s.back_in, s.back_scale_in, p, c, k, False
            )
            s.leaving[p] = through(state, by_block(s.outflow[p]), p, False)

        over_couples(k, complete)

        def respond(p, c):
            grad = s.grad[p]
            drive_grad = s.response[p] + product(two(s.leaving[p]), s.back[p], TURNED)
            norm_grad = drive_grad * s.mask[...]
            for i, value in enumerate((norm_grad * s.own_normed[p], norm_grad, grad * s.drive[p])):
                for side, line in enumerate(split(total_rows(value))):
                    s.part[k, pl.ds(5 * couples + i * own + 2 * c + side, 1), :] = line
            put_couple(c, norm_grad * scalar_rows(0, p))

        over_couples(k, respond)
        rows_out(s.d_out, k)
        for m in range(count):
            s.d_in[m, dp, k, pl.ds(here, 1)] = s.d_out[k, m, pl.ds(me, 1)]
            to_holders(s.d_out.at[k, m], s.d_in.at[m, :, k], s.d_sem.at[k, m])

    for k in range(HALVES):
        backward_first(k)
    for k in range(HALVES):
        backward_local(k)
    for k in range(HALVES):
        backward_second(k)
    sum_hop(2)

    def sum_of_products(first, second):
        (a, b), (c, d) = (split(first), split(second))
        return (total_rows(a * c - b * d), total_rows(a * d + b * c))

    def lag_sums(p, c):
        drive, grad = (two(s.drive[p]), two(s.grad[p]))
        lines = []
        for side in range(2):
            lanes = slice(side * BLOCK, (side + 1) * BLOCK)
            left = over(drive[0][:, lanes], drive[1][:, lanes], drive[0][:, lanes])
            right = over(grad[0][:, lanes], grad[0][:, lanes], grad[1][:, lanes])
            cross = jnp.where(lane_id >= row_id, dot(left, right, SIDEWAYS), 0.0)
            lags = cross[:8]
            for i in range(1, BLOCK // 8):
                lags = lags + pltpu.roll(cross[8 * i : 8 * i + 8], BLOCK - 8 * i, 1)
            for bit in range(3):
                moved = pltpu.roll(lags, BLOCK - (1 << bit), 1)
                lags = jnp.where((row_id[:8] >> bit) & 1 == 1, moved, lags)
            lines.append(total_rows(lags))
        later = [jnp.where(row_lane < BLOCK - 1, pltpu.roll(line, BLOCK - 1, 1), 0.0) for line in lines]
        eight = lax.broadcasted_iota(jnp.int32, (8, 2 * BLOCK), 0)
        near = jnp.where(eight == 0, beside(*(line * shrink for line in lines)), beside(*later))
        s.lags[p] = near

    def correlate(p, c):
        drive, grad, near = (two(s.drive[p]), two(s.grad[p]), two(s.lags[p]))
        entering, leaving = (s.entering[p], s.leaving[p])
        second = folded(over(*drive), s.down_ramp[p])
        third = dot(over(*grad, *near), s.base_ramp[p])
        near = third[2 * full_rows : 2 * full_rows + 8] + third[2 * full_rows + 8 :]
        third = third[:full_rows] + third[full_rows : 2 * full_rows]
        moment = times(sum_of_products(entering, s.outflow[p]), power_of(0, p))
        moment = plus(moment, split(near[:1]))
        paired = times(sum_of_products(leaving, entering), power_of(7, p))
        paired = (paired[0] * float(BLOCK), paired[1] * float(BLOCK))
        paired = plus(paired, plus(sum_of_products(leaving, second), sum_of_products(entering, third)))
        paired = plus(paired, split(near[1:2]))
        for i, line in enumerate(moment + paired):
            s.sums[i, pl.ds(p, 1), :] = line

    shrink = 1.0 / (row_lane.astype(F32) + 1.0)
    for k in range(HALVES):
        over_couples(k, lag_sums)
    for k in range(HALVES):
        over_couples(k, correlate)
    raw = tuple(s.raw[i] for i in range(5))
    moment, paired = ((s.sums[0], s.sums[1]), (s.sums[2], s.sums[3]))
    paired = times(paired, (s.coeff[0], s.coeff[1]))
    _, pull = jax.vjp(coefficient_parts, *raw)
    for i, grad in enumerate(pull((paired[0], -paired[1], moment[0], -moment[1]))):
        for k in range(HALVES):
            s.part[k, i * couples : (i + 1) * couples] = grad[k * couples : (k + 1) * couples]
    send(s.part.at[other], s.part_in, s.part_sem, partner)
    for m in range(count):
        result[m] = s.result[m].T

    def norm_backward(m):
        for k in range(HALVES):
            wait_for(s.d_out.at[k, m, pl.ds(0, members - 1)], s.d_sem.at[k, m, 1])
        inverse = s.inverse[m : m + 1]
        scaled = s.d_in[m].reshape(width, span)
        plain = jnp.zeros((1, span), F32)
        along = jnp.zeros((1, span), F32)
        for j in range(tiles):
            rows = slice(j * BLOCK, (j + 1) * BLOCK)
            piece = scaled[rows].astype(F32)
            plain += total_rows(piece)
            along += total_rows(piece * s.normed[m, rows])
        plain, along = (plain * (1.0 / width), along * (1.0 / width))
        for j in range(tiles):
            rows = slice(j * BLOCK, (j + 1) * BLOCK)
            piece = scaled[rows].astype(F32) - plain - s.normed[m, rows] * along
            piece = s.upstream[m, rows].astype(F32) + inverse * piece
            token_grad[m, :, rows] = piece.astype(BF16).T

    for m in range(count):
        norm_backward(m)

    wait_for(s.part_in, s.part_sem.at[0])
    wait_for(s.part_in, s.part_sem.at[1])
    mine = s.part[half] + s.part_in[...]
    grads = [mine[i * couples : (i + 1) * couples] for i in range(5)]

    def uncoupled(value):
        s.turn[pl.ds(0, couples, stride=2), :] = value
        s.turn[pl.ds(1, couples, stride=2), :] = pltpu.roll(value, states, 1)
        return s.turn[...]

    rate_grad[...] = uncoupled(grads[0])[:, :states]
    turn_grad[...] = uncoupled(grads[1])[:, :states]
    mix_low = own_lane < states
    mix_re = uncoupled(grads[3])
    mixing_grad[...] = jnp.where(mix_low, mix_re, pltpu.roll(uncoupled(grads[4]), states, 1))
    lines = [jnp.where(mix_low, uncoupled(grads[2]), 0.0)]
    lines += [mine[5 * couples + i * own : 5 * couples + (i + 1) * own] for i in range(3)]
    ones = jnp.ones((8, BLOCK), F32)
    for rows, out in zip(lines, (spacing_grad, gain_grad, bias_grad, skip_grad), strict=True):
        line = lax.dot_general(ones, rows, (TURNED, ((), ())), preferred_element_type=F32, precision=HIGH)
        out[...] = line[:1]

    sum_hop(3)

    wait_for(many(s.note_in), s.note_sem.at[0])
    for m in range(count):
        wait_for(many(s.scale_in.at[m]), s.scale_sem.at[m, 0])
        for k in range(HALVES):
            wait_for(many(s.x_in.at[k, m]), s.x_sem.at[k, m, 0])
            wait_for(many(s.a_out.at[k, m]), s.a_sem.at[k, m, 0])
            wait_for(many(s.g_in.at[k, m]), s.g_sem.at[k, m, 0])
            wait_for(many(s.d_out.at[k, m]), s.d_sem.at[k, m, 0])
    for k in range(HALVES):
        rows = pl.ds(k * couples, couples)

        @pl.when(half == 0)
        def _():
            wait_for(s.carry_out.at[rows], s.carry_sem.at[k, 0, 0])
            wait_for(s.carry_scale_out.at[k], s.carry_sem.at[k, 1, 0])

        @pl.when(half == 1)
        def _():
            wait_for(s.back_out.at[rows], s.back_sem.at[k, 0, 0])
            wait_for(s.back_scale_out.at[k], s.back_sem.at[k, 1, 0])


class Scratch:
    def __init__(self, names, refs):
        for name, ref in zip(names, refs, strict=True):
            setattr(self, name, ref)


def scratch_of(size, states):
    groups, parts, own, width, span, count = size
    local, blocks, zs = (parts // HALVES, span // BLOCK, parts // 2)
    members, couples = (groups * local, own // 2)
    every = HALVES * couples
    rows = blocks * count * members
    bits = 7 + (blocks * local).bit_length()
    wide = 2 * width + BLOCK
    vmem, sems = (pltpu.VMEM, pltpu.SemaphoreType.DMA)
    by_holder = (HALVES, count, groups, local, own, span)
    by_owner = (HALVES, count, members, own, span)
    filed = (count, groups, HALVES, local, own, span)
    chunk_sems = sems((HALVES, count, 2))
    held = vmem((every, rows, 2 * BLOCK), F32)
    table, plain = (vmem((every, 2, 2 * BLOCK, 2 * BLOCK), BF16), vmem((every, 2 * BLOCK, 2 * BLOCK), BF16))
    kept = vmem((every, BLOCK, 2 * BLOCK), F32)
    carry, carry_sems = (vmem((every, 2 * count * groups, BLOCK), I16), sems((HALVES, 2, 2)))
    carry_scale = vmem((HALVES, count * groups, BLOCK), F32)
    part_rows = 5 * couples + 3 * own
    return {
        "tokens": vmem((count, width, span), BF16),
        "upstream": vmem((count, width, span), BF16),
        "result": vmem((count, width, span), BF16),
        "normed": vmem((count, width, span), F32),
        "inverse": vmem((count, span), F32),
        "valid": vmem((count, span), F32),
        "x_out": vmem(by_holder, I16), "x_in": vmem(by_owner, I16), "x_sem": chunk_sems,
        "a_out": vmem(by_owner, BF16), "a_in": vmem(filed, BF16), "a_sem": chunk_sems,
        "g_out": vmem(by_holder, I16), "g_in": vmem(by_owner, I16), "g_sem": chunk_sems,
        "d_out": vmem(by_owner, BF16), "d_in": vmem(filed, BF16), "d_sem": chunk_sems,
        "note_out": vmem((1, 1, BLOCK), F32), "note_in": vmem((members, 1, BLOCK), F32), "note_sem": sems((2,)),
        "scale_out": vmem((count, 1, BLOCK), F32), "scale_in": vmem((count, members, 1, BLOCK), F32),
        "scale_sem": sems((count, 2)),
        "scales": vmem((rows, 2 * BLOCK), F32),
        "params": vmem((HALVES, own, 3 * BLOCK), F32), "params_sem": sems((2,)),
        "weight_out": vmem((own, wide), BF16),
        "weight": vmem((groups, zs, 2, own, wide), BF16), "weight_sem": sems((3, 2)),
        "flat": vmem((width, 2 * width), BF16),
        "flipped": vmem((2 * width, width), BF16),
        "shift": vmem((2 * width, BLOCK), F32),
        "pre_grad": vmem((2 * width, count * span), BF16),
        "pre": vmem((2 * width, span), F32),
        "act_grad": vmem((width, span), F32),
        "total": vmem((groups, zs, 2, own, wide), F32),
        "sum_core": vmem((groups, zs, own, wide), F32),
        "sum_dp_out": vmem((groups, zs, own, wide), BF16),
        "sum_dp_in": vmem((groups, zs, own, wide), BF16),
        "sum_z_out": vmem((zs, own, wide), BF16),
        "sum_z_in": vmem((zs, own, wide), BF16),
        "sum_sem": sems((3, 2)),
        "turn": vmem((own, BLOCK), F32),
        "scalars": vmem((3, HALVES * own, BLOCK), F32),
        "power": vmem((bits, 2, every, BLOCK), F32),
        "lead": vmem((2, every, BLOCK), F32),
        "coeff": vmem((2, every, BLOCK), F32),
        "base": table, "down": table, "up": table, "back": table, "toeplitz": table,
        "base_ramp": plain, "down_ramp": plain, "base_kept": kept, "down_kept": kept, "response": held,
        "stage_in": vmem((blocks, count, members * own, BLOCK), F32),
        "stage_out": vmem((blocks, count, members * own, BLOCK), F32),
        "mask": vmem((rows, 2 * BLOCK), F32),
        "own_normed": held, "drive": held, "entering": held, "slope": held, "inflow": held,
        "grad": held, "outflow": held, "leaving": held,
        "widen": vmem((every, 2, count * members, BLOCK), F32),
        "carry_out": carry, "carry_in": carry, "carry_sem": carry_sems,
        "back_out": carry, "back_in": carry, "back_sem": carry_sems,
        "carry_scale_out": carry_scale, "carry_scale_in": carry_scale,
        "back_scale_out": carry_scale, "back_scale_in": carry_scale,
        "sums": vmem((4, every, BLOCK), F32),
        "raw": vmem((5, every, BLOCK), F32), "lags": vmem((every, 8, 2 * BLOCK), F32),
        "part": vmem((HALVES, part_rows, BLOCK), F32), "part_in": vmem((part_rows, BLOCK), F32),
        "part_sem": sems((2,)),
    }


def handed_over(values):
    def kernel(*refs):
        for given, out in zip(refs[: len(values)], refs[len(values) :], strict=True):
            out[...] = given[...].reshape(out.shape)

    shapes = [(value.size,) if value.shape[0] == 1 else value.shape for value in values]
    return pl.pallas_call(
        kernel,
        out_shape=[jax.ShapeDtypeStruct(shape, value.dtype) for shape, value in zip(shapes, values, strict=True)],
        in_specs=[pl.BlockSpec(memory_space=pltpu.VMEM)] * len(values),
        out_specs=[pl.BlockSpec(memory_space=pltpu.VMEM)] * len(values),
    )(*values)


def in_one_kernel(groups, parts, *args):
    inputs, lengths, ln_gain, ln_bias, lam_log, lam_im, log_dt, mix_weight, skip, glu_weight, glu_bias, out_grad = args
    count, span, width = inputs.shape
    own = ln_gain.shape[0]
    size = (groups, parts, own, width, span, count)
    scratch = scratch_of(size, lam_log.shape[1])

    def kernel(*refs):
        arguments, results, kept = (refs[:12], refs[12:23], refs[23:])
        whole_kernel(size, *arguments, *results, Scratch(scratch, kept))

    vmem, smem = (pl.BlockSpec(memory_space=pltpu.VMEM), pl.BlockSpec(memory_space=pltpu.SMEM))
    line = jax.ShapeDtypeStruct((1, own), F32)
    outs = pl.pallas_call(
        kernel,
        out_shape=(
            jax.ShapeDtypeStruct(inputs.shape, BF16),
            jax.ShapeDtypeStruct(inputs.shape, BF16),
            line,
            line,
            jax.ShapeDtypeStruct(lam_log.shape, F32),
            jax.ShapeDtypeStruct(lam_im.shape, F32),
            line,
            jax.ShapeDtypeStruct(mix_weight.shape, F32),
            line,
            jax.ShapeDtypeStruct(glu_weight.shape, F32),
            jax.ShapeDtypeStruct((1, 2 * own), F32),
        ),
        in_specs=[vmem, smem, smem, smem, vmem, vmem, smem, vmem, smem, vmem, smem, vmem],
        out_specs=[vmem] * 11,
        scratch_shapes=list(scratch.values()),
        compiler_params=pltpu.CompilerParams(
            collective_id=0, has_side_effects=True, vmem_limit_bytes=62 * 1024 * 1024
        ),
    )(*args)
    return tuple(handed_over(outs))


def solution(mesh):
    tokens, vector, matrix = (P("dp", "seq", None), P(BOTH), P(BOTH, None))
    groups, parts = (mesh.shape["dp"], mesh.shape["seq"])

    def step(*args):
        own = args[2].shape[0]
        if own % 16 == 0 and parts % 4 == 0:
            return in_one_kernel(groups, parts, *args)
        return per_device(*args)

    return jax.shard_map(
        step,
        mesh=mesh,
        in_specs=(
            tokens, P("dp"), vector, vector, matrix, matrix, vector, matrix, vector, matrix, vector, tokens,
        ),
        out_specs=(
            tokens, tokens, vector, vector, matrix, matrix, vector, matrix, vector, matrix, vector,
        ),
        check_vma=False,
    )
```

```python
import math
from functools import partial

import jax
import jax.numpy as jnp
from jax import lax
from jax.experimental import pallas as pl
from jax.experimental.pallas import tpu as pltpu
from jax.sharding import PartitionSpec as P

BLOCK = 128
EPS = 1e-05
HIGH = lax.Precision.HIGHEST
BOTH = ("dp", "seq")


def halves(packed):
    count = packed.shape[-1] // 2
    return (packed[..., :count], packed[..., count:])


def cmul(first, second):
    first_re, first_im = halves(first)
    second_re, second_im = halves(second)
    return jnp.concatenate(
        [first_re * second_re - first_im * second_im, first_re * second_im + first_im * second_re],
        axis=-1,
    )


def conjugate(packed):
    real_half, imag_half = halves(packed)
    return jnp.concatenate([real_half, -imag_half], axis=-1)


def coefficients(lam_log, lam_im, log_dt, mix_weight):
    spacing = jnp.exp(log_dt)[:, None]
    rate = jnp.exp(lam_log)
    shrink = -rate * spacing
    angle = lam_im * spacing
    scale = jnp.exp(shrink)
    decay = jnp.concatenate([scale * jnp.cos(angle), scale * jnp.sin(angle)], axis=-1)
    less_re = jnp.expm1(shrink) * jnp.cos(angle) - 2.0 * jnp.sin(0.5 * angle) ** 2
    less_im = scale * jnp.sin(angle)
    modulus = rate * rate + lam_im * lam_im
    ratio = jnp.concatenate(
        [
            (lam_im * less_im - rate * less_re) / modulus,
            -(rate * less_im + lam_im * less_re) / modulus,
        ],
        axis=-1,
    )
    return (decay, cmul(mix_weight, ratio))


def powers(decay):
    real_half, imag_half = halves(decay)
    table = jnp.concatenate([jnp.ones_like(real_half), jnp.zeros_like(imag_half)], axis=-1)[:, None]
    step = decay[:, None]
    while table.shape[1] < BLOCK:
        table = jnp.concatenate([table, cmul(step, table)], axis=1)
        step = cmul(step, step)
    return (table, step[:, 0])


def link(earlier, later):
    return (cmul(earlier[0], later[0]), cmul(later[0], earlier[1]) + later[1])


def shifted(pieces, step, back):
    leads = jnp.broadcast_to(step[:, None, None], pieces.shape)
    _, reach = lax.associative_scan(link, (leads, pieces), axis=2, reverse=back)
    none = jnp.zeros_like(reach[:, :, :1])
    if back:
        return jnp.concatenate([reach[:, :, 1:], none], axis=2)
    return jnp.concatenate([none, reach[:, :, :-1]], axis=2)


def to_owner(rows):
    count, span, width = rows.shape
    groups, parts = (lax.axis_size("dp"), lax.axis_size("seq"))
    own = width // (groups * parts)
    sent = rows.reshape(count * span, width).T.reshape(-1, own, count, span)
    held = lax.all_to_all(sent, BOTH, 0, 0, tiled=True).reshape(groups, parts, own, count, span)
    held = held.transpose(2, 0, 3, 1, 4).reshape(own, groups * count, -1, BLOCK)
    return held


def to_holder(held, count, span):
    groups, parts = (lax.axis_size("dp"), lax.axis_size("seq"))
    own = held.shape[0]
    sent = held.astype(jnp.bfloat16).reshape(own, groups, count, parts, span).transpose(1, 3, 0, 2, 4)
    sent = sent.reshape(groups * parts, own, count, span)
    rows = lax.all_to_all(sent, BOTH, 0, 0, tiled=True)
    return rows.reshape(-1, count * span).T.reshape(count, span, -1).astype(jnp.float32)


def per_device(
    inputs,
    lengths,
    ln_gain,
    ln_bias,
    lam_log,
    lam_im,
    log_dt,
    mix_weight,
    skip,
    glu_weight,
    glu_bias,
    out_grad,
):
    count, span, width = inputs.shape
    offset = lax.axis_index("seq") * span
    positions = offset + jnp.arange(span, dtype=jnp.int32)
    valid = (positions[None, :] < lengths[:, None]).astype(jnp.float32)[..., None]
    rows = lax.all_gather(glu_weight, BOTH, axis=0, tiled=True)
    shift = lax.all_gather(glu_bias, BOTH, axis=0, tiled=True)
    spans = lax.all_gather(lengths, "dp", axis=0, tiled=True)
    whole_span = span * lax.axis_size("seq")
    mask = (jnp.arange(whole_span, dtype=jnp.int32)[None] < spans[:, None]).astype(jnp.float32)
    mask = mask.reshape(1, -1, whole_span // BLOCK, BLOCK)

    tokens = inputs.astype(jnp.float32)
    mean = jnp.mean(tokens, axis=-1, keepdims=True)
    centered = tokens - mean
    inverse = lax.rsqrt(jnp.mean(centered * centered, axis=-1, keepdims=True) + EPS)
    normed = centered * inverse

    (decay, coeff), coeff_pull = jax.vjp(coefficients, lam_log, lam_im, log_dt, mix_weight)
    base, whole = powers(decay)
    down = base[:, ::-1]
    real_half, imag_half = halves(coeff)
    kernel = jnp.einsum("cz,ckz->ck", conjugate(coeff), base, precision=HIGH)
    lead = cmul(coeff, decay)[:, None]
    up = conjugate(cmul(lead, base))
    back = conjugate(cmul(lead, down))
    steps = jnp.arange(BLOCK)
    lag = steps[:, None] - steps[None, :]
    toeplitz = jnp.where(lag >= 0, kernel[:, jnp.maximum(lag, 0)], 0.0)
    ramp = steps.astype(jnp.float32)[:, None]

    gain, bias, skipping = (p[:, None, None, None] for p in (ln_gain, ln_bias, skip))
    own_normed = to_owner(normed)
    drive = (own_normed * gain + bias) * mask
    entering = shifted(jnp.einsum("cbqj,cjz->cbqz", drive, down, precision=HIGH), whole, False)
    response = jnp.einsum("cij,cbqj->cbqi", toeplitz, drive, precision=HIGH)
    response += jnp.einsum("ciz,cbqz->cbqi", up, entering, precision=HIGH) + skipping * drive
    activated, gelu_pull = jax.vjp(partial(jax.nn.gelu, approximate=False), response)
    activated = to_holder(activated, count, span).astype(jnp.bfloat16).reshape(-1, width)
    pre = jnp.dot(activated, rows, preferred_element_type=jnp.float32) + shift
    gate = jax.nn.sigmoid(pre[:, width:])
    flat_valid = valid.reshape(-1, 1)
    result = (tokens + (pre[:, :width] * gate * flat_valid).reshape(tokens.shape)).astype(jnp.bfloat16)
    upstream = out_grad.astype(jnp.float32)
    gated = upstream.reshape(-1, width) * flat_valid
    pre_grad = jnp.concatenate(
        [gated * gate, gated * pre[:, :width] * gate * (1.0 - gate)], axis=-1
    ).astype(jnp.bfloat16)
    rows_grad = lax.dot_general(
        activated, pre_grad, (((0,), (0,)), ((), ())), preferred_element_type=jnp.float32
    )
    shift_grad = jnp.sum(pre_grad.astype(jnp.float32), axis=0)
    act_grad = lax.dot_general(
        pre_grad, rows, (((1,), (1,)), ((), ())), preferred_element_type=jnp.float32
    )
    response_grad = gelu_pull(to_owner(act_grad.reshape(tokens.shape)))[0]

    skip_grad = jnp.sum(response_grad * drive, axis=(1, 2, 3))
    outflow = jnp.einsum("cbqt,ctz->cbqz", response_grad, base, precision=HIGH)
    leaving = shifted(outflow, whole, True)
    drive_grad = jnp.einsum("cij,cbqi->cbqj", toeplitz, response_grad, precision=HIGH)
    drive_grad += jnp.einsum("cjz,cbqz->cbqj", back, leaving, precision=HIGH) + skipping * response_grad
    norm_grad = drive_grad * mask
    gain_grad = jnp.sum(norm_grad * own_normed, axis=(1, 2, 3))
    bias_grad = jnp.sum(norm_grad, axis=(1, 2, 3))
    scaled = to_holder(norm_grad * gain, count, span)
    token_grad = upstream + inverse * (
        scaled
        - jnp.mean(scaled, axis=-1, keepdims=True)
        - normed * jnp.mean(scaled * normed, axis=-1, keepdims=True)
    )

    cross = jnp.einsum("cbqj,cbqi->cij", drive, response_grad, precision=HIGH)
    lags = jnp.stack([jnp.trace(cross, offset=-k, axis1=1, axis2=2) for k in range(BLOCK)], axis=-1)
    second = jnp.einsum("cbqj,cjz->cbqz", drive, down * ramp[::-1], precision=HIGH)
    third = jnp.einsum("cbqt,ctz->cbqz", response_grad, base * (ramp + 1.0), precision=HIGH)
    total = partial(jnp.sum, axis=(1, 2))
    moment = cmul(decay, total(cmul(entering, outflow))) + jnp.einsum("ck,ckz->cz", lags, base, precision=HIGH)
    before = jnp.concatenate([jnp.zeros_like(base[:, :1]), base[:, :-1]], axis=1) * ramp
    paired = BLOCK * cmul(whole, total(cmul(leaving, entering)))
    paired += total(cmul(leaving, second) + cmul(entering, third))
    paired = cmul(coeff, paired + jnp.einsum("ck,ckz->cz", lags, before, precision=HIGH))
    rate_grad, turn_grad, spacing_grad, mixing_grad = coeff_pull((conjugate(paired), conjugate(moment)))

    scatter = partial(lax.psum_scatter, axis_name=BOTH, scatter_dimension=0, tiled=True)
    return (
        result,
        token_grad.astype(jnp.bfloat16),
        gain_grad,
        bias_grad,
        rate_grad,
        turn_grad,
        spacing_grad,
        mixing_grad,
        skip_grad,
        scatter(rows_grad),
        scatter(shift_grad),
    )


MESH = pl.DeviceIdType.MESH
F32, BF16, I16 = (jnp.float32, jnp.bfloat16, jnp.int16)
STEPS = 32700.0
GROUP = 4
HALVES = 2


def two(value):
    high = value.astype(BF16)
    return (high, (value - high.astype(F32)).astype(BF16))


def dot(left, right, dims=((1,), (0,))):
    return lax.dot_general(left, right, (dims, ((), ())), preferred_element_type=F32)


TURNED = ((1,), (1,))
SIDEWAYS = ((0,), (0,))


def product(left, table, dims=((1,), (0,))):
    return folded(over(*left), table[0], dims) + dot(left[0], table[1], dims)


def folded(rows, table, dims=((1,), (0,))):
    value = dot(rows, table, dims)
    half = value.shape[0] // 2
    return value[:half] + value[half:]


def times(value, factor):
    return (value[0] * factor[0] - value[1] * factor[1], value[0] * factor[1] + value[1] * factor[0])


def plus(first, second):
    return (first[0] + second[0], first[1] + second[1])


def choose(condition, first, second):
    return (jnp.where(condition, first[0], second[0]), jnp.where(condition, first[1], second[1]))


def split(value):
    return (value[:, :BLOCK], value[:, BLOCK:])


def beside(*parts):
    return jnp.concatenate(parts, axis=1)


def over(*parts):
    return jnp.concatenate(parts, axis=0)


def total_rows(value):
    return jnp.sum(value, axis=0, keepdims=True)


def small_expm1(value):
    near = jnp.abs(value) < 0.5
    small = jnp.where(near, value, 0.0)
    series = jnp.ones_like(small)
    for order in range(10, 1, -1):
        series = 1.0 + small * (1.0 / order) * series
    return jnp.where(near, small * series, jnp.exp(value) - 1.0)


def coefficient_parts(lam_log, lam_im, log_dt, mix_re, mix_im):
    spacing, rate = (jnp.exp(log_dt), jnp.exp(lam_log))
    shrink, angle = (-rate * spacing, lam_im * spacing)
    scale = jnp.exp(shrink)
    cosine, sine, half = (jnp.cos(angle), jnp.sin(angle), jnp.sin(0.5 * angle))
    less_re = small_expm1(shrink) * cosine - 2.0 * half * half
    less_im = scale * sine
    modulus = rate * rate + lam_im * lam_im
    ratio = (
        (lam_im * less_im - rate * less_re) / modulus,
        -(rate * less_im + lam_im * less_re) / modulus,
    )
    return (scale * cosine, less_im) + times((mix_re, mix_im), ratio)


def whole_kernel(
    size,
    inputs, lengths, ln_gain, ln_bias, lam_log, lam_im, log_dt, mix_weight, skip, glu_weight, glu_bias, out_grad,
    result, token_grad, gain_grad, bias_grad, rate_grad, turn_grad, spacing_grad, mixing_grad, skip_grad,
    rows_grad, shift_grad,
    s,
):
    groups, parts, own, width, span, count = size
    local, blocks, zs = (parts // HALVES, span // BLOCK, parts // 2)
    members = groups * local
    tiles, couples, states = (width // BLOCK, own // 2, lam_log.shape[1])
    wide = 2 * width
    dp, seq = (lax.axis_index("dp"), lax.axis_index("seq"))
    core, z = (lax.rem(seq, 2), seq // 2)
    half, here = (seq // local, lax.rem(seq, local))
    other = 1 - half
    me = dp * local + here
    partner = (dp, other * local + here)

    def place(member):
        return (member // local, half * local + lax.rem(member, local))

    def send(source, target, sems, device):
        pltpu.make_async_remote_copy(
            src_ref=source, dst_ref=target, send_sem=sems.at[0], recv_sem=sems.at[1],
            device_id=device, device_id_type=MESH,
        ).start()

    def wait_for(ref, sem):
        pltpu.make_async_copy(ref, ref, sem).wait()

    def to_owners(out, into, sems):
        for k in range(1, members):
            member = lax.rem(me + k, members)
            send(out.at[member // local, lax.rem(member, local)], into.at[me], sems, place(member))

    def to_holders(out, into, sems):
        for k in range(1, members):
            member = lax.rem(me + k, members)
            send(out.at[member], into.at[dp, here], sems, place(member))

    def to_all(out, into, sems):
        for k in range(1, members):
            send(out, into.at[me], sems, place(lax.rem(me + k, members)))

    def many(ref):
        return ref.at[pl.ds(0, members - 1)]

    barrier = pltpu.get_barrier_semaphore()

    def greet(k, carry):
        member = place(lax.rem(me + k, members))
        pl.semaphore_signal(barrier, inc=1, device_id=member, device_id_type=MESH)
        return carry

    lax.fori_loop(1, members, greet, 0)
    for k in range(zs // HALVES):
        there = other * local + 2 * k + core
        pl.semaphore_signal(barrier, inc=1, device_id=(dp, there), device_id_type=MESH)

    lane = lax.broadcasted_iota(jnp.int32, (1, span), 1) + seq * span
    quantum = math.sqrt(width) / STEPS

    def chunk_rows(j):
        per = BLOCK // own
        for i in range(per):
            shard = j * per + i
            yield slice(i * own, (i + 1) * own), shard // parts, shard % parts // local, shard % local

    def norm(m):
        tokens = inputs[m].T
        s.tokens[m] = tokens
        total = jnp.zeros((1, span), F32)
        for j in range(tiles):
            total += total_rows(tokens[j * BLOCK : (j + 1) * BLOCK].astype(F32))
        mean = total * (1.0 / width)
        total = jnp.zeros((1, span), F32)
        for j in range(tiles):
            off = tokens[j * BLOCK : (j + 1) * BLOCK].astype(F32) - mean
            total += total_rows(off * off)
        inverse = lax.rsqrt(total * (1.0 / width) + EPS)
        valid = (lane < lengths[m]).astype(F32)
        s.inverse[m : m + 1] = inverse
        s.valid[m : m + 1] = valid
        for j in range(tiles):
            normed = (tokens[j * BLOCK : (j + 1) * BLOCK].astype(F32) - mean) * inverse
            s.normed[m, j * BLOCK : (j + 1) * BLOCK] = normed
            coded = jnp.round(normed * valid * (1.0 / quantum)).astype(I16)
            for rows, a, k, p in chunk_rows(j):
                s.x_out[k, m, a, p] = coded[rows]
        for k in range(HALVES):
            s.x_in[k, m, pl.ds(me, 1)] = s.x_out[k, m, dp, pl.ds(here, 1)]

    for p in range(HALVES * couples):
        for part in range(2):
            s.toeplitz[p, part, :BLOCK, BLOCK:] = jnp.zeros((BLOCK, BLOCK), BF16)
            s.toeplitz[p, part, BLOCK:, :BLOCK] = jnp.zeros((BLOCK, BLOCK), BF16)

    row_lane = lax.broadcasted_iota(jnp.int32, (1, BLOCK), 1)
    row = jnp.zeros((1, BLOCK), F32)
    for m in range(count):
        row = jnp.where(row_lane == m, lengths[m].astype(F32), row)
    s.note_out[0] = row
    s.note_in[pl.ds(me, 1)] = row[None]

    own_row = lax.broadcasted_iota(jnp.int32, (own, BLOCK), 0)
    own_lane = lax.broadcasted_iota(jnp.int32, (own, BLOCK), 1)
    scalars = jnp.zeros((own, BLOCK), F32)
    shifts = jnp.zeros((own, BLOCK), F32)
    for c in range(own):
        for i, ref in enumerate((log_dt, ln_gain, ln_bias, skip)):
            scalars = jnp.where((own_row == c) & (own_lane == i), ref[c], scalars)
        for i in range(2):
            shifts = jnp.where((own_row == c) & (own_lane % 2 == i), glu_bias[i * own + c], shifts)
    s.params[pl.ds(half, 1), :, :states] = lam_log[...][None]
    s.params[pl.ds(half, 1), :, states : 2 * states] = lam_im[...][None]
    s.params[pl.ds(half, 1), :, BLOCK : 2 * BLOCK] = mix_weight[...][None]
    s.params[pl.ds(half, 1), :, 2 * BLOCK :] = scalars[None]
    high = shifts.astype(BF16)
    rest = shifts - high.astype(F32)
    middle = rest.astype(BF16)
    lowest = (rest - middle.astype(F32)).astype(BF16)
    thirds = jnp.where(own_lane < 2, high, jnp.where(own_lane < 4, middle, lowest))
    s.weight_out[:, :wide] = glu_weight[...]
    s.weight_out[:, wide:] = thirds
    s.weight[pl.ds(dp, 1), pl.ds(z, 1), pl.ds(core, 1)] = s.weight_out[...][None, None, None]

    def weight_hop(hop):
        sems = s.weight_sem.at[hop]
        if hop == 0:
            for k in range(1, zs):
                there = lax.rem(z + k, zs)
                send(s.weight_out, s.weight.at[dp, z, core], sems, (dp, there * 2 + core))
        elif hop == 1:
            for k in range(1, groups):
                mine = s.weight.at[dp, :, core]
                send(mine, mine, sems, (lax.rem(dp + k, groups), seq))
        else:
            mine = s.weight.at[:, :, core]
            send(mine, mine, sems, (dp, z * 2 + 1 - core))

    def weight_wait(hop):
        if hop == 0:
            ref = s.weight.at[0, pl.ds(0, zs - 1), 0]
        elif hop == 1:
            ref = s.weight.at[pl.ds(0, groups - 1), :, 0]
        else:
            ref = s.weight.at[:, :, 0]
        wait_for(ref, s.weight_sem.at[hop, 0])
        wait_for(ref, s.weight_sem.at[hop, 1])

    pl.semaphore_wait(barrier, members - 1 + zs // HALVES)
    send(s.params.at[half], s.params.at[half], s.params_sem, partner)
    to_all(s.note_out.at[0], s.note_in, s.note_sem)
    weight_hop(0)
    for m in range(count):
        norm(m)
    for k in range(HALVES):
        for m in range(count):
            to_owners(s.x_out.at[k, m], s.x_in.at[k, m], s.x_sem.at[k, m])

    wait_for(s.params.at[0], s.params_sem.at[0])
    wait_for(s.params.at[0], s.params_sem.at[1])
    pair_low = lax.broadcasted_iota(jnp.int32, (couples, BLOCK), 1) < states

    def coupled(value):
        s.turn[...] = value
        even = s.turn[pl.ds(0, couples, stride=2), :]
        odd = s.turn[pl.ds(1, couples, stride=2), :]
        return jnp.where(pair_low, even, pltpu.roll(odd, states, 1))

    def raw_params(k):
        packed = [s.params[k, :, i * BLOCK : (i + 1) * BLOCK] for i in range(3)]
        lam, mix, rest = packed
        log_step = jnp.broadcast_to(rest[:, :1], (own, BLOCK))
        return tuple(
            coupled(value)
            for value in (lam, pltpu.roll(lam, states, 1), log_step, mix, pltpu.roll(mix, states, 1))
        )

    for k in range(HALVES):
        rest = s.params[k, :, 2 * BLOCK :]
        for i in range(1, 4):
            s.scalars[i - 1, k * own : (k + 1) * own] = jnp.broadcast_to(rest[:, i : i + 1], (own, BLOCK))
        rows = slice(k * couples, (k + 1) * couples)
        for i, value in enumerate(raw_params(k)):
            s.raw[i, rows] = value
        parts_k = coefficient_parts(*(s.raw[i, rows] for i in range(5)))
        decay, coeff = (parts_k[:2], parts_k[2:])
        s.coeff[0, rows], s.coeff[1, rows] = coeff
        s.lead[0, rows], s.lead[1, rows] = times(coeff, decay)
        power = decay
        for bit in range(s.power.shape[0]):
            s.power[bit, 0, rows], s.power[bit, 1, rows] = power
            power = times(power, power)

    def power_of(bit, p):
        return (s.power[bit, 0, pl.ds(p, 1), :], s.power[bit, 1, pl.ds(p, 1), :])

    square = (BLOCK, BLOCK)
    row_id = lax.broadcasted_iota(jnp.int32, square, 0)
    lane_id = lax.broadcasted_iota(jnp.int32, square, 1)
    ramp = row_id.astype(F32)
    first_states = lax.rem(lax.broadcasted_iota(jnp.int32, (BLOCK, 2 * BLOCK), 1), BLOCK) < states

    def stacked(value):
        none = jnp.zeros_like(value)
        return over(jnp.where(first_states, value, none), jnp.where(first_states, none, value))

    def put_table(ref, p, value):
        for i, part in enumerate(two(beside(*value))):
            ref[p, i] = stacked(part)

    def tables_first(p):
        eight = row_id[:8]
        unit = (jnp.ones((8, BLOCK), F32), jnp.zeros((8, BLOCK), F32))
        base, down = (unit, unit)
        for bit in range(3):
            step = power_of(bit, p)
            base = choose((eight >> bit) & 1 == 1, times(base, step), base)
            down = choose(((7 - eight) >> bit) & 1 == 1, times(down, step), down)
        for bit in range(3, 7):
            step = power_of(bit, p)
            more, most = (times(base, step), times(down, step))
            base = (over(base[0], more[0]), over(base[1], more[1]))
            down = (over(most[0], down[0]), over(most[1], down[1]))
        s.base_kept[p] = beside(*base)
        s.down_kept[p] = beside(*down)
        put_table(s.down, p, down)

    def tables_middle(p):
        base = split(s.base_kept[p])
        up = times(base, (s.lead[0, pl.ds(p, 1), :], s.lead[1, pl.ds(p, 1), :]))
        put_table(s.up, p, (up[0], -up[1]))
        weights = beside(s.coeff[0, pl.ds(p, 1), :], -s.coeff[1, pl.ds(p, 1), :])
        weights = jnp.broadcast_to(weights, (8, 2 * BLOCK))
        pick = lax.rem(lax.broadcasted_iota(jnp.int32, (8, 2 * BLOCK), 1), BLOCK) < states
        pick = pick == (lax.broadcasted_iota(jnp.int32, (8, 2 * BLOCK), 0) == 0)
        weights, base = (two(jnp.where(pick, weights, 0.0)), two(beside(*base)))
        kernel = folded(over(*weights), base[0], TURNED) + dot(weights[0], base[1], TURNED)
        for i in range(2):
            slanted = jnp.broadcast_to(kernel[i : i + 1], square)
            slanted = pltpu.roll(slanted, 0, 1, stride=1, stride_axis=0)
            side = slice(i * BLOCK, (i + 1) * BLOCK)
            for part, value in enumerate(two(jnp.where(lane_id >= row_id, slanted, 0.0))):
                s.toeplitz[p, part, side, side] = value

    def tables_second(p):
        base, down = (split(s.base_kept[p]), split(s.down_kept[p]))
        back = times(down, (s.lead[0, pl.ds(p, 1), :], s.lead[1, pl.ds(p, 1), :]))
        put_table(s.base, p, base)
        put_table(s.back, p, (back[0], -back[1]))
        for ref, value, slope in (
            (s.base_ramp, base, ramp + 1.0),
            (s.down_ramp, down, BLOCK - 1.0 - ramp),
        ):
            ref[p] = stacked(beside(value[0] * slope, value[1] * slope).astype(BF16))

    def over_couples(k, body, group=GROUP):
        def some(g, carry):
            for u in range(group):
                body(k * couples + g * group + u, g * group + u)
            return carry

        lax.fori_loop(0, couples // group, some, 0)

    for k in range(HALVES):
        over_couples(k, lambda p, c: tables_first(p))

    half_rows = count * members
    full_rows = blocks * half_rows
    place_of = lax.rem(lax.broadcasted_iota(jnp.int32, (half_rows, BLOCK), 0), local)
    place_lane = lax.broadcasted_iota(jnp.int32, (half_rows, BLOCK), 1)
    step_bit = 7 + blocks.bit_length() - 1

    def rows_in(ref, k):
        for m in range(count):
            for q in range(blocks):
                piece = ref[k, m, :, :, q * BLOCK : (q + 1) * BLOCK]
                s.stage_in[q, m] = piece.astype(F32).reshape(members * own, BLOCK)

    def rows_out(ref, k):
        for m in range(count):
            for q in range(blocks):
                ref[k, m, :, :, q * BLOCK : (q + 1) * BLOCK] = (
                    s.stage_out[q, m].astype(BF16).reshape(members, own, BLOCK)
                )

    def gather_couple(c):
        sides = []
        for i in range(2):
            sides.append(
                over(
                    *(
                        s.stage_in[q, m, pl.ds(2 * c + i, members, stride=own), :]
                        for q in range(blocks)
                        for m in range(count)
                    )
                )
            )
        return beside(*sides)

    def put_couple(c, value):
        for i, side in enumerate(split(value)):
            for q in range(blocks):
                for m in range(count):
                    first = (q * count + m) * members
                    s.stage_out[q, m, pl.ds(2 * c + i, members, stride=own), :] = side[first : first + members]

    def scalar_rows(i, p):
        return beside(s.scalars[i, pl.ds(2 * p, 1), :], s.scalars[i, pl.ds(2 * p + 1, 1), :])

    def by_block(value):
        return [split(value[q * half_rows : (q + 1) * half_rows]) for q in range(blocks)]

    def scan(flows, p, upward):
        block_step = power_of(7, p)
        flows = flows if upward else flows[::-1]
        total = flows[0]
        for flow in flows[1:]:
            total = plus(times(total, block_step), flow)

        def moved(value, reach):
            shift = reach if upward else half_rows - reach
            inside = place_of >= reach if upward else place_of < local - reach
            return tuple(jnp.where(inside, pltpu.roll(part, shift, 0), 0.0) for part in value)

        reach = 1
        while reach < local:
            total = plus(total, times(moved(total, reach), power_of(step_bit + reach.bit_length() - 1, p)))
            reach *= 2
        return moved(total, 1), total

    def carried(state, ref, scales, p, c, k, upward):
        scale = jnp.sum(jnp.where(carry_lane == c, scales[k], 0.0), axis=1, keepdims=True)
        lines = ref[p].astype(F32)
        lines = (lines[: count * groups] * scale, lines[count * groups :] * scale)
        for j in range(local):
            for i in range(2):
                s.widen[p, i, pl.ds(j, count * groups, stride=local), :] = lines[i]
        carry = (s.widen[p, 0], s.widen[p, 1])
        distance = place_of if upward else local - 1 - place_of
        for bit in range(local.bit_length() - 1):
            further = times(carry, power_of(step_bit + bit, p))
            carry = choose((distance >> bit) & 1 == 1, further, carry)
        return plus(state, carry)

    def through(state, flows, p, upward):
        block_step = power_of(7, p)
        listing = [state]
        flows = flows if upward else flows[::-1]
        for flow in flows[:-1]:
            state = plus(times(state, block_step), flow)
            listing.append(state)
        listing = listing if upward else listing[::-1]
        return over(*(beside(*state) for state in listing))

    def read_notes():
        wait_for(many(s.note_in), s.note_sem.at[1])
        notes = s.note_in[...].reshape(members, BLOCK)
        member_lane = lax.broadcasted_iota(jnp.int32, (members, BLOCK), 1)
        member_place = lax.rem(lax.broadcasted_iota(jnp.int32, (members, BLOCK), 0), local)
        start = (half * local + member_place) * span + member_lane
        for m in range(count):
            length = jnp.sum(jnp.where(member_lane == m, notes, 0.0), axis=1, keepdims=True)
            for q in range(blocks):
                first = (q * count + m) * members
                within = ((start + q * BLOCK).astype(F32) < length).astype(F32)
                s.mask[first : first + members] = beside(within, within)

    carry_lane = lax.broadcasted_iota(jnp.int32, (count * groups, BLOCK), 1)

    def pick_last(p, c, k, total, out, scales, first):
        lines = []
        for i in range(2):
            s.widen[p, i] = total[i]
            lines.append(s.widen[p, i, pl.ds(first, count * groups, stride=local), :])
        top = jnp.max(jnp.maximum(jnp.abs(lines[0]), jnp.abs(lines[1])), axis=1, keepdims=True)
        top = jnp.maximum(top, 1e-30)
        factor = STEPS / top
        out[p] = jnp.round(over(lines[0] * factor, lines[1] * factor)).astype(I16)
        scales[k] = jnp.where(carry_lane == c, top * (1.0 / STEPS), scales[k])

    def forward_first(k):
        for m in range(count):
            wait_for(many(s.x_in.at[k, m]), s.x_sem.at[k, m, 1])
        rows_in(s.x_in, k)

        def inflow(p, c):
            own_normed = gather_couple(c) * quantum
            drive = (own_normed * scalar_rows(0, p) + scalar_rows(1, p)) * s.mask[...]
            s.own_normed[p] = own_normed
            s.drive[p] = drive
            s.inflow[p] = product(two(drive), s.down[p])

        over_couples(k, inflow)

        s.carry_scale_out[k] = jnp.zeros((count * groups, BLOCK), F32)

        def scanned(p, c):
            state, total = scan(by_block(s.inflow[p]), p, True)
            s.entering[p, :half_rows] = beside(*state)
            pick_last(p, c, k, total, s.carry_out, s.carry_scale_out, local - 1)

        over_couples(k, scanned)
        rows = pl.ds(k * couples, couples)

        @pl.when(half == 0)
        def _():
            send(s.carry_out.at[rows], s.carry_in.at[rows], s.carry_sem.at[k, 0], partner)
            send(s.carry_scale_out.at[k], s.carry_scale_in.at[k], s.carry_sem.at[k, 1], partner)

    def forward_local(k):
        def nearby(p, c):
            drive = s.drive[p]
            s.response[p] = product(two(drive), s.toeplitz[p]) + scalar_rows(2, p) * drive

        over_couples(k, nearby)

    def share_below(response):
        return 0.5 * (1.0 + lax.erf(response * math.sqrt(0.5)))

    def slopes(p, c):
        response = s.response[p]
        density = jnp.exp(-0.5 * response * response) * (1.0 / math.sqrt(2.0 * math.pi))
        s.slope[p] = share_below(response) + response * density

    def forward_second(k):
        rows = pl.ds(k * couples, couples)

        @pl.when(half == 0)
        def _():
            s.carry_in[rows] = jnp.zeros((couples, 2 * count * groups, BLOCK), I16)
            s.carry_scale_in[k] = jnp.zeros((count * groups, BLOCK), F32)

        @pl.when(half == 1)
        def _():
            wait_for(s.carry_in.at[rows], s.carry_sem.at[k, 0, 1])
            wait_for(s.carry_scale_in.at[k], s.carry_sem.at[k, 1, 1])

        def complete(p, c):
            state = carried(
                split(s.entering[p, :half_rows]), s.carry_in, s.carry_scale_in, p, c, k, True
            )
            s.entering[p] = through(state, by_block(s.inflow[p]), p, True)

        over_couples(k, complete)

        def respond(p, c):
            response = s.response[p] + product(two(s.entering[p]), s.up[p], TURNED)
            s.response[p] = response
            put_couple(c, response * share_below(response))

        over_couples(k, respond)
        rows_out(s.a_out, k)
        for m in range(count):
            s.a_in[m, dp, k, pl.ds(here, 1)] = s.a_out[k, m, pl.ds(me, 1)]
            to_holders(s.a_out.at[k, m], s.a_in.at[m, :, k], s.a_sem.at[k, m])

    read_notes()
    over_couples(0, lambda p, c: tables_middle(p))
    weight_wait(0)
    weight_hop(1)
    over_couples(1, lambda p, c: tables_middle(p))
    for k in range(HALVES):
        forward_first(k)
    for k in range(HALVES):
        forward_local(k)
    for k in range(HALVES):
        forward_second(k)
        if k == 0:
            weight_wait(1)
            weight_hop(2)
    for k in range(HALVES):
        over_couples(k, lambda p, c: tables_second(p))

    for m in range(count):
        s.upstream[m] = out_grad[m].T
    weight_wait(2)
    for j in range(tiles):
        rows = slice(j * BLOCK, (j + 1) * BLOCK)
        per = BLOCK // own
        flat = s.weight[...].reshape(-1, own, wide + BLOCK)[j * per : (j + 1) * per].reshape(BLOCK, -1)
        s.flat[rows] = flat[:, :wide]
        s.flipped[:, rows] = flat[:, :wide].T
        shifts = flat[:, wide:].astype(F32)
        shifts = shifts + pltpu.roll(shifts, BLOCK - 2, 1) + pltpu.roll(shifts, BLOCK - 4, 1)
        for i in range(2):
            column = jnp.broadcast_to(shifts[:, i : i + 1], (BLOCK, BLOCK)).reshape(per, own, BLOCK)
            for n in range(per):
                first = ((j * per + n) * 2 + i) * own
                s.shift[first : first + own] = column[n]

    def project(m):
        for k in range(HALVES):
            ref = s.a_out.at[k, m, pl.ds(0, members - 1)]
            wait_for(ref, s.a_sem.at[k, m, 1])
        activated = s.a_in[m].reshape(width, span)
        valid = s.valid[m : m + 1]
        lanes = slice(m * span, (m + 1) * span)
        s.pre[...] = dot(s.flipped[...], activated)
        for j in range(tiles):
            rows = slice(j * BLOCK, (j + 1) * BLOCK)
            gates = slice(width + j * BLOCK, width + (j + 1) * BLOCK)
            value = s.pre[rows] + beside(*[s.shift[rows]] * blocks)
            gate = jax.nn.sigmoid(s.pre[gates] + beside(*[s.shift[gates]] * blocks))
            gated = s.upstream[m, rows].astype(F32) * valid
            s.pre_grad[rows, lanes] = (gated * gate).astype(BF16)
            s.pre_grad[gates, lanes] = (gated * value * gate * (1.0 - gate)).astype(BF16)
            s.result[m, rows] = (s.tokens[m, rows].astype(F32) + value * gate * valid).astype(BF16)
        s.act_grad[...] = dot(s.flat[...], s.pre_grad[:, lanes])
        largest = jnp.zeros((1, 1), F32)
        for j in range(tiles):
            piece = s.act_grad[j * BLOCK : (j + 1) * BLOCK]
            largest = jnp.maximum(largest, jnp.max(jnp.abs(piece), axis=(0, 1), keepdims=True))
        largest = jnp.maximum(largest, 1e-30)
        s.scale_out[m] = jnp.broadcast_to(largest * (1.0 / STEPS), (1, BLOCK))
        s.scale_in[m, pl.ds(me, 1)] = s.scale_out[m][None]
        to_all(s.scale_out.at[m], s.scale_in.at[m], s.scale_sem.at[m])
        factor = STEPS / largest
        for j in range(tiles):
            coded = jnp.round(s.act_grad[j * BLOCK : (j + 1) * BLOCK] * factor).astype(I16)
            for rows, a, k, p in chunk_rows(j):
                s.g_out[k, m, a, p] = coded[rows]
        for k in range(HALVES):
            s.g_in[k, m, pl.ds(me, 1)] = s.g_out[k, m, dp, pl.ds(here, 1)]
            to_owners(s.g_out.at[k, m], s.g_in.at[k, m], s.g_sem.at[k, m])
    def weight_gradient():
        ones = jnp.ones((count * span, BLOCK), BF16)
        per = width // groups
        lane4 = lax.broadcasted_iota(jnp.int32, (zs, 2, own, BLOCK), 3)
        for j in range(groups):
            activated = beside(*(s.a_in[m, j].reshape(per, span) for m in range(count)))
            piece = dot(activated, s.pre_grad[...], TURNED).reshape(zs, 2, own, wide)
            sums = dot(s.pre_grad[2 * j * per : 2 * (j + 1) * per], ones).reshape(zs, 2, 2, own, BLOCK)
            sums = jnp.where(lane4 == 0, sums[:, :, 0], jnp.where(lane4 == 1, sums[:, :, 1], 0.0))
            s.total[j, :, :, :, :wide] = piece
            s.total[j, :, :, :, wide:] = sums

    for m in range(count):
        project(m)
    weight_gradient()

    def sum_hop(hop):
        sems = s.sum_sem
        if hop == 0:
            send(s.total.at[:, :, 1 - core], s.sum_core, sems.at[0], (dp, z * 2 + 1 - core))
        elif hop == "ready":
            wait_for(s.sum_core, sems.at[0, 0])
            wait_for(s.sum_core, sems.at[0, 1])
            for j in range(groups):
                part = s.total[j, :, pl.ds(core, 1)].reshape(zs, own, -1) + s.sum_core[j]
                s.sum_core[j] = part
                s.sum_dp_out[j] = part.astype(BF16)
        elif hop == 1:
            for k in range(1, groups):
                there = lax.rem(dp + k, groups)
                send(s.sum_dp_out.at[there], s.sum_dp_in.at[dp], sems.at[1], (there, seq))
        elif hop == 2:
            ref = s.sum_dp_in.at[pl.ds(0, groups - 1)]
            wait_for(ref, sems.at[1, 0])
            wait_for(ref, sems.at[1, 1])
            part = s.sum_core[dp]
            for k in range(1, groups):
                part += s.sum_dp_in[lax.rem(dp + k, groups)].astype(F32)
            s.sum_core[0] = part
            s.sum_z_out[...] = part.astype(BF16)
            for k in range(1, zs):
                there = lax.rem(z + k, zs)
                send(s.sum_z_out.at[there], s.sum_z_in.at[z], sems.at[2], (dp, there * 2 + core))
        else:
            ref = s.sum_z_in.at[pl.ds(0, zs - 1)]
            wait_for(ref, sems.at[2, 0])
            wait_for(ref, sems.at[2, 1])
            part = s.sum_core[0, pl.ds(z, 1)].reshape(own, -1)
            for k in range(1, zs):
                part += s.sum_z_in[lax.rem(z + k, zs)].astype(F32)
            rows_grad[...] = part[:, :wide]
            columns = part[:, wide:].T
            shift_grad[...] = beside(columns[:1], columns[1:2])

    sum_hop(0)
    for k in range(HALVES):
        over_couples(k, slopes)
    sum_hop("ready")
    for m in range(count):
        result[m] = s.result[m].T

    def backward_first(k):
        for m in range(count):
            wait_for(many(s.g_in.at[k, m]), s.g_sem.at[k, m, 1])
            if k == 0:
                wait_for(many(s.scale_in.at[m]), s.scale_sem.at[m, 1])
                scale = s.scale_in[m].reshape(members, BLOCK)
                for q in range(blocks):
                    first = (q * count + m) * members
                    s.scales[first : first + members] = beside(scale, scale)
        if k == 0:
            sum_hop(1)
        rows_in(s.g_in, k)

        def outflow(p, c):
            grad = gather_couple(c) * s.scales[...] * s.slope[p]
            s.grad[p] = grad
            s.outflow[p] = product(two(grad), s.base[p])

        over_couples(k, outflow)

        s.back_scale_out[k] = jnp.zeros((count * groups, BLOCK), F32)

        def scanned(p, c):
            state, total = scan(by_block(s.outflow[p]), p, False)
            s.leaving[p, full_rows - half_rows :] = beside(*state)
            pick_last(p, c, k, total, s.back_out, s.back_scale_out, 0)

        over_couples(k, scanned)
        rows = pl.ds(k * couples, couples)

        @pl.when(half == 1)
        def _():
            send(s.back_out.at[rows], s.back_in.at[rows], s.back_sem.at[k, 0], partner)
            send(s.back_scale_out.at[k], s.back_scale_in.at[k], s.back_sem.at[k, 1], partner)

    def backward_local(k):
        def nearby(p, c):
            grad = s.grad[p]
            s.response[p] = product(two(grad), s.toeplitz[p], TURNED) + scalar_rows(2, p) * grad

        over_couples(k, nearby)

    def backward_second(k):
        rows = pl.ds(k * couples, couples)

        @pl.when(half == 1)
        def _():
            s.back_in[rows] = jnp.zeros((couples, 2 * count * groups, BLOCK), I16)
            s.back_scale_in[k] = jnp.zeros((count * groups, BLOCK), F32)

        @pl.when(half == 0)
        def _():
            wait_for(s.back_in.at[rows], s.back_sem.at[k, 0, 1])
            wait_for(s.back_scale_in.at[k], s.back_sem.at[k, 1, 1])

        def complete(p, c):
            state = carried(
                split(s.leaving[p, full_rows - half_rows :]), s.back_in, s.back_scale_in, p, c, k, False
            )
            s.leaving[p] = through(state, by_block(s.outflow[p]), p, False)

        over_couples(k, complete)

        def respond(p, c):
            grad = s.grad[p]
            drive_grad = s.response[p] + product(two(s.leaving[p]), s.back[p], TURNED)
            norm_grad = drive_grad * s.mask[...]
            for i, value in enumerate((norm_grad * s.own_normed[p], norm_grad, grad * s.drive[p])):
                for side, line in enumerate(split(total_rows(value))):
                    s.part[k, pl.ds(5 * couples + i * own + 2 * c + side, 1), :] = line
            put_couple(c, norm_grad * scalar_rows(0, p))

        over_couples(k, respond)
        rows_out(s.d_out, k)
        for m in range(count):
            s.d_in[m, dp, k, pl.ds(here, 1)] = s.d_out[k, m, pl.ds(me, 1)]
            to_holders(s.d_out.at[k, m], s.d_in.at[m, :, k], s.d_sem.at[k, m])

    for k in range(HALVES):
        backward_first(k)
    for k in range(HALVES):
        backward_local(k)
    for k in range(HALVES):
        backward_second(k)
    sum_hop(2)

    def sum_of_products(first, second):
        (a, b), (c, d) = (split(first), split(second))
        return (total_rows(a * c - b * d), total_rows(a * d + b * c))

    def lag_sums(p, c):
        drive, grad = (two(s.drive[p]), two(s.grad[p]))
        lines = []
        for side in range(2):
            lanes = slice(side * BLOCK, (side + 1) * BLOCK)
            left = over(drive[0][:, lanes], drive[1][:, lanes], drive[0][:, lanes])
            right = over(grad[0][:, lanes], grad[0][:, lanes], grad[1][:, lanes])
            cross = jnp.where(lane_id >= row_id, dot(left, right, SIDEWAYS), 0.0)
            lags = cross[:8]
            for i in range(1, BLOCK // 8):
                lags = lags + pltpu.roll(cross[8 * i : 8 * i + 8], BLOCK - 8 * i, 1)
            for bit in range(3):
                moved = pltpu.roll(lags, BLOCK - (1 << bit), 1)
                lags = jnp.where((row_id[:8] >> bit) & 1 == 1, moved, lags)
            lines.append(total_rows(lags))
        later = [jnp.where(row_lane < BLOCK - 1, pltpu.roll(line, BLOCK - 1, 1), 0.0) for line in lines]
        eight = lax.broadcasted_iota(jnp.int32, (8, 2 * BLOCK), 0)
        near = jnp.where(eight == 0, beside(*(line * shrink for line in lines)), beside(*later))
        s.lags[p] = near

    def correlate(p, c):
        drive, grad, near = (two(s.drive[p]), two(s.grad[p]), two(s.lags[p]))
        entering, leaving = (s.entering[p], s.leaving[p])
        second = folded(over(*drive), s.down_ramp[p])
        third = dot(over(*grad, *near), s.base_ramp[p])
        near = third[2 * full_rows : 2 * full_rows + 8] + third[2 * full_rows + 8 :]
        third = third[:full_rows] + third[full_rows : 2 * full_rows]
        moment = times(sum_of_products(entering, s.outflow[p]), power_of(0, p))
        moment = plus(moment, split(near[:1]))
        paired = times(sum_of_products(leaving, entering), power_of(7, p))
        paired = (paired[0] * float(BLOCK), paired[1] * float(BLOCK))
        paired = plus(paired, plus(sum_of_products(leaving, second), sum_of_products(entering, third)))
        paired = plus(paired, split(near[1:2]))
        for i, line in enumerate(moment + paired):
            s.sums[i, pl.ds(p, 1), :] = line

    shrink = 1.0 / (row_lane.astype(F32) + 1.0)
    def parameters(k):
        over_couples(k, lag_sums)
        over_couples(k, correlate)
        rows = pl.ds(pl.multiple_of(k * couples, couples), couples)
        moment, paired = ((s.sums[0, rows], s.sums[1, rows]), (s.sums[2, rows], s.sums[3, rows]))
        paired = times(paired, (s.coeff[0, rows], s.coeff[1, rows]))
        _, pull = jax.vjp(coefficient_parts, *(s.raw[i, rows] for i in range(5)))
        for i, grad in enumerate(pull((paired[0], -paired[1], moment[0], -moment[1]))):
            s.part[pl.ds(k, 1), i * couples : (i + 1) * couples] = grad[None]

    parameters(other)
    send(s.part.at[other], s.part_in, s.part_sem, partner)
    parameters(half)

    def norm_backward(m):
        for k in range(HALVES):
            wait_for(s.d_out.at[k, m, pl.ds(0, members - 1)], s.d_sem.at[k, m, 1])
        inverse = s.inverse[m : m + 1]
        scaled = s.d_in[m].reshape(width, span)
        plain = jnp.zeros((1, span), F32)
        along = jnp.zeros((1, span), F32)
        for j in range(tiles):
            rows = slice(j * BLOCK, (j + 1) * BLOCK)
            piece = scaled[rows].astype(F32)
            plain += total_rows(piece)
            along += total_rows(piece * s.normed[m, rows])
        plain, along = (plain * (1.0 / width), along * (1.0 / width))
        for j in range(tiles):
            rows = slice(j * BLOCK, (j + 1) * BLOCK)
            piece = scaled[rows].astype(F32) - plain - s.normed[m, rows] * along
            piece = s.upstream[m, rows].astype(F32) + inverse * piece
            token_grad[m, :, rows] = piece.astype(BF16).T

    for m in range(count):
        norm_backward(m)

    wait_for(s.part_in, s.part_sem.at[0])
    wait_for(s.part_in, s.part_sem.at[1])
    mine = s.part[half] + s.part_in[...]
    grads = [mine[i * couples : (i + 1) * couples] for i in range(5)]

    def uncoupled(value):
        s.turn[pl.ds(0, couples, stride=2), :] = value
        s.turn[pl.ds(1, couples, stride=2), :] = pltpu.roll(value, states, 1)
        return s.turn[...]

    rate_grad[...] = uncoupled(grads[0])[:, :states]
    turn_grad[...] = uncoupled(grads[1])[:, :states]
    mix_low = own_lane < states
    mix_re = uncoupled(grads[3])
    mixing_grad[...] = jnp.where(mix_low, mix_re, pltpu.roll(uncoupled(grads[4]), states, 1))
    lines = [jnp.where(mix_low, uncoupled(grads[2]), 0.0)]
    lines += [mine[5 * couples + i * own : 5 * couples + (i + 1) * own] for i in range(3)]
    ones = jnp.ones((8, BLOCK), F32)
    for rows, out in zip(lines, (spacing_grad, gain_grad, bias_grad, skip_grad), strict=True):
        line = lax.dot_general(ones, rows, (TURNED, ((), ())), preferred_element_type=F32, precision=HIGH)
        out[...] = line[:1]

    sum_hop(3)

    wait_for(many(s.note_in), s.note_sem.at[0])
    for m in range(count):
        wait_for(many(s.scale_in.at[m]), s.scale_sem.at[m, 0])
        for k in range(HALVES):
            wait_for(many(s.x_in.at[k, m]), s.x_sem.at[k, m, 0])
            wait_for(many(s.a_out.at[k, m]), s.a_sem.at[k, m, 0])
            wait_for(many(s.g_in.at[k, m]), s.g_sem.at[k, m, 0])
            wait_for(many(s.d_out.at[k, m]), s.d_sem.at[k, m, 0])
    for k in range(HALVES):
        rows = pl.ds(k * couples, couples)

        @pl.when(half == 0)
        def _():
            wait_for(s.carry_out.at[rows], s.carry_sem.at[k, 0, 0])
            wait_for(s.carry_scale_out.at[k], s.carry_sem.at[k, 1, 0])

        @pl.when(half == 1)
        def _():
            wait_for(s.back_out.at[rows], s.back_sem.at[k, 0, 0])
            wait_for(s.back_scale_out.at[k], s.back_sem.at[k, 1, 0])


class Scratch:
    def __init__(self, names, refs):
        for name, ref in zip(names, refs, strict=True):
            setattr(self, name, ref)


def scratch_of(size, states):
    groups, parts, own, width, span, count = size
    local, blocks, zs = (parts // HALVES, span // BLOCK, parts // 2)
    members, couples = (groups * local, own // 2)
    every = HALVES * couples
    rows = blocks * count * members
    bits = 7 + (blocks * local).bit_length()
    wide = 2 * width + BLOCK
    vmem, sems = (pltpu.VMEM, pltpu.SemaphoreType.DMA)
    by_holder = (HALVES, count, groups, local, own, span)
    by_owner = (HALVES, count, members, own, span)
    filed = (count, groups, HALVES, local, own, span)
    chunk_sems = sems((HALVES, count, 2))
    held = vmem((every, rows, 2 * BLOCK), F32)
    table, plain = (vmem((every, 2, 2 * BLOCK, 2 * BLOCK), BF16), vmem((every, 2 * BLOCK, 2 * BLOCK), BF16))
    kept = vmem((every, BLOCK, 2 * BLOCK), F32)
    carry, carry_sems = (vmem((every, 2 * count * groups, BLOCK), I16), sems((HALVES, 2, 2)))
    carry_scale = vmem((HALVES, count * groups, BLOCK), F32)
    part_rows = 5 * couples + 3 * own
    return {
        "tokens": vmem((count, width, span), BF16),
        "upstream": vmem((count, width, span), BF16),
        "result": vmem((count, width, span), BF16),
        "normed": vmem((count, width, span), F32),
        "inverse": vmem((count, span), F32),
        "valid": vmem((count, span), F32),
        "x_out": vmem(by_holder, I16), "x_in": vmem(by_owner, I16), "x_sem": chunk_sems,
        "a_out": vmem(by_owner, BF16), "a_in": vmem(filed, BF16), "a_sem": chunk_sems,
        "g_out": vmem(by_holder, I16), "g_in": vmem(by_owner, I16), "g_sem": chunk_sems,
        "d_out": vmem(by_owner, BF16), "d_in": vmem(filed, BF16), "d_sem": chunk_sems,
        "note_out": vmem((1, 1, BLOCK), F32), "note_in": vmem((members, 1, BLOCK), F32), "note_sem": sems((2,)),
        "scale_out": vmem((count, 1, BLOCK), F32), "scale_in": vmem((count, members, 1, BLOCK), F32),
        "scale_sem": sems((count, 2)),
        "scales": vmem((rows, 2 * BLOCK), F32),
        "params": vmem((HALVES, own, 3 * BLOCK), F32), "params_sem": sems((2,)),
        "weight_out": vmem((own, wide), BF16),
        "weight": vmem((groups, zs, 2, own, wide), BF16), "weight_sem": sems((3, 2)),
        "flat": vmem((width, 2 * width), BF16),
        "flipped": vmem((2 * width, width), BF16),
        "shift": vmem((2 * width, BLOCK), F32),
        "pre_grad": vmem((2 * width, count * span), BF16),
        "pre": vmem((2 * width, span), F32),
        "act_grad": vmem((width, span), F32),
        "total": vmem((groups, zs, 2, own, wide), F32),
        "sum_core": vmem((groups, zs, own, wide), F32),
        "sum_dp_out": vmem((groups, zs, own, wide), BF16),
        "sum_dp_in": vmem((groups, zs, own, wide), BF16),
        "sum_z_out": vmem((zs, own, wide), BF16),
        "sum_z_in": vmem((zs, own, wide), BF16),
        "sum_sem": sems((3, 2)),
        "turn": vmem((own, BLOCK), F32),
        "scalars": vmem((3, HALVES * own, BLOCK), F32),
        "power": vmem((bits, 2, every, BLOCK), F32),
        "lead": vmem((2, every, BLOCK), F32),
        "coeff": vmem((2, every, BLOCK), F32),
        "base": table, "down": table, "up": table, "back": table, "toeplitz": table,
        "base_ramp": plain, "down_ramp": plain, "base_kept": kept, "down_kept": kept, "response": held,
        "stage_in": vmem((blocks, count, members * own, BLOCK), F32),
        "stage_out": vmem((blocks, count, members * own, BLOCK), F32),
        "mask": vmem((rows, 2 * BLOCK), F32),
        "own_normed": held, "drive": held, "entering": held, "slope": held, "inflow": held,
        "grad": held, "outflow": held, "leaving": held,
        "widen": vmem((every, 2, count * members, BLOCK), F32),
        "carry_out": carry, "carry_in": carry, "carry_sem": carry_sems,
        "back_out": carry, "back_in": carry, "back_sem": carry_sems,
        "carry_scale_out": carry_scale, "carry_scale_in": carry_scale,
        "back_scale_out": carry_scale, "back_scale_in": carry_scale,
        "sums": vmem((4, every, BLOCK), F32),
        "raw": vmem((5, every, BLOCK), F32), "lags": vmem((every, 8, 2 * BLOCK), F32),
        "part": vmem((HALVES, part_rows, BLOCK), F32), "part_in": vmem((part_rows, BLOCK), F32),
        "part_sem": sems((2,)),
    }


def handed_over(values):
    def kernel(*refs):
        for given, out in zip(refs[: len(values)], refs[len(values) :], strict=True):
            out[...] = given[...].reshape(out.shape)

    shapes = [(value.size,) if value.shape[0] == 1 else value.shape for value in values]
    return pl.pallas_call(
        kernel,
        out_shape=[jax.ShapeDtypeStruct(shape, value.dtype) for shape, value in zip(shapes, values, strict=True)],
        in_specs=[pl.BlockSpec(memory_space=pltpu.VMEM)] * len(values),
        out_specs=[pl.BlockSpec(memory_space=pltpu.VMEM)] * len(values),
    )(*values)


def in_one_kernel(groups, parts, *args):
    inputs, lengths, ln_gain, ln_bias, lam_log, lam_im, log_dt, mix_weight, skip, glu_weight, glu_bias, out_grad = args
    count, span, width = inputs.shape
    own = ln_gain.shape[0]
    size = (groups, parts, own, width, span, count)
    scratch = scratch_of(size, lam_log.shape[1])

    def kernel(*refs):
        arguments, results, kept = (refs[:12], refs[12:23], refs[23:])
        whole_kernel(size, *arguments, *results, Scratch(scratch, kept))

    vmem, smem = (pl.BlockSpec(memory_space=pltpu.VMEM), pl.BlockSpec(memory_space=pltpu.SMEM))
    line = jax.ShapeDtypeStruct((1, own), F32)
    outs = pl.pallas_call(
        kernel,
        out_shape=(
            jax.ShapeDtypeStruct(inputs.shape, BF16),
            jax.ShapeDtypeStruct(inputs.shape, BF16),
            line,
            line,
            jax.ShapeDtypeStruct(lam_log.shape, F32),
            jax.ShapeDtypeStruct(lam_im.shape, F32),
            line,
            jax.ShapeDtypeStruct(mix_weight.shape, F32),
            line,
            jax.ShapeDtypeStruct(glu_weight.shape, F32),
            jax.ShapeDtypeStruct((1, 2 * own), F32),
        ),
        in_specs=[vmem, smem, smem, smem, vmem, vmem, smem, vmem, smem, vmem, smem, vmem],
        out_specs=[vmem] * 11,
        scratch_shapes=list(scratch.values()),
        compiler_params=pltpu.CompilerParams(
            collective_id=0, has_side_effects=True, vmem_limit_bytes=62 * 1024 * 1024
        ),
    )(*args)
    return tuple(handed_over(outs))


def solution(mesh):
    tokens, vector, matrix = (P("dp", "seq", None), P(BOTH), P(BOTH, None))
    groups, parts = (mesh.shape["dp"], mesh.shape["seq"])

    def step(*args):
        own = args[2].shape[0]
        if own % 16 == 0 and parts % 4 == 0:
            return in_one_kernel(groups, parts, *args)
        return per_device(*args)

    return jax.shard_map(
        step,
        mesh=mesh,
        in_specs=(
            tokens, P("dp"), vector, vector, matrix, matrix, vector, matrix, vector, matrix, vector, tokens,
        ),
        out_specs=(
            tokens, tokens, vector, vector, matrix, matrix, vector, matrix, vector, matrix, vector,
        ),
        check_vma=False,
    )
```

```python
import math
from functools import partial

import jax
import jax.numpy as jnp
from jax import lax
from jax.experimental import pallas as pl
from jax.experimental.pallas import tpu as pltpu
from jax.sharding import PartitionSpec as P

BLOCK = 128
EPS = 1e-05
HIGH = lax.Precision.HIGHEST
BOTH = ("dp", "seq")


def halves(packed):
    count = packed.shape[-1] // 2
    return (packed[..., :count], packed[..., count:])


def cmul(first, second):
    first_re, first_im = halves(first)
    second_re, second_im = halves(second)
    return jnp.concatenate(
        [first_re * second_re - first_im * second_im, first_re * second_im + first_im * second_re],
        axis=-1,
    )


def conjugate(packed):
    real_half, imag_half = halves(packed)
    return jnp.concatenate([real_half, -imag_half], axis=-1)


def coefficients(lam_log, lam_im, log_dt, mix_weight):
    spacing = jnp.exp(log_dt)[:, None]
    rate = jnp.exp(lam_log)
    shrink = -rate * spacing
    angle = lam_im * spacing
    scale = jnp.exp(shrink)
    decay = jnp.concatenate([scale * jnp.cos(angle), scale * jnp.sin(angle)], axis=-1)
    less_re = jnp.expm1(shrink) * jnp.cos(angle) - 2.0 * jnp.sin(0.5 * angle) ** 2
    less_im = scale * jnp.sin(angle)
    modulus = rate * rate + lam_im * lam_im
    ratio = jnp.concatenate(
        [
            (lam_im * less_im - rate * less_re) / modulus,
            -(rate * less_im + lam_im * less_re) / modulus,
        ],
        axis=-1,
    )
    return (decay, cmul(mix_weight, ratio))


def powers(decay):
    real_half, imag_half = halves(decay)
    table = jnp.concatenate([jnp.ones_like(real_half), jnp.zeros_like(imag_half)], axis=-1)[:, None]
    step = decay[:, None]
    while table.shape[1] < BLOCK:
        table = jnp.concatenate([table, cmul(step, table)], axis=1)
        step = cmul(step, step)
    return (table, step[:, 0])


def link(earlier, later):
    return (cmul(earlier[0], later[0]), cmul(later[0], earlier[1]) + later[1])


def shifted(pieces, step, back):
    leads = jnp.broadcast_to(step[:, None, None], pieces.shape)
    _, reach = lax.associative_scan(link, (leads, pieces), axis=2, reverse=back)
    none = jnp.zeros_like(reach[:, :, :1])
    if back:
        return jnp.concatenate([reach[:, :, 1:], none], axis=2)
    return jnp.concatenate([none, reach[:, :, :-1]], axis=2)


def to_owner(rows):
    count, span, width = rows.shape
    groups, parts = (lax.axis_size("dp"), lax.axis_size("seq"))
    own = width // (groups * parts)
    sent = rows.reshape(count * span, width).T.reshape(-1, own, count, span)
    held = lax.all_to_all(sent, BOTH, 0, 0, tiled=True).reshape(groups, parts, own, count, span)
    held = held.transpose(2, 0, 3, 1, 4).reshape(own, groups * count, -1, BLOCK)
    return held


def to_holder(held, count, span):
    groups, parts = (lax.axis_size("dp"), lax.axis_size("seq"))
    own = held.shape[0]
    sent = held.astype(jnp.bfloat16).reshape(own, groups, count, parts, span).transpose(1, 3, 0, 2, 4)
    sent = sent.reshape(groups * parts, own, count, span)
    rows = lax.all_to_all(sent, BOTH, 0, 0, tiled=True)
    return rows.reshape(-1, count * span).T.reshape(count, span, -1).astype(jnp.float32)


def per_device(
    inputs,
    lengths,
    ln_gain,
    ln_bias,
    lam_log,
    lam_im,
    log_dt,
    mix_weight,
    skip,
    glu_weight,
    glu_bias,
    out_grad,
):
    count, span, width = inputs.shape
    offset = lax.axis_index("seq") * span
    positions = offset + jnp.arange(span, dtype=jnp.int32)
    valid = (positions[None, :] < lengths[:, None]).astype(jnp.float32)[..., None]
    rows = lax.all_gather(glu_weight, BOTH, axis=0, tiled=True)
    shift = lax.all_gather(glu_bias, BOTH, axis=0, tiled=True)
    spans = lax.all_gather(lengths, "dp", axis=0, tiled=True)
    whole_span = span * lax.axis_size("seq")
    mask = (jnp.arange(whole_span, dtype=jnp.int32)[None] < spans[:, None]).astype(jnp.float32)
    mask = mask.reshape(1, -1, whole_span // BLOCK, BLOCK)

    tokens = inputs.astype(jnp.float32)
    mean = jnp.mean(tokens, axis=-1, keepdims=True)
    centered = tokens - mean
    inverse = lax.rsqrt(jnp.mean(centered * centered, axis=-1, keepdims=True) + EPS)
    normed = centered * inverse

    (decay, coeff), coeff_pull = jax.vjp(coefficients, lam_log, lam_im, log_dt, mix_weight)
    base, whole = powers(decay)
    down = base[:, ::-1]
    real_half, imag_half = halves(coeff)
    kernel = jnp.einsum("cz,ckz->ck", conjugate(coeff), base, precision=HIGH)
    lead = cmul(coeff, decay)[:, None]
    up = conjugate(cmul(lead, base))
    back = conjugate(cmul(lead, down))
    steps = jnp.arange(BLOCK)
    lag = steps[:, None] - steps[None, :]
    toeplitz = jnp.where(lag >= 0, kernel[:, jnp.maximum(lag, 0)], 0.0)
    ramp = steps.astype(jnp.float32)[:, None]

    gain, bias, skipping = (p[:, None, None, None] for p in (ln_gain, ln_bias, skip))
    own_normed = to_owner(normed)
    drive = (own_normed * gain + bias) * mask
    entering = shifted(jnp.einsum("cbqj,cjz->cbqz", drive, down, precision=HIGH), whole, False)
    response = jnp.einsum("cij,cbqj->cbqi", toeplitz, drive, precision=HIGH)
    response += jnp.einsum("ciz,cbqz->cbqi", up, entering, precision=HIGH) + skipping * drive
    activated, gelu_pull = jax.vjp(partial(jax.nn.gelu, approximate=False), response)
    activated = to_holder(activated, count, span).astype(jnp.bfloat16).reshape(-1, width)
    pre = jnp.dot(activated, rows, preferred_element_type=jnp.float32) + shift
    gate = jax.nn.sigmoid(pre[:, width:])
    flat_valid = valid.reshape(-1, 1)
    result = (tokens + (pre[:, :width] * gate * flat_valid).reshape(tokens.shape)).astype(jnp.bfloat16)
    upstream = out_grad.astype(jnp.float32)
    gated = upstream.reshape(-1, width) * flat_valid
    pre_grad = jnp.concatenate(
        [gated * gate, gated * pre[:, :width] * gate * (1.0 - gate)], axis=-1
    ).astype(jnp.bfloat16)
    rows_grad = lax.dot_general(
        activated, pre_grad, (((0,), (0,)), ((), ())), preferred_element_type=jnp.float32
    )
    shift_grad = jnp.sum(pre_grad.astype(jnp.float32), axis=0)
    act_grad = lax.dot_general(
        pre_grad, rows, (((1,), (1,)), ((), ())), preferred_element_type=jnp.float32
    )
    response_grad = gelu_pull(to_owner(act_grad.reshape(tokens.shape)))[0]

    skip_grad = jnp.sum(response_grad * drive, axis=(1, 2, 3))
    outflow = jnp.einsum("cbqt,ctz->cbqz", response_grad, base, precision=HIGH)
    leaving = shifted(outflow, whole, True)
    drive_grad = jnp.einsum("cij,cbqi->cbqj", toeplitz, response_grad, precision=HIGH)
    drive_grad += jnp.einsum("cjz,cbqz->cbqj", back, leaving, precision=HIGH) + skipping * response_grad
    norm_grad = drive_grad * mask
    gain_grad = jnp.sum(norm_grad * own_normed, axis=(1, 2, 3))
    bias_grad = jnp.sum(norm_grad, axis=(1, 2, 3))
    scaled = to_holder(norm_grad * gain, count, span)
    token_grad = upstream + inverse * (
        scaled
        - jnp.mean(scaled, axis=-1, keepdims=True)
        - normed * jnp.mean(scaled * normed, axis=-1, keepdims=True)
    )

    cross = jnp.einsum("cbqj,cbqi->cij", drive, response_grad, precision=HIGH)
    lags = jnp.stack([jnp.trace(cross, offset=-k, axis1=1, axis2=2) for k in range(BLOCK)], axis=-1)
    second = jnp.einsum("cbqj,cjz->cbqz", drive, down * ramp[::-1], precision=HIGH)
    third = jnp.einsum("cbqt,ctz->cbqz", response_grad, base * (ramp + 1.0), precision=HIGH)
    total = partial(jnp.sum, axis=(1, 2))
    moment = cmul(decay, total(cmul(entering, outflow))) + jnp.einsum("ck,ckz->cz", lags, base, precision=HIGH)
    before = jnp.concatenate([jnp.zeros_like(base[:, :1]), base[:, :-1]], axis=1) * ramp
    paired = BLOCK * cmul(whole, total(cmul(leaving, entering)))
    paired += total(cmul(leaving, second) + cmul(entering, third))
    paired = cmul(coeff, paired + jnp.einsum("ck,ckz->cz", lags, before, precision=HIGH))
    rate_grad, turn_grad, spacing_grad, mixing_grad = coeff_pull((conjugate(paired), conjugate(moment)))

    scatter = partial(lax.psum_scatter, axis_name=BOTH, scatter_dimension=0, tiled=True)
    return (
        result,
        token_grad.astype(jnp.bfloat16),
        gain_grad,
        bias_grad,
        rate_grad,
        turn_grad,
        spacing_grad,
        mixing_grad,
        skip_grad,
        scatter(rows_grad),
        scatter(shift_grad),
    )


MESH = pl.DeviceIdType.MESH
F32, BF16, I16 = (jnp.float32, jnp.bfloat16, jnp.int16)
STEPS = 32700.0
GROUP = 4
HALVES = 2


def two(value):
    high = value.astype(BF16)
    return (high, (value - high.astype(F32)).astype(BF16))


def dot(left, right, dims=((1,), (0,))):
    return lax.dot_general(left, right, (dims, ((), ())), preferred_element_type=F32)


TURNED = ((1,), (1,))
SIDEWAYS = ((0,), (0,))


def product(left, table, dims=((1,), (0,))):
    return folded(over(*left), table[0], dims) + dot(left[0], table[1], dims)


def folded(rows, table, dims=((1,), (0,))):
    value = dot(rows, table, dims)
    half = value.shape[0] // 2
    return value[:half] + value[half:]


def times(value, factor):
    return (value[0] * factor[0] - value[1] * factor[1], value[0] * factor[1] + value[1] * factor[0])


def plus(first, second):
    return (first[0] + second[0], first[1] + second[1])


def choose(condition, first, second):
    return (jnp.where(condition, first[0], second[0]), jnp.where(condition, first[1], second[1]))


def split(value):
    return (value[:, :BLOCK], value[:, BLOCK:])


def beside(*parts):
    return jnp.concatenate(parts, axis=1)


def over(*parts):
    return jnp.concatenate(parts, axis=0)


def total_rows(value):
    return jnp.sum(value, axis=0, keepdims=True)


def small_expm1(value):
    near = jnp.abs(value) < 0.5
    small = jnp.where(near, value, 0.0)
    series = jnp.ones_like(small)
    for order in range(10, 1, -1):
        series = 1.0 + small * (1.0 / order) * series
    return jnp.where(near, small * series, jnp.exp(value) - 1.0)


def coefficient_parts(lam_log, lam_im, log_dt, mix_re, mix_im):
    spacing, rate = (jnp.exp(log_dt), jnp.exp(lam_log))
    shrink, angle = (-rate * spacing, lam_im * spacing)
    scale = jnp.exp(shrink)
    cosine, sine, half = (jnp.cos(angle), jnp.sin(angle), jnp.sin(0.5 * angle))
    less_re = small_expm1(shrink) * cosine - 2.0 * half * half
    less_im = scale * sine
    modulus = rate * rate + lam_im * lam_im
    ratio = (
        (lam_im * less_im - rate * less_re) / modulus,
        -(rate * less_im + lam_im * less_re) / modulus,
    )
    return (scale * cosine, less_im) + times((mix_re, mix_im), ratio)


def whole_kernel(
    size,
    inputs, lengths, ln_gain, ln_bias, lam_log, lam_im, log_dt, mix_weight, skip, glu_weight, glu_bias, out_grad,
    result, token_grad, gain_grad, bias_grad, rate_grad, turn_grad, spacing_grad, mixing_grad, skip_grad,
    rows_grad, shift_grad,
    s,
):
    groups, parts, own, width, span, count = size
    local, blocks, zs = (parts // HALVES, span // BLOCK, parts // 2)
    members = groups * local
    tiles, couples, states = (width // BLOCK, own // 2, lam_log.shape[1])
    wide = 2 * width
    dp, seq = (lax.axis_index("dp"), lax.axis_index("seq"))
    core, z = (lax.rem(seq, 2), seq // 2)
    half, here = (seq // local, lax.rem(seq, local))
    other = 1 - half
    me = dp * local + here
    partner = (dp, other * local + here)

    def place(member):
        return (member // local, half * local + lax.rem(member, local))

    def send(source, target, sems, device):
        pltpu.make_async_remote_copy(
            src_ref=source, dst_ref=target, send_sem=sems.at[0], recv_sem=sems.at[1],
            device_id=device, device_id_type=MESH,
        ).start()

    def wait_for(ref, sem):
        pltpu.make_async_copy(ref, ref, sem).wait()

    def to_owners(out, into, sems):
        for k in range(1, members):
            member = lax.rem(me + k, members)
            send(out.at[member // local, lax.rem(member, local)], into.at[me], sems, place(member))

    def to_holders(out, into, sems):
        for k in range(1, members):
            member = lax.rem(me + k, members)
            send(out.at[member], into.at[dp, here], sems, place(member))

    def to_all(out, into, sems):
        for k in range(1, members):
            send(out, into.at[me], sems, place(lax.rem(me + k, members)))

    def many(ref):
        return ref.at[pl.ds(0, members - 1)]

    barrier = pltpu.get_barrier_semaphore()

    def greet(k, carry):
        member = place(lax.rem(me + k, members))
        pl.semaphore_signal(barrier, inc=1, device_id=member, device_id_type=MESH)
        return carry

    lax.fori_loop(1, members, greet, 0)
    for k in range(zs // HALVES):
        there = other * local + 2 * k + core
        pl.semaphore_signal(barrier, inc=1, device_id=(dp, there), device_id_type=MESH)

    lane = lax.broadcasted_iota(jnp.int32, (1, span), 1) + seq * span
    quantum = math.sqrt(width) / STEPS

    def chunk_rows(j):
        per = BLOCK // own
        for i in range(per):
            shard = j * per + i
            yield slice(i * own, (i + 1) * own), shard // parts, shard % parts // local, shard % local

    def norm(m):
        tokens = inputs[m].T
        s.tokens[m] = tokens
        total = jnp.zeros((1, span), F32)
        for j in range(tiles):
            total += total_rows(tokens[j * BLOCK : (j + 1) * BLOCK].astype(F32))
        mean = total * (1.0 / width)
        total = jnp.zeros((1, span), F32)
        for j in range(tiles):
            off = tokens[j * BLOCK : (j + 1) * BLOCK].astype(F32) - mean
            total += total_rows(off * off)
        inverse = lax.rsqrt(total * (1.0 / width) + EPS)
        valid = (lane < lengths[m]).astype(F32)
        s.inverse[m : m + 1] = inverse
        s.valid[m : m + 1] = valid
        for j in range(tiles):
            normed = (tokens[j * BLOCK : (j + 1) * BLOCK].astype(F32) - mean) * inverse
            s.normed[m, j * BLOCK : (j + 1) * BLOCK] = normed
            coded = jnp.round(normed * valid * (1.0 / quantum)).astype(I16)
            for rows, a, k, p in chunk_rows(j):
                s.x_out[k, m, a, p] = coded[rows]
        for k in range(HALVES):
            s.x_in[k, m, pl.ds(me, 1)] = s.x_out[k, m, dp, pl.ds(here, 1)]

    for p in range(HALVES * couples):
        for part in range(2):
            s.toeplitz[p, part, :BLOCK, BLOCK:] = jnp.zeros((BLOCK, BLOCK), BF16)
            s.toeplitz[p, part, BLOCK:, :BLOCK] = jnp.zeros((BLOCK, BLOCK), BF16)

    row_lane = lax.broadcasted_iota(jnp.int32, (1, BLOCK), 1)
    row = jnp.zeros((1, BLOCK), F32)
    for m in range(count):
        row = jnp.where(row_lane == m, lengths[m].astype(F32), row)
    s.note_out[0] = row
    s.note_in[pl.ds(me, 1)] = row[None]

    own_row = lax.broadcasted_iota(jnp.int32, (own, BLOCK), 0)
    own_lane = lax.broadcasted_iota(jnp.int32, (own, BLOCK), 1)
    scalars = jnp.zeros((own, BLOCK), F32)
    shifts = jnp.zeros((own, BLOCK), F32)
    for c in range(own):
        for i, ref in enumerate((log_dt, ln_gain, ln_bias, skip)):
            scalars = jnp.where((own_row == c) & (own_lane == i), ref[c], scalars)
        for i in range(2):
            shifts = jnp.where((own_row == c) & (own_lane % 2 == i), glu_bias[i * own + c], shifts)
    s.params[pl.ds(half, 1), :, :states] = lam_log[...][None]
    s.params[pl.ds(half, 1), :, states : 2 * states] = lam_im[...][None]
    s.params[pl.ds(half, 1), :, BLOCK : 2 * BLOCK] = mix_weight[...][None]
    s.params[pl.ds(half, 1), :, 2 * BLOCK :] = scalars[None]
    high = shifts.astype(BF16)
    rest = shifts - high.astype(F32)
    middle = rest.astype(BF16)
    lowest = (rest - middle.astype(F32)).astype(BF16)
    thirds = jnp.where(own_lane < 2, high, jnp.where(own_lane < 4, middle, lowest))
    s.weight_out[:, :wide] = glu_weight[...]
    s.weight_out[:, wide:] = thirds
    s.weight[pl.ds(dp, 1), pl.ds(z, 1), pl.ds(core, 1)] = s.weight_out[...][None, None, None]

    def weight_hop(hop):
        sems = s.weight_sem.at[hop]
        if hop == 0:
            for k in range(1, zs):
                there = lax.rem(z + k, zs)
                send(s.weight_out, s.weight.at[dp, z, core], sems, (dp, there * 2 + core))
        elif hop == 1:
            for k in range(1, groups):
                mine = s.weight.at[dp, :, core]
                send(mine, mine, sems, (lax.rem(dp + k, groups), seq))
        else:
            mine = s.weight.at[:, :, core]
            send(mine, mine, sems, (dp, z * 2 + 1 - core))

    def weight_wait(hop):
        if hop == 0:
            ref = s.weight.at[0, pl.ds(0, zs - 1), 0]
        elif hop == 1:
            ref = s.weight.at[pl.ds(0, groups - 1), :, 0]
        else:
            ref = s.weight.at[:, :, 0]
        wait_for(ref, s.weight_sem.at[hop, 0])
        wait_for(ref, s.weight_sem.at[hop, 1])

    pl.semaphore_wait(barrier, members - 1 + zs // HALVES)
    send(s.params.at[half], s.params.at[half], s.params_sem, partner)
    to_all(s.note_out.at[0], s.note_in, s.note_sem)
    weight_hop(0)
    for m in range(count):
        norm(m)
    for k in range(HALVES):
        for m in range(count):
            to_owners(s.x_out.at[k, m], s.x_in.at[k, m], s.x_sem.at[k, m])

    wait_for(s.params.at[0], s.params_sem.at[0])
    wait_for(s.params.at[0], s.params_sem.at[1])
    pair_low = lax.broadcasted_iota(jnp.int32, (couples, BLOCK), 1) < states

    def coupled(value):
        s.turn[:own] = value
        even = s.turn[pl.ds(0, couples, stride=2), :]
        odd = s.turn[pl.ds(1, couples, stride=2), :]
        return jnp.where(pair_low, even, pltpu.roll(odd, states, 1))

    def raw_params(k):
        packed = [s.params[k, :, i * BLOCK : (i + 1) * BLOCK] for i in range(3)]
        lam, mix, rest = packed
        log_step = jnp.broadcast_to(rest[:, :1], (own, BLOCK))
        return tuple(
            coupled(value)
            for value in (lam, pltpu.roll(lam, states, 1), log_step, mix, pltpu.roll(mix, states, 1))
        )

    for k in range(HALVES):
        rest = s.params[k, :, 2 * BLOCK :]
        for i in range(1, 4):
            s.scalars[i - 1, k * own : (k + 1) * own] = jnp.broadcast_to(rest[:, i : i + 1], (own, BLOCK))
        rows = slice(k * couples, (k + 1) * couples)
        for i, value in enumerate(raw_params(k)):
            s.raw[i, rows] = value
        parts_k = coefficient_parts(*(s.raw[i, rows] for i in range(5)))
        decay, coeff = (parts_k[:2], parts_k[2:])
        s.coeff[0, rows], s.coeff[1, rows] = coeff
        s.lead[0, rows], s.lead[1, rows] = times(coeff, decay)
        power = decay
        for bit in range(s.power.shape[0]):
            s.power[bit, 0, rows], s.power[bit, 1, rows] = power
            power = times(power, power)

    def power_of(bit, p):
        return (s.power[bit, 0, pl.ds(p, 1), :], s.power[bit, 1, pl.ds(p, 1), :])

    square = (BLOCK, BLOCK)
    row_id = lax.broadcasted_iota(jnp.int32, square, 0)
    lane_id = lax.broadcasted_iota(jnp.int32, square, 1)
    ramp = row_id.astype(F32)
    first_states = lax.rem(lax.broadcasted_iota(jnp.int32, (BLOCK, 2 * BLOCK), 1), BLOCK) < states

    def stacked(value):
        none = jnp.zeros_like(value)
        return over(jnp.where(first_states, value, none), jnp.where(first_states, none, value))

    def put_table(ref, p, value):
        for i, part in enumerate(two(beside(*value))):
            ref[p, i] = stacked(part)

    def tables_first(p):
        eight = row_id[:8]
        unit = (jnp.ones((8, BLOCK), F32), jnp.zeros((8, BLOCK), F32))
        base, down = (unit, unit)
        for bit in range(3):
            step = power_of(bit, p)
            base = choose((eight >> bit) & 1 == 1, times(base, step), base)
            down = choose(((7 - eight) >> bit) & 1 == 1, times(down, step), down)
        for bit in range(3, 7):
            step = power_of(bit, p)
            more, most = (times(base, step), times(down, step))
            base = (over(base[0], more[0]), over(base[1], more[1]))
            down = (over(most[0], down[0]), over(most[1], down[1]))
        s.base_kept[p] = beside(*base)
        s.down_kept[p] = beside(*down)
        put_table(s.down, p, down)

    def tables_middle(p):
        base = split(s.base_kept[p])
        up = times(base, (s.lead[0, pl.ds(p, 1), :], s.lead[1, pl.ds(p, 1), :]))
        put_table(s.up, p, (up[0], -up[1]))
        weights = beside(s.coeff[0, pl.ds(p, 1), :], -s.coeff[1, pl.ds(p, 1), :])
        weights = jnp.broadcast_to(weights, (8, 2 * BLOCK))
        pick = lax.rem(lax.broadcasted_iota(jnp.int32, (8, 2 * BLOCK), 1), BLOCK) < states
        pick = pick == (lax.broadcasted_iota(jnp.int32, (8, 2 * BLOCK), 0) == 0)
        weights, base = (two(jnp.where(pick, weights, 0.0)), two(beside(*base)))
        kernel = folded(over(*weights), base[0], TURNED) + dot(weights[0], base[1], TURNED)
        for i in range(2):
            slanted = jnp.broadcast_to(kernel[i : i + 1], square)
            slanted = pltpu.roll(slanted, 0, 1, stride=1, stride_axis=0)
            side = slice(i * BLOCK, (i + 1) * BLOCK)
            for part, value in enumerate(two(jnp.where(lane_id >= row_id, slanted, 0.0))):
                s.toeplitz[p, part, side, side] = value

    def tables_second(p):
        base, down = (split(s.base_kept[p]), split(s.down_kept[p]))
        back = times(down, (s.lead[0, pl.ds(p, 1), :], s.lead[1, pl.ds(p, 1), :]))
        put_table(s.base, p, base)
        put_table(s.back, p, (back[0], -back[1]))
        for ref, value, slope in (
            (s.base_ramp, base, ramp + 1.0),
            (s.down_ramp, down, BLOCK - 1.0 - ramp),
        ):
            ref[p] = stacked(beside(value[0] * slope, value[1] * slope).astype(BF16))

    def over_couples(k, body, group=GROUP):
        def some(g, carry):
            for u in range(group):
                body(k * couples + g * group + u, g * group + u)
            return carry

        lax.fori_loop(0, couples // group, some, 0)

    for k in range(HALVES):
        over_couples(k, lambda p, c: tables_first(p))

    half_rows = count * members
    full_rows = blocks * half_rows
    place_of = lax.rem(lax.broadcasted_iota(jnp.int32, (half_rows, BLOCK), 0), local)
    place_lane = lax.broadcasted_iota(jnp.int32, (half_rows, BLOCK), 1)
    step_bit = 7 + blocks.bit_length() - 1

    def rows_in(ref, k):
        for m in range(count):
            for q in range(blocks):
                piece = ref[k, m, :, :, q * BLOCK : (q + 1) * BLOCK]
                s.stage_in[q, m, : members * own] = piece.astype(F32).reshape(members * own, BLOCK)

    def rows_out(ref, k):
        for m in range(count):
            for q in range(blocks):
                ref[k, m, :, :, q * BLOCK : (q + 1) * BLOCK] = (
                    s.stage_out[q, m, : members * own].astype(BF16).reshape(members, own, BLOCK)
                )

    def gather_couple(c):
        sides = []
        for i in range(2):
            sides.append(
                over(
                    *(
                        s.stage_in[q, m, pl.ds(2 * c + i, members, stride=own), :]
                        for q in range(blocks)
                        for m in range(count)
                    )
                )
            )
        return beside(*sides)

    def put_couple(c, value):
        for i, side in enumerate(split(value)):
            for q in range(blocks):
                for m in range(count):
                    first = (q * count + m) * members
                    s.stage_out[q, m, pl.ds(2 * c + i, members, stride=own), :] = side[first : first + members]

    def scalar_rows(i, p):
        return beside(s.scalars[i, pl.ds(2 * p, 1), :], s.scalars[i, pl.ds(2 * p + 1, 1), :])

    def by_block(value):
        return [split(value[q * half_rows : (q + 1) * half_rows]) for q in range(blocks)]

    def scan(flows, p, upward):
        block_step = power_of(7, p)
        flows = flows if upward else flows[::-1]
        total = flows[0]
        for flow in flows[1:]:
            total = plus(times(total, block_step), flow)

        def moved(value, reach):
            shift = reach if upward else half_rows - reach
            inside = place_of >= reach if upward else place_of < local - reach
            return tuple(jnp.where(inside, pltpu.roll(part, shift, 0), 0.0) for part in value)

        reach = 1
        while reach < local:
            total = plus(total, times(moved(total, reach), power_of(step_bit + reach.bit_length() - 1, p)))
            reach *= 2
        return moved(total, 1), total

    def carried(state, ref, scales, p, c, k, upward):
        scale = jnp.sum(jnp.where(carry_lane == c, scales[k], 0.0), axis=1, keepdims=True)
        lines = ref[p].astype(F32)
        lines = (lines[: count * groups] * scale, lines[count * groups :] * scale)
        for j in range(local):
            for i in range(2):
                s.widen[p, i, pl.ds(j, count * groups, stride=local), :] = lines[i]
        carry = (s.widen[p, 0, :half_rows], s.widen[p, 1, :half_rows])
        distance = place_of if upward else local - 1 - place_of
        for bit in range(local.bit_length() - 1):
            further = times(carry, power_of(step_bit + bit, p))
            carry = choose((distance >> bit) & 1 == 1, further, carry)
        return plus(state, carry)

    def through(state, flows, p, upward):
        block_step = power_of(7, p)
        listing = [state]
        flows = flows if upward else flows[::-1]
        for flow in flows[:-1]:
            state = plus(times(state, block_step), flow)
            listing.append(state)
        listing = listing if upward else listing[::-1]
        return over(*(beside(*state) for state in listing))

    def read_notes():
        wait_for(many(s.note_in), s.note_sem.at[1])
        notes = s.note_in[...].reshape(members, BLOCK)
        member_lane = lax.broadcasted_iota(jnp.int32, (members, BLOCK), 1)
        member_place = lax.rem(lax.broadcasted_iota(jnp.int32, (members, BLOCK), 0), local)
        start = (half * local + member_place) * span + member_lane
        for m in range(count):
            length = jnp.sum(jnp.where(member_lane == m, notes, 0.0), axis=1, keepdims=True)
            for q in range(blocks):
                first = (q * count + m) * members
                within = ((start + q * BLOCK).astype(F32) < length).astype(F32)
                s.mask[first : first + members] = beside(within, within)

    carry_lane = lax.broadcasted_iota(jnp.int32, (count * groups, BLOCK), 1)

    def pick_last(p, c, k, total, out, scales, first):
        lines = []
        for i in range(2):
            s.widen[p, i, :half_rows] = total[i]
            lines.append(s.widen[p, i, pl.ds(first, count * groups, stride=local), :])
        top = jnp.max(jnp.maximum(jnp.abs(lines[0]), jnp.abs(lines[1])), axis=1, keepdims=True)
        top = jnp.maximum(top, 1e-30)
        factor = STEPS / top
        out[p] = jnp.round(over(lines[0] * factor, lines[1] * factor)).astype(I16)
        scales[k] = jnp.where(carry_lane == c, top * (1.0 / STEPS), scales[k])

    def forward_first(k):
        for m in range(count):
            wait_for(many(s.x_in.at[k, m]), s.x_sem.at[k, m, 1])
        rows_in(s.x_in, k)

        def inflow(p, c):
            own_normed = gather_couple(c) * quantum
            drive = (own_normed * scalar_rows(0, p) + scalar_rows(1, p)) * s.mask[...]
            s.own_normed[p] = own_normed
            s.drive[p] = drive
            s.inflow[p] = product(two(drive), s.down[p])

        over_couples(k, inflow)

        s.carry_scale_out[k] = jnp.zeros((count * groups, BLOCK), F32)

        def scanned(p, c):
            state, total = scan(by_block(s.inflow[p]), p, True)
            s.entering[p, :half_rows] = beside(*state)
            pick_last(p, c, k, total, s.carry_out, s.carry_scale_out, local - 1)

        over_couples(k, scanned)
        rows = pl.ds(k * couples, couples)

        @pl.when(half == 0)
        def _():
            send(s.carry_out.at[rows], s.carry_in.at[rows], s.carry_sem.at[k, 0], partner)
            send(s.carry_scale_out.at[k], s.carry_scale_in.at[k], s.carry_sem.at[k, 1], partner)

    def forward_local(k):
        def nearby(p, c):
            drive = s.drive[p]
            s.response[p] = product(two(drive), s.toeplitz[p]) + scalar_rows(2, p) * drive

        over_couples(k, nearby)

    def share_below(response):
        return 0.5 * (1.0 + lax.erf(response * math.sqrt(0.5)))

    def slopes(p, c):
        response = s.response[p]
        density = jnp.exp(-0.5 * response * response) * (1.0 / math.sqrt(2.0 * math.pi))
        s.slope[p] = share_below(response) + response * density

    def forward_second(k):
        rows = pl.ds(k * couples, couples)

        @pl.when(half == 0)
        def _():
            s.carry_in[rows] = jnp.zeros((couples, 2 * count * groups, BLOCK), I16)
            s.carry_scale_in[k] = jnp.zeros((count * groups, BLOCK), F32)

        @pl.when(half == 1)
        def _():
            wait_for(s.carry_in.at[rows], s.carry_sem.at[k, 0, 1])
            wait_for(s.carry_scale_in.at[k], s.carry_sem.at[k, 1, 1])

        def complete(p, c):
            state = carried(
                split(s.entering[p, :half_rows]), s.carry_in, s.carry_scale_in, p, c, k, True
            )
            s.entering[p] = through(state, by_block(s.inflow[p]), p, True)

        over_couples(k, complete)

        def respond(p, c):
            response = s.response[p] + product(two(s.entering[p]), s.up[p], TURNED)
            s.response[p] = response
            put_couple(c, response * share_below(response))

        over_couples(k, respond)
        rows_out(s.a_out, k)
        for m in range(count):
            s.a_in[m, dp, k, pl.ds(here, 1)] = s.a_out[k, m, pl.ds(me, 1)]
            to_holders(s.a_out.at[k, m], s.a_in.at[m, :, k], s.a_sem.at[k, m])

    read_notes()
    over_couples(0, lambda p, c: tables_middle(p))
    weight_wait(0)
    weight_hop(1)
    over_couples(1, lambda p, c: tables_middle(p))
    for k in range(HALVES):
        forward_first(k)
    for k in range(HALVES):
        forward_local(k)
    for k in range(HALVES):
        forward_second(k)
        if k == 0:
            weight_wait(1)
            weight_hop(2)
    for k in range(HALVES):
        over_couples(k, lambda p, c: tables_second(p))

    for m in range(count):
        s.upstream[m] = out_grad[m].T
    weight_wait(2)
    for j in range(tiles):
        rows = slice(j * BLOCK, (j + 1) * BLOCK)
        per = BLOCK // own
        flat = s.weight[...].reshape(-1, own, wide + BLOCK)[j * per : (j + 1) * per].reshape(BLOCK, -1)
        s.flat[rows] = flat[:, :wide]
        s.flipped[:, rows] = flat[:, :wide].T
        shifts = flat[:, wide:].astype(F32)
        shifts = shifts + pltpu.roll(shifts, BLOCK - 2, 1) + pltpu.roll(shifts, BLOCK - 4, 1)
        for i in range(2):
            column = jnp.broadcast_to(shifts[:, i : i + 1], (BLOCK, BLOCK)).reshape(per, own, BLOCK)
            for n in range(per):
                first = ((j * per + n) * 2 + i) * own
                s.shift[first : first + own] = column[n]

    def project(m):
        for k in range(HALVES):
            ref = s.a_out.at[k, m, pl.ds(0, members - 1)]
            wait_for(ref, s.a_sem.at[k, m, 1])
        activated = s.a_in[m].reshape(width, span)
        valid = s.valid[m : m + 1]
        lanes = slice(m * span, (m + 1) * span)
        s.pre[...] = dot(s.flipped[...], activated)
        for j in range(tiles):
            rows = slice(j * BLOCK, (j + 1) * BLOCK)
            gates = slice(width + j * BLOCK, width + (j + 1) * BLOCK)
            value = s.pre[rows] + beside(*[s.shift[rows]] * blocks)
            gate = jax.nn.sigmoid(s.pre[gates] + beside(*[s.shift[gates]] * blocks))
            gated = s.upstream[m, rows].astype(F32) * valid
            s.pre_grad[rows, lanes] = (gated * gate).astype(BF16)
            s.pre_grad[gates, lanes] = (gated * value * gate * (1.0 - gate)).astype(BF16)
            s.result[m, rows] = (s.tokens[m, rows].astype(F32) + value * gate * valid).astype(BF16)
        s.act_grad[...] = dot(s.flat[...], s.pre_grad[:, lanes])
        largest = jnp.zeros((1, 1), F32)
        for j in range(tiles):
            piece = s.act_grad[j * BLOCK : (j + 1) * BLOCK]
            largest = jnp.maximum(largest, jnp.max(jnp.abs(piece), axis=(0, 1), keepdims=True))
        largest = jnp.maximum(largest, 1e-30)
        s.scale_out[m] = jnp.broadcast_to(largest * (1.0 / STEPS), (1, BLOCK))
        s.scale_in[m, pl.ds(me, 1)] = s.scale_out[m][None]
        to_all(s.scale_out.at[m], s.scale_in.at[m], s.scale_sem.at[m])
        factor = STEPS / largest
        for j in range(tiles):
            coded = jnp.round(s.act_grad[j * BLOCK : (j + 1) * BLOCK] * factor).astype(I16)
            for rows, a, k, p in chunk_rows(j):
                s.g_out[k, m, a, p] = coded[rows]
        for k in range(HALVES):
            s.g_in[k, m, pl.ds(me, 1)] = s.g_out[k, m, dp, pl.ds(here, 1)]
            to_owners(s.g_out.at[k, m], s.g_in.at[k, m], s.g_sem.at[k, m])
    def weight_gradient():
        ones = jnp.ones((count * span, BLOCK), BF16)
        per = width // groups
        lane4 = lax.broadcasted_iota(jnp.int32, (zs, 2, own, BLOCK), 3)
        for j in range(groups):
            activated = beside(*(s.a_in[m, j].reshape(per, span) for m in range(count)))
            piece = dot(activated, s.pre_grad[...], TURNED).reshape(zs, 2, own, wide)
            sums = dot(s.pre_grad[2 * j * per : 2 * (j + 1) * per], ones).reshape(zs, 2, 2, own, BLOCK)
            sums = jnp.where(lane4 == 0, sums[:, :, 0], jnp.where(lane4 == 1, sums[:, :, 1], 0.0))
            s.total[j, :, :, :, :wide] = piece
            s.total[j, :, :, :, wide:] = sums

    for m in range(count):
        project(m)
    weight_gradient()

    def sum_hop(hop):
        sems = s.sum_sem
        if hop == 0:
            send(s.total.at[:, :, 1 - core], s.sum_core, sems.at[0], (dp, z * 2 + 1 - core))
        elif hop == "ready":
            wait_for(s.sum_core, sems.at[0, 0])
            wait_for(s.sum_core, sems.at[0, 1])
            for j in range(groups):
                part = s.total[j, :, pl.ds(core, 1)].reshape(zs, own, -1) + s.sum_core[j]
                s.sum_core[j] = part
                s.sum_dp_out[j] = part.astype(BF16)
        elif hop == 1:
            for k in range(1, groups):
                there = lax.rem(dp + k, groups)
                send(s.sum_dp_out.at[there], s.sum_dp_in.at[dp], sems.at[1], (there, seq))
        elif hop == 2:
            ref = s.sum_dp_in.at[pl.ds(0, groups - 1)]
            wait_for(ref, sems.at[1, 0])
            wait_for(ref, sems.at[1, 1])
            part = s.sum_core[dp]
            for k in range(1, groups):
                part += s.sum_dp_in[lax.rem(dp + k, groups)].astype(F32)
            s.sum_core[0] = part
            s.sum_z_out[...] = part.astype(BF16)
            for k in range(1, zs):
                there = lax.rem(z + k, zs)
                send(s.sum_z_out.at[there], s.sum_z_in.at[z], sems.at[2], (dp, there * 2 + core))
        else:
            ref = s.sum_z_in.at[pl.ds(0, zs - 1)]
            wait_for(ref, sems.at[2, 0])
            wait_for(ref, sems.at[2, 1])
            part = s.sum_core[0, pl.ds(z, 1)].reshape(own, -1)
            for k in range(1, zs):
                part += s.sum_z_in[lax.rem(z + k, zs)].astype(F32)
            rows_grad[...] = part[:, :wide]
            columns = part[:, wide:].T
            shift_grad[...] = beside(columns[:1], columns[1:2])

    sum_hop(0)
    for k in range(HALVES):
        over_couples(k, slopes)
    sum_hop("ready")
    for m in range(count):
        result[m] = s.result[m].T

    def backward_first(k):
        for m in range(count):
            wait_for(many(s.g_in.at[k, m]), s.g_sem.at[k, m, 1])
            if k == 0:
                wait_for(many(s.scale_in.at[m]), s.scale_sem.at[m, 1])
                scale = s.scale_in[m].reshape(members, BLOCK)
                for q in range(blocks):
                    first = (q * count + m) * members
                    s.scales[first : first + members] = beside(scale, scale)
        if k == 0:
            sum_hop(1)
        rows_in(s.g_in, k)

        def outflow(p, c):
            grad = gather_couple(c) * s.scales[...] * s.slope[p]
            s.grad[p] = grad
            s.outflow[p] = product(two(grad), s.base[p])

        over_couples(k, outflow)

        s.back_scale_out[k] = jnp.zeros((count * groups, BLOCK), F32)

        def scanned(p, c):
            state, total = scan(by_block(s.outflow[p]), p, False)
            s.leaving[p, full_rows - half_rows :] = beside(*state)
            pick_last(p, c, k, total, s.back_out, s.back_scale_out, 0)

        over_couples(k, scanned)
        rows = pl.ds(k * couples, couples)

        @pl.when(half == 1)
        def _():
            send(s.back_out.at[rows], s.back_in.at[rows], s.back_sem.at[k, 0], partner)
            send(s.back_scale_out.at[k], s.back_scale_in.at[k], s.back_sem.at[k, 1], partner)

    def backward_local(k):
        def nearby(p, c):
            grad = s.grad[p]
            s.response[p] = product(two(grad), s.toeplitz[p], TURNED) + scalar_rows(2, p) * grad

        over_couples(k, nearby)

    def backward_second(k):
        rows = pl.ds(k * couples, couples)

        @pl.when(half == 1)
        def _():
            s.back_in[rows] = jnp.zeros((couples, 2 * count * groups, BLOCK), I16)
            s.back_scale_in[k] = jnp.zeros((count * groups, BLOCK), F32)

        @pl.when(half == 0)
        def _():
            wait_for(s.back_in.at[rows], s.back_sem.at[k, 0, 1])
            wait_for(s.back_scale_in.at[k], s.back_sem.at[k, 1, 1])

        def complete(p, c):
            state = carried(
                split(s.leaving[p, full_rows - half_rows :]), s.back_in, s.back_scale_in, p, c, k, False
            )
            s.leaving[p] = through(state, by_block(s.outflow[p]), p, False)

        over_couples(k, complete)

        def respond(p, c):
            grad = s.grad[p]
            drive_grad = s.response[p] + product(two(s.leaving[p]), s.back[p], TURNED)
            norm_grad = drive_grad * s.mask[...]
            for i, value in enumerate((norm_grad * s.own_normed[p], norm_grad, grad * s.drive[p])):
                for side, line in enumerate(split(total_rows(value))):
                    s.part[k, pl.ds(5 * couples + i * own + 2 * c + side, 1), :] = line
            put_couple(c, norm_grad * scalar_rows(0, p))

        over_couples(k, respond)
        rows_out(s.d_out, k)
        for m in range(count):
            s.d_in[m, dp, k, pl.ds(here, 1)] = s.d_out[k, m, pl.ds(me, 1)]
            to_holders(s.d_out.at[k, m], s.d_in.at[m, :, k], s.d_sem.at[k, m])

    for k in range(HALVES):
        backward_first(k)
    for k in range(HALVES):
        backward_local(k)
    for k in range(HALVES):
        backward_second(k)
    sum_hop(2)

    def sum_of_products(first, second):
        (a, b), (c, d) = (split(first), split(second))
        return (total_rows(a * c - b * d), total_rows(a * d + b * c))

    def lag_sums(p, c):
        drive, grad = (two(s.drive[p]), two(s.grad[p]))
        lines = []
        for side in range(2):
            lanes = slice(side * BLOCK, (side + 1) * BLOCK)
            left = over(drive[0][:, lanes], drive[1][:, lanes], drive[0][:, lanes])
            right = over(grad[0][:, lanes], grad[0][:, lanes], grad[1][:, lanes])
            cross = jnp.where(lane_id >= row_id, dot(left, right, SIDEWAYS), 0.0)
            lags = cross[:8]
            for i in range(1, BLOCK // 8):
                lags = lags + pltpu.roll(cross[8 * i : 8 * i + 8], BLOCK - 8 * i, 1)
            for bit in range(3):
                moved = pltpu.roll(lags, BLOCK - (1 << bit), 1)
                lags = jnp.where((row_id[:8] >> bit) & 1 == 1, moved, lags)
            lines.append(total_rows(lags))
        later = [jnp.where(row_lane < BLOCK - 1, pltpu.roll(line, BLOCK - 1, 1), 0.0) for line in lines]
        eight = lax.broadcasted_iota(jnp.int32, (8, 2 * BLOCK), 0)
        near = jnp.where(eight == 0, beside(*(line * shrink for line in lines)), beside(*later))
        s.lags[p] = near

    def correlate(p, c):
        drive, grad, near = (two(s.drive[p]), two(s.grad[p]), two(s.lags[p]))
        entering, leaving = (s.entering[p], s.leaving[p])
        second = folded(over(*drive), s.down_ramp[p])
        third = dot(over(*grad, *near), s.base_ramp[p])
        near = third[2 * full_rows : 2 * full_rows + 8] + third[2 * full_rows + 8 :]
        third = third[:full_rows] + third[full_rows : 2 * full_rows]
        moment = times(sum_of_products(entering, s.outflow[p]), power_of(0, p))
        moment = plus(moment, split(near[:1]))
        paired = times(sum_of_products(leaving, entering), power_of(7, p))
        paired = (paired[0] * float(BLOCK), paired[1] * float(BLOCK))
        paired = plus(paired, plus(sum_of_products(leaving, second), sum_of_products(entering, third)))
        paired = plus(paired, split(near[1:2]))
        for i, line in enumerate(moment + paired):
            s.sums[i, pl.ds(p, 1), :] = line

    shrink = 1.0 / (row_lane.astype(F32) + 1.0)
    def parameters(k):
        over_couples(k, lag_sums)
        over_couples(k, correlate)
        rows = pl.ds(pl.multiple_of(k * couples, couples), couples)
        moment, paired = ((s.sums[0, rows], s.sums[1, rows]), (s.sums[2, rows], s.sums[3, rows]))
        paired = times(paired, (s.coeff[0, rows], s.coeff[1, rows]))
        _, pull = jax.vjp(coefficient_parts, *(s.raw[i, rows] for i in range(5)))
        for i, grad in enumerate(pull((paired[0], -paired[1], moment[0], -moment[1]))):
            s.part[pl.ds(k, 1), i * couples : (i + 1) * couples] = grad[None]

    parameters(other)
    send(s.part.at[other], s.part_in, s.part_sem, partner)
    parameters(half)

    def norm_backward(m):
        for k in range(HALVES):
            wait_for(s.d_out.at[k, m, pl.ds(0, members - 1)], s.d_sem.at[k, m, 1])
        inverse = s.inverse[m : m + 1]
        scaled = s.d_in[m].reshape(width, span)
        plain = jnp.zeros((1, span), F32)
        along = jnp.zeros((1, span), F32)
        for j in range(tiles):
            rows = slice(j * BLOCK, (j + 1) * BLOCK)
            piece = scaled[rows].astype(F32)
            plain += total_rows(piece)
            along += total_rows(piece * s.normed[m, rows])
        plain, along = (plain * (1.0 / width), along * (1.0 / width))
        for j in range(tiles):
            rows = slice(j * BLOCK, (j + 1) * BLOCK)
            piece = scaled[rows].astype(F32) - plain - s.normed[m, rows] * along
            piece = s.upstream[m, rows].astype(F32) + inverse * piece
            token_grad[m, :, rows] = piece.astype(BF16).T

    for m in range(count):
        norm_backward(m)

    wait_for(s.part_in, s.part_sem.at[0])
    wait_for(s.part_in, s.part_sem.at[1])
    mine = s.part[half] + s.part_in[...]
    grads = [mine[i * couples : (i + 1) * couples] for i in range(5)]

    def uncoupled(value):
        s.turn[pl.ds(0, couples, stride=2), :] = value
        s.turn[pl.ds(1, couples, stride=2), :] = pltpu.roll(value, states, 1)
        return s.turn[:own]

    rate_grad[...] = uncoupled(grads[0])[:, :states]
    turn_grad[...] = uncoupled(grads[1])[:, :states]
    mix_low = own_lane < states
    mix_re = uncoupled(grads[3])
    mixing_grad[...] = jnp.where(mix_low, mix_re, pltpu.roll(uncoupled(grads[4]), states, 1))
    lines = [jnp.where(mix_low, uncoupled(grads[2]), 0.0)]
    lines += [mine[5 * couples + i * own : 5 * couples + (i + 1) * own] for i in range(3)]
    ones = jnp.ones((8, BLOCK), F32)
    for rows, out in zip(lines, (spacing_grad, gain_grad, bias_grad, skip_grad), strict=True):
        line = lax.dot_general(ones, rows, (TURNED, ((), ())), preferred_element_type=F32, precision=HIGH)
        out[...] = line[:1]

    sum_hop(3)

    wait_for(many(s.note_in), s.note_sem.at[0])
    for m in range(count):
        wait_for(many(s.scale_in.at[m]), s.scale_sem.at[m, 0])
        for k in range(HALVES):
            wait_for(many(s.x_in.at[k, m]), s.x_sem.at[k, m, 0])
            wait_for(many(s.a_out.at[k, m]), s.a_sem.at[k, m, 0])
            wait_for(many(s.g_in.at[k, m]), s.g_sem.at[k, m, 0])
            wait_for(many(s.d_out.at[k, m]), s.d_sem.at[k, m, 0])
    for k in range(HALVES):
        rows = pl.ds(k * couples, couples)

        @pl.when(half == 0)
        def _():
            wait_for(s.carry_out.at[rows], s.carry_sem.at[k, 0, 0])
            wait_for(s.carry_scale_out.at[k], s.carry_sem.at[k, 1, 0])

        @pl.when(half == 1)
        def _():
            wait_for(s.back_out.at[rows], s.back_sem.at[k, 0, 0])
            wait_for(s.back_scale_out.at[k], s.back_sem.at[k, 1, 0])


class Scratch:
    def __init__(self, names, refs):
        for name, ref in zip(names, refs, strict=True):
            setattr(self, name, ref)


def scratch_of(size, states):
    groups, parts, own, width, span, count = size
    local, blocks, zs = (parts // HALVES, span // BLOCK, parts // 2)
    members, couples = (groups * local, own // 2)
    every = HALVES * couples
    rows = blocks * count * members
    bits = 7 + (blocks * local).bit_length()
    wide = 2 * width + BLOCK
    vmem, sems = (pltpu.VMEM, pltpu.SemaphoreType.DMA)
    by_holder = (HALVES, count, groups, local, own, span)
    by_owner = (HALVES, count, members, own, span)
    filed = (count, groups, HALVES, local, own, span)
    chunk_sems = sems((HALVES, count, 2))
    held = vmem((every, rows, 2 * BLOCK), F32)
    table, plain = (vmem((every, 2, 2 * BLOCK, 2 * BLOCK), BF16), vmem((every, 2 * BLOCK, 2 * BLOCK), BF16))
    kept = vmem((every, BLOCK, 2 * BLOCK), F32)
    carry, carry_sems = (vmem((every, 2 * count * groups, BLOCK), I16), sems((HALVES, 2, 2)))
    carry_scale = vmem((HALVES, count * groups, BLOCK), F32)
    part_rows = 5 * couples + 3 * own
    return {
        "tokens": vmem((count, width, span), BF16),
        "upstream": vmem((count, width, span), BF16),
        "result": vmem((count, width, span), BF16),
        "normed": vmem((count, width, span), F32),
        "inverse": vmem((count, span), F32),
        "valid": vmem((count, span), F32),
        "x_out": vmem(by_holder, I16), "x_in": vmem(by_owner, I16), "x_sem": chunk_sems,
        "a_out": vmem(by_owner, BF16), "a_in": vmem(filed, BF16), "a_sem": chunk_sems,
        "g_out": vmem(by_holder, I16), "g_in": vmem(by_owner, I16), "g_sem": chunk_sems,
        "d_out": vmem(by_owner, BF16), "d_in": vmem(filed, BF16), "d_sem": chunk_sems,
        "note_out": vmem((1, 1, BLOCK), F32), "note_in": vmem((members, 1, BLOCK), F32), "note_sem": sems((2,)),
        "scale_out": vmem((count, 1, BLOCK), F32), "scale_in": vmem((count, members, 1, BLOCK), F32),
        "scale_sem": sems((count, 2)),
        "scales": vmem((rows, 2 * BLOCK), F32),
        "params": vmem((HALVES, own, 3 * BLOCK), F32), "params_sem": sems((2,)),
        "weight_out": vmem((own, wide), BF16),
        "weight": vmem((groups, zs, 2, own, wide), BF16), "weight_sem": sems((3, 2)),
        "flat": vmem((width, 2 * width), BF16),
        "flipped": vmem((2 * width, width), BF16),
        "shift": vmem((2 * width, BLOCK), F32),
        "pre_grad": vmem((2 * width, count * span), BF16),
        "pre": vmem((2 * width, span), F32),
        "act_grad": vmem((width, span), F32),
        "total": vmem((groups, zs, 2, own, wide), F32),
        "sum_core": vmem((groups, zs, own, wide), F32),
        "sum_dp_out": vmem((groups, zs, own, wide), BF16),
        "sum_dp_in": vmem((groups, zs, own, wide), BF16),
        "sum_z_out": vmem((zs, own, wide), BF16),
        "sum_z_in": vmem((zs, own, wide), BF16),
        "sum_sem": sems((3, 2)),
        "turn": vmem((own + 8, BLOCK), F32),
        "scalars": vmem((3, HALVES * own, BLOCK), F32),
        "power": vmem((bits, 2, every, BLOCK), F32),
        "lead": vmem((2, every, BLOCK), F32),
        "coeff": vmem((2, every, BLOCK), F32),
        "base": table, "down": table, "up": table, "back": table, "toeplitz": table,
        "base_ramp": plain, "down_ramp": plain, "base_kept": kept, "down_kept": kept, "response": held,
        "stage_in": vmem((blocks, count, (members + 1) * own, BLOCK), F32),
        "stage_out": vmem((blocks, count, (members + 1) * own, BLOCK), F32),
        "mask": vmem((rows, 2 * BLOCK), F32),
        "own_normed": held, "drive": held, "entering": held, "slope": held, "inflow": held,
        "grad": held, "outflow": held, "leaving": held,
        "widen": vmem((every, 2, count * members + 8, BLOCK), F32),
        "carry_out": carry, "carry_in": carry, "carry_sem": carry_sems,
        "back_out": carry, "back_in": carry, "back_sem": carry_sems,
        "carry_scale_out": carry_scale, "carry_scale_in": carry_scale,
        "back_scale_out": carry_scale, "back_scale_in": carry_scale,
        "sums": vmem((4, every, BLOCK), F32),
        "raw": vmem((5, every, BLOCK), F32), "lags": vmem((every, 8, 2 * BLOCK), F32),
        "part": vmem((HALVES, part_rows, BLOCK), F32), "part_in": vmem((part_rows, BLOCK), F32),
        "part_sem": sems((2,)),
    }


def handed_over(values):
    def kernel(*refs):
        for given, out in zip(refs[: len(values)], refs[len(values) :], strict=True):
            out[...] = given[...].reshape(out.shape)

    shapes = [(value.size,) if value.shape[0] == 1 else value.shape for value in values]
    return pl.pallas_call(
        kernel,
        out_shape=[jax.ShapeDtypeStruct(shape, value.dtype) for shape, value in zip(shapes, values, strict=True)],
        in_specs=[pl.BlockSpec(memory_space=pltpu.VMEM)] * len(values),
        out_specs=[pl.BlockSpec(memory_space=pltpu.VMEM)] * len(values),
    )(*values)


def in_one_kernel(groups, parts, *args):
    inputs, lengths, ln_gain, ln_bias, lam_log, lam_im, log_dt, mix_weight, skip, glu_weight, glu_bias, out_grad = args
    count, span, width = inputs.shape
    own = ln_gain.shape[0]
    size = (groups, parts, own, width, span, count)
    scratch = scratch_of(size, lam_log.shape[1])

    def kernel(*refs):
        arguments, results, kept = (refs[:12], refs[12:23], refs[23:])
        whole_kernel(size, *arguments, *results, Scratch(scratch, kept))

    vmem, smem = (pl.BlockSpec(memory_space=pltpu.VMEM), pl.BlockSpec(memory_space=pltpu.SMEM))
    line = jax.ShapeDtypeStruct((1, own), F32)
    outs = pl.pallas_call(
        kernel,
        out_shape=(
            jax.ShapeDtypeStruct(inputs.shape, BF16),
            jax.ShapeDtypeStruct(inputs.shape, BF16),
            line,
            line,
            jax.ShapeDtypeStruct(lam_log.shape, F32),
            jax.ShapeDtypeStruct(lam_im.shape, F32),
            line,
            jax.ShapeDtypeStruct(mix_weight.shape, F32),
            line,
            jax.ShapeDtypeStruct(glu_weight.shape, F32),
            jax.ShapeDtypeStruct((1, 2 * own), F32),
        ),
        in_specs=[vmem, smem, smem, smem, vmem, vmem, smem, vmem, smem, vmem, smem, vmem],
        out_specs=[vmem] * 11,
        scratch_shapes=list(scratch.values()),
        compiler_params=pltpu.CompilerParams(
            collective_id=0, has_side_effects=True, vmem_limit_bytes=62 * 1024 * 1024
        ),
    )(*args)
    return tuple(handed_over(outs))


def solution(mesh):
    tokens, vector, matrix = (P("dp", "seq", None), P(BOTH), P(BOTH, None))
    groups, parts = (mesh.shape["dp"], mesh.shape["seq"])

    def step(*args):
        own = args[2].shape[0]
        if own % 16 == 0 and parts % 4 == 0:
            return in_one_kernel(groups, parts, *args)
        return per_device(*args)

    return jax.shard_map(
        step,
        mesh=mesh,
        in_specs=(
            tokens, P("dp"), vector, vector, matrix, matrix, vector, matrix, vector, matrix, vector, tokens,
        ),
        out_specs=(
            tokens, tokens, vector, vector, matrix, matrix, vector, matrix, vector, matrix, vector,
        ),
        check_vma=False,
    )
```

```python
import math
from functools import partial

import jax
import jax.numpy as jnp
from jax import lax
from jax.experimental import pallas as pl
from jax.experimental.pallas import tpu as pltpu
from jax.sharding import PartitionSpec as P

BLOCK = 128
EPS = 1e-05
HIGH = lax.Precision.HIGHEST
BOTH = ("dp", "seq")


def halves(packed):
    count = packed.shape[-1] // 2
    return (packed[..., :count], packed[..., count:])


def cmul(first, second):
    first_re, first_im = halves(first)
    second_re, second_im = halves(second)
    return jnp.concatenate(
        [first_re * second_re - first_im * second_im, first_re * second_im + first_im * second_re],
        axis=-1,
    )


def conjugate(packed):
    real_half, imag_half = halves(packed)
    return jnp.concatenate([real_half, -imag_half], axis=-1)


def coefficients(lam_log, lam_im, log_dt, mix_weight):
    spacing = jnp.exp(log_dt)[:, None]
    rate = jnp.exp(lam_log)
    shrink = -rate * spacing
    angle = lam_im * spacing
    scale = jnp.exp(shrink)
    decay = jnp.concatenate([scale * jnp.cos(angle), scale * jnp.sin(angle)], axis=-1)
    less_re = jnp.expm1(shrink) * jnp.cos(angle) - 2.0 * jnp.sin(0.5 * angle) ** 2
    less_im = scale * jnp.sin(angle)
    modulus = rate * rate + lam_im * lam_im
    ratio = jnp.concatenate(
        [
            (lam_im * less_im - rate * less_re) / modulus,
            -(rate * less_im + lam_im * less_re) / modulus,
        ],
        axis=-1,
    )
    return (decay, cmul(mix_weight, ratio))


def powers(decay):
    real_half, imag_half = halves(decay)
    table = jnp.concatenate([jnp.ones_like(real_half), jnp.zeros_like(imag_half)], axis=-1)[:, None]
    step = decay[:, None]
    while table.shape[1] < BLOCK:
        table = jnp.concatenate([table, cmul(step, table)], axis=1)
        step = cmul(step, step)
    return (table, step[:, 0])


def link(earlier, later):
    return (cmul(earlier[0], later[0]), cmul(later[0], earlier[1]) + later[1])


def shifted(pieces, step, back):
    leads = jnp.broadcast_to(step[:, None, None], pieces.shape)
    _, reach = lax.associative_scan(link, (leads, pieces), axis=2, reverse=back)
    none = jnp.zeros_like(reach[:, :, :1])
    if back:
        return jnp.concatenate([reach[:, :, 1:], none], axis=2)
    return jnp.concatenate([none, reach[:, :, :-1]], axis=2)


def to_owner(rows):
    count, span, width = rows.shape
    groups, parts = (lax.axis_size("dp"), lax.axis_size("seq"))
    own = width // (groups * parts)
    sent = rows.reshape(count * span, width).T.reshape(-1, own, count, span)
    held = lax.all_to_all(sent, BOTH, 0, 0, tiled=True).reshape(groups, parts, own, count, span)
    held = held.transpose(2, 0, 3, 1, 4).reshape(own, groups * count, -1, BLOCK)
    return held


def to_holder(held, count, span):
    groups, parts = (lax.axis_size("dp"), lax.axis_size("seq"))
    own = held.shape[0]
    sent = held.astype(jnp.bfloat16).reshape(own, groups, count, parts, span).transpose(1, 3, 0, 2, 4)
    sent = sent.reshape(groups * parts, own, count, span)
    rows = lax.all_to_all(sent, BOTH, 0, 0, tiled=True)
    return rows.reshape(-1, count * span).T.reshape(count, span, -1).astype(jnp.float32)


def per_device(
    inputs,
    lengths,
    ln_gain,
    ln_bias,
    lam_log,
    lam_im,
    log_dt,
    mix_weight,
    skip,
    glu_weight,
    glu_bias,
    out_grad,
):
    count, span, width = inputs.shape
    offset = lax.axis_index("seq") * span
    positions = offset + jnp.arange(span, dtype=jnp.int32)
    valid = (positions[None, :] < lengths[:, None]).astype(jnp.float32)[..., None]
    rows = lax.all_gather(glu_weight, BOTH, axis=0, tiled=True)
    shift = lax.all_gather(glu_bias, BOTH, axis=0, tiled=True)
    spans = lax.all_gather(lengths, "dp", axis=0, tiled=True)
    whole_span = span * lax.axis_size("seq")
    mask = (jnp.arange(whole_span, dtype=jnp.int32)[None] < spans[:, None]).astype(jnp.float32)
    mask = mask.reshape(1, -1, whole_span // BLOCK, BLOCK)

    tokens = inputs.astype(jnp.float32)
    mean = jnp.mean(tokens, axis=-1, keepdims=True)
    centered = tokens - mean
    inverse = lax.rsqrt(jnp.mean(centered * centered, axis=-1, keepdims=True) + EPS)
    normed = centered * inverse

    (decay, coeff), coeff_pull = jax.vjp(coefficients, lam_log, lam_im, log_dt, mix_weight)
    base, whole = powers(decay)
    down = base[:, ::-1]
    real_half, imag_half = halves(coeff)
    kernel = jnp.einsum("cz,ckz->ck", conjugate(coeff), base, precision=HIGH)
    lead = cmul(coeff, decay)[:, None]
    up = conjugate(cmul(lead, base))
    back = conjugate(cmul(lead, down))
    steps = jnp.arange(BLOCK)
    lag = steps[:, None] - steps[None, :]
    toeplitz = jnp.where(lag >= 0, kernel[:, jnp.maximum(lag, 0)], 0.0)
    ramp = steps.astype(jnp.float32)[:, None]

    gain, bias, skipping = (p[:, None, None, None] for p in (ln_gain, ln_bias, skip))
    own_normed = to_owner(normed)
    drive = (own_normed * gain + bias) * mask
    entering = shifted(jnp.einsum("cbqj,cjz->cbqz", drive, down, precision=HIGH), whole, False)
    response = jnp.einsum("cij,cbqj->cbqi", toeplitz, drive, precision=HIGH)
    response += jnp.einsum("ciz,cbqz->cbqi", up, entering, precision=HIGH) + skipping * drive
    activated, gelu_pull = jax.vjp(partial(jax.nn.gelu, approximate=False), response)
    activated = to_holder(activated, count, span).astype(jnp.bfloat16).reshape(-1, width)
    pre = jnp.dot(activated, rows, preferred_element_type=jnp.float32) + shift
    gate = jax.nn.sigmoid(pre[:, width:])
    flat_valid = valid.reshape(-1, 1)
    result = (tokens + (pre[:, :width] * gate * flat_valid).reshape(tokens.shape)).astype(jnp.bfloat16)
    upstream = out_grad.astype(jnp.float32)
    gated = upstream.reshape(-1, width) * flat_valid
    pre_grad = jnp.concatenate(
        [gated * gate, gated * pre[:, :width] * gate * (1.0 - gate)], axis=-1
    ).astype(jnp.bfloat16)
    rows_grad = lax.dot_general(
        activated, pre_grad, (((0,), (0,)), ((), ())), preferred_element_type=jnp.float32
    )
    shift_grad = jnp.sum(pre_grad.astype(jnp.float32), axis=0)
    act_grad = lax.dot_general(
        pre_grad, rows, (((1,), (1,)), ((), ())), preferred_element_type=jnp.float32
    )
    response_grad = gelu_pull(to_owner(act_grad.reshape(tokens.shape)))[0]

    skip_grad = jnp.sum(response_grad * drive, axis=(1, 2, 3))
    outflow = jnp.einsum("cbqt,ctz->cbqz", response_grad, base, precision=HIGH)
    leaving = shifted(outflow, whole, True)
    drive_grad = jnp.einsum("cij,cbqi->cbqj", toeplitz, response_grad, precision=HIGH)
    drive_grad += jnp.einsum("cjz,cbqz->cbqj", back, leaving, precision=HIGH) + skipping * response_grad
    norm_grad = drive_grad * mask
    gain_grad = jnp.sum(norm_grad * own_normed, axis=(1, 2, 3))
    bias_grad = jnp.sum(norm_grad, axis=(1, 2, 3))
    scaled = to_holder(norm_grad * gain, count, span)
    token_grad = upstream + inverse * (
        scaled
        - jnp.mean(scaled, axis=-1, keepdims=True)
        - normed * jnp.mean(scaled * normed, axis=-1, keepdims=True)
    )

    cross = jnp.einsum("cbqj,cbqi->cij", drive, response_grad, precision=HIGH)
    lags = jnp.stack([jnp.trace(cross, offset=-k, axis1=1, axis2=2) for k in range(BLOCK)], axis=-1)
    second = jnp.einsum("cbqj,cjz->cbqz", drive, down * ramp[::-1], precision=HIGH)
    third = jnp.einsum("cbqt,ctz->cbqz", response_grad, base * (ramp + 1.0), precision=HIGH)
    total = partial(jnp.sum, axis=(1, 2))
    moment = cmul(decay, total(cmul(entering, outflow))) + jnp.einsum("ck,ckz->cz", lags, base, precision=HIGH)
    before = jnp.concatenate([jnp.zeros_like(base[:, :1]), base[:, :-1]], axis=1) * ramp
    paired = BLOCK * cmul(whole, total(cmul(leaving, entering)))
    paired += total(cmul(leaving, second) + cmul(entering, third))
    paired = cmul(coeff, paired + jnp.einsum("ck,ckz->cz", lags, before, precision=HIGH))
    rate_grad, turn_grad, spacing_grad, mixing_grad = coeff_pull((conjugate(paired), conjugate(moment)))

    scatter = partial(lax.psum_scatter, axis_name=BOTH, scatter_dimension=0, tiled=True)
    return (
        result,
        token_grad.astype(jnp.bfloat16),
        gain_grad,
        bias_grad,
        rate_grad,
        turn_grad,
        spacing_grad,
        mixing_grad,
        skip_grad,
        scatter(rows_grad),
        scatter(shift_grad),
    )


MESH = pl.DeviceIdType.MESH
F32, BF16, I16 = (jnp.float32, jnp.bfloat16, jnp.int16)
STEPS = 32700.0
GROUP = 8
HALVES = 2


def two(value):
    high = value.astype(BF16)
    return (high, (value - high.astype(F32)).astype(BF16))


def dot(left, right, dims=((1,), (0,))):
    return lax.dot_general(left, right, (dims, ((), ())), preferred_element_type=F32)


TURNED = ((1,), (1,))
SIDEWAYS = ((0,), (0,))


def product(left, table, dims=((1,), (0,))):
    return folded(over(*left), table[0], dims) + dot(left[0], table[1], dims)


def folded(rows, table, dims=((1,), (0,))):
    value = dot(rows, table, dims)
    half = value.shape[0] // 2
    return value[:half] + value[half:]


def times(value, factor):
    return (value[0] * factor[0] - value[1] * factor[1], value[0] * factor[1] + value[1] * factor[0])


def plus(first, second):
    return (first[0] + second[0], first[1] + second[1])


def choose(condition, first, second):
    return (jnp.where(condition, first[0], second[0]), jnp.where(condition, first[1], second[1]))


def split(value):
    return (value[:, :BLOCK], value[:, BLOCK:])


def beside(*parts):
    return jnp.concatenate(parts, axis=1)


def over(*parts):
    return jnp.concatenate(parts, axis=0)


def total_rows(value):
    return jnp.sum(value, axis=0, keepdims=True)


def small_expm1(value):
    near = jnp.abs(value) < 0.5
    small = jnp.where(near, value, 0.0)
    series = jnp.ones_like(small)
    for order in range(10, 1, -1):
        series = 1.0 + small * (1.0 / order) * series
    return jnp.where(near, small * series, jnp.exp(value) - 1.0)


def coefficient_parts(lam_log, lam_im, log_dt, mix_re, mix_im):
    spacing, rate = (jnp.exp(log_dt), jnp.exp(lam_log))
    shrink, angle = (-rate * spacing, lam_im * spacing)
    scale = jnp.exp(shrink)
    cosine, sine, half = (jnp.cos(angle), jnp.sin(angle), jnp.sin(0.5 * angle))
    less_re = small_expm1(shrink) * cosine - 2.0 * half * half
    less_im = scale * sine
    modulus = rate * rate + lam_im * lam_im
    ratio = (
        (lam_im * less_im - rate * less_re) / modulus,
        -(rate * less_im + lam_im * less_re) / modulus,
    )
    return (scale * cosine, less_im) + times((mix_re, mix_im), ratio)


def whole_kernel(
    size,
    inputs, lengths, ln_gain, ln_bias, lam_log, lam_im, log_dt, mix_weight, skip, glu_weight, glu_bias, out_grad,
    result, token_grad, gain_grad, bias_grad, rate_grad, turn_grad, spacing_grad, mixing_grad, skip_grad,
    rows_grad, shift_grad,
    s,
):
    groups, parts, own, width, span, count = size
    local, blocks, zs = (parts // HALVES, span // BLOCK, parts // 2)
    members = groups * local
    tiles, couples, states = (width // BLOCK, own // 2, lam_log.shape[1])
    wide = 2 * width
    dp, seq = (lax.axis_index("dp"), lax.axis_index("seq"))
    core, z = (lax.rem(seq, 2), seq // 2)
    half, here = (seq // local, lax.rem(seq, local))
    other = 1 - half
    me = dp * local + here
    partner = (dp, other * local + here)

    def place(member):
        return (member // local, half * local + lax.rem(member, local))

    def send(source, target, sems, device):
        pltpu.make_async_remote_copy(
            src_ref=source, dst_ref=target, send_sem=sems.at[0], recv_sem=sems.at[1],
            device_id=device, device_id_type=MESH,
        ).start()

    def wait_for(ref, sem):
        pltpu.make_async_copy(ref, ref, sem).wait()

    def to_owners(out, into, sems):
        for k in range(1, members):
            member = lax.rem(me + k, members)
            send(out.at[member // local, lax.rem(member, local)], into.at[me], sems, place(member))

    def to_holders(out, into, sems):
        for k in range(1, members):
            member = lax.rem(me + k, members)
            send(out.at[member], into.at[dp, here], sems, place(member))

    def to_all(out, into, sems):
        for k in range(1, members):
            send(out, into.at[me], sems, place(lax.rem(me + k, members)))

    def many(ref):
        return ref.at[pl.ds(0, members - 1)]

    barrier = pltpu.get_barrier_semaphore()

    def greet(k, carry):
        member = place(lax.rem(me + k, members))
        pl.semaphore_signal(barrier, inc=1, device_id=member, device_id_type=MESH)
        return carry

    lax.fori_loop(1, members, greet, 0)
    for k in range(zs // HALVES):
        there = other * local + 2 * k + core
        pl.semaphore_signal(barrier, inc=1, device_id=(dp, there), device_id_type=MESH)

    lane = lax.broadcasted_iota(jnp.int32, (1, span), 1) + seq * span
    quantum = math.sqrt(width) / STEPS

    def chunk_rows(j):
        per = BLOCK // own
        for i in range(per):
            shard = j * per + i
            yield slice(i * own, (i + 1) * own), shard // parts, shard % parts // local, shard % local

    def norm(m):
        tokens = inputs[m].T
        s.tokens[m] = tokens
        total = jnp.zeros((1, span), F32)
        for j in range(tiles):
            total += total_rows(tokens[j * BLOCK : (j + 1) * BLOCK].astype(F32))
        mean = total * (1.0 / width)
        total = jnp.zeros((1, span), F32)
        for j in range(tiles):
            off = tokens[j * BLOCK : (j + 1) * BLOCK].astype(F32) - mean
            total += total_rows(off * off)
        inverse = lax.rsqrt(total * (1.0 / width) + EPS)
        valid = (lane < lengths[m]).astype(F32)
        s.inverse[m : m + 1] = inverse
        s.valid[m : m + 1] = valid
        for j in range(tiles):
            normed = (tokens[j * BLOCK : (j + 1) * BLOCK].astype(F32) - mean) * inverse
            s.normed[m, j * BLOCK : (j + 1) * BLOCK] = normed
            coded = jnp.round(normed * valid * (1.0 / quantum)).astype(I16)
            for rows, a, k, p in chunk_rows(j):
                s.x_out[k, m, a, p] = coded[rows]
        for k in range(HALVES):
            s.x_in[k, m, pl.ds(me, 1)] = s.x_out[k, m, dp, pl.ds(here, 1)]

    for p in range(HALVES * couples):
        for part in range(2):
            s.toeplitz[p, part, :BLOCK, BLOCK:] = jnp.zeros((BLOCK, BLOCK), BF16)
            s.toeplitz[p, part, BLOCK:, :BLOCK] = jnp.zeros((BLOCK, BLOCK), BF16)

    row_lane = lax.broadcasted_iota(jnp.int32, (1, BLOCK), 1)
    row = jnp.zeros((1, BLOCK), F32)
    for m in range(count):
        row = jnp.where(row_lane == m, lengths[m].astype(F32), row)
    s.note_out[0] = row
    s.note_in[pl.ds(me, 1)] = row[None]

    own_row = lax.broadcasted_iota(jnp.int32, (own, BLOCK), 0)
    own_lane = lax.broadcasted_iota(jnp.int32, (own, BLOCK), 1)
    scalars = jnp.zeros((own, BLOCK), F32)
    shifts = jnp.zeros((own, BLOCK), F32)
    for c in range(own):
        for i, ref in enumerate((log_dt, ln_gain, ln_bias, skip)):
            scalars = jnp.where((own_row == c) & (own_lane == i), ref[c], scalars)
        for i in range(2):
            shifts = jnp.where((own_row == c) & (own_lane % 2 == i), glu_bias[i * own + c], shifts)
    s.params[pl.ds(half, 1), :, :states] = lam_log[...][None]
    s.params[pl.ds(half, 1), :, states : 2 * states] = lam_im[...][None]
    s.params[pl.ds(half, 1), :, BLOCK : 2 * BLOCK] = mix_weight[...][None]
    s.params[pl.ds(half, 1), :, 2 * BLOCK :] = scalars[None]
    high = shifts.astype(BF16)
    rest = shifts - high.astype(F32)
    middle = rest.astype(BF16)
    lowest = (rest - middle.astype(F32)).astype(BF16)
    thirds = jnp.where(own_lane < 2, high, jnp.where(own_lane < 4, middle, lowest))
    s.weight_out[:, :wide] = glu_weight[...]
    s.weight_out[:, wide:] = thirds
    s.weight[pl.ds(dp, 1), pl.ds(z, 1), pl.ds(core, 1)] = s.weight_out[...][None, None, None]

    def weight_hop(hop):
        sems = s.weight_sem.at[hop]
        if hop == 0:
            for k in range(1, zs):
                there = lax.rem(z + k, zs)
                send(s.weight_out, s.weight.at[dp, z, core], sems, (dp, there * 2 + core))
        elif hop == 1:
            for k in range(1, groups):
                mine = s.weight.at[dp, :, core]
                send(mine, mine, sems, (lax.rem(dp + k, groups), seq))
        else:
            mine = s.weight.at[:, :, core]
            send(mine, mine, sems, (dp, z * 2 + 1 - core))

    def weight_wait(hop):
        if hop == 0:
            ref = s.weight.at[0, pl.ds(0, zs - 1), 0]
        elif hop == 1:
            ref = s.weight.at[pl.ds(0, groups - 1), :, 0]
        else:
            ref = s.weight.at[:, :, 0]
        wait_for(ref, s.weight_sem.at[hop, 0])
        wait_for(ref, s.weight_sem.at[hop, 1])

    pl.semaphore_wait(barrier, members - 1 + zs // HALVES)
    send(s.params.at[half], s.params.at[half], s.params_sem, partner)
    to_all(s.note_out.at[0], s.note_in, s.note_sem)
    weight_hop(0)
    for m in range(count):
        norm(m)
    for k in range(HALVES):
        for m in range(count):
            to_owners(s.x_out.at[k, m], s.x_in.at[k, m], s.x_sem.at[k, m])

    wait_for(s.params.at[0], s.params_sem.at[0])
    wait_for(s.params.at[0], s.params_sem.at[1])
    pair_low = lax.broadcasted_iota(jnp.int32, (couples, BLOCK), 1) < states

    def coupled(value):
        s.turn[:own] = value
        even = s.turn[pl.ds(0, couples, stride=2), :]
        odd = s.turn[pl.ds(1, couples, stride=2), :]
        return jnp.where(pair_low, even, pltpu.roll(odd, states, 1))

    def raw_params(k):
        packed = [s.params[k, :, i * BLOCK : (i + 1) * BLOCK] for i in range(3)]
        lam, mix, rest = packed
        log_step = jnp.broadcast_to(rest[:, :1], (own, BLOCK))
        return tuple(
            coupled(value)
            for value in (lam, pltpu.roll(lam, states, 1), log_step, mix, pltpu.roll(mix, states, 1))
        )

    for k in range(HALVES):
        rest = s.params[k, :, 2 * BLOCK :]
        for i in range(1, 4):
            s.scalars[i - 1, k * own : (k + 1) * own] = jnp.broadcast_to(rest[:, i : i + 1], (own, BLOCK))
        rows = slice(k * couples, (k + 1) * couples)
        for i, value in enumerate(raw_params(k)):
            s.raw[i, rows] = value
        parts_k = coefficient_parts(*(s.raw[i, rows] for i in range(5)))
        decay, coeff = (parts_k[:2], parts_k[2:])
        s.coeff[0, rows], s.coeff[1, rows] = coeff
        s.lead[0, rows], s.lead[1, rows] = times(coeff, decay)
        power = decay
        for bit in range(s.power.shape[0]):
            s.power[bit, 0, rows], s.power[bit, 1, rows] = power
            power = times(power, power)

    def power_of(bit, p):
        return (s.power[bit, 0, pl.ds(p, 1), :], s.power[bit, 1, pl.ds(p, 1), :])

    square = (BLOCK, BLOCK)
    row_id = lax.broadcasted_iota(jnp.int32, square, 0)
    lane_id = lax.broadcasted_iota(jnp.int32, square, 1)
    ramp = row_id.astype(F32)
    first_states = lax.rem(lax.broadcasted_iota(jnp.int32, (BLOCK, 2 * BLOCK), 1), BLOCK) < states

    def stacked(value):
        none = jnp.zeros_like(value)
        return over(jnp.where(first_states, value, none), jnp.where(first_states, none, value))

    def put_table(ref, p, value):
        for i, part in enumerate(two(beside(*value))):
            ref[p, i] = stacked(part)

    def tables_first(p):
        eight = row_id[:8]
        unit = (jnp.ones((8, BLOCK), F32), jnp.zeros((8, BLOCK), F32))
        base, down = (unit, unit)
        for bit in range(3):
            step = power_of(bit, p)
            base = choose((eight >> bit) & 1 == 1, times(base, step), base)
            down = choose(((7 - eight) >> bit) & 1 == 1, times(down, step), down)
        for bit in range(3, 7):
            step = power_of(bit, p)
            more, most = (times(base, step), times(down, step))
            base = (over(base[0], more[0]), over(base[1], more[1]))
            down = (over(most[0], down[0]), over(most[1], down[1]))
        s.base_kept[p] = beside(*base)
        s.down_kept[p] = beside(*down)
        put_table(s.down, p, down)

    def tables_middle(p):
        base = split(s.base_kept[p])
        up = times(base, (s.lead[0, pl.ds(p, 1), :], s.lead[1, pl.ds(p, 1), :]))
        put_table(s.up, p, (up[0], -up[1]))
        weights = beside(s.coeff[0, pl.ds(p, 1), :], -s.coeff[1, pl.ds(p, 1), :])
        weights = jnp.broadcast_to(weights, (8, 2 * BLOCK))
        pick = lax.rem(lax.broadcasted_iota(jnp.int32, (8, 2 * BLOCK), 1), BLOCK) < states
        pick = pick == (lax.broadcasted_iota(jnp.int32, (8, 2 * BLOCK), 0) == 0)
        weights, base = (two(jnp.where(pick, weights, 0.0)), two(beside(*base)))
        kernel = folded(over(*weights), base[0], TURNED) + dot(weights[0], base[1], TURNED)
        for i in range(2):
            slanted = jnp.broadcast_to(kernel[i : i + 1], square)
            slanted = pltpu.roll(slanted, 0, 1, stride=1, stride_axis=0)
            side = slice(i * BLOCK, (i + 1) * BLOCK)
            for part, value in enumerate(two(jnp.where(lane_id >= row_id, slanted, 0.0))):
                s.toeplitz[p, part, side, side] = value

    def tables_second(p):
        base, down = (split(s.base_kept[p]), split(s.down_kept[p]))
        back = times(down, (s.lead[0, pl.ds(p, 1), :], s.lead[1, pl.ds(p, 1), :]))
        put_table(s.base, p, base)
        put_table(s.back, p, (back[0], -back[1]))
        for ref, value, slope in (
            (s.base_ramp, base, ramp + 1.0),
            (s.down_ramp, down, BLOCK - 1.0 - ramp),
        ):
            ref[p] = stacked(beside(value[0] * slope, value[1] * slope).astype(BF16))

    def over_couples(k, body, group=GROUP):
        def some(g, carry):
            for u in range(group):
                body(k * couples + g * group + u, g * group + u)
            return carry

        lax.fori_loop(0, couples // group, some, 0)

    for k in range(HALVES):
        over_couples(k, lambda p, c: tables_first(p))

    half_rows = count * members
    full_rows = blocks * half_rows
    place_of = lax.rem(lax.broadcasted_iota(jnp.int32, (half_rows, BLOCK), 0), local)
    place_lane = lax.broadcasted_iota(jnp.int32, (half_rows, BLOCK), 1)
    step_bit = 7 + blocks.bit_length() - 1

    def rows_in(ref, k):
        for m in range(count):
            for q in range(blocks):
                piece = ref[k, m, :, :, q * BLOCK : (q + 1) * BLOCK]
                s.stage_in[q, m, : members * own] = piece.astype(F32).reshape(members * own, BLOCK)

    def rows_out(ref, k):
        for m in range(count):
            for q in range(blocks):
                ref[k, m, :, :, q * BLOCK : (q + 1) * BLOCK] = (
                    s.stage_out[q, m, : members * own].astype(BF16).reshape(members, own, BLOCK)
                )

    def gather_couple(c):
        sides = []
        for i in range(2):
            sides.append(
                over(
                    *(
                        s.stage_in[q, m, pl.ds(2 * c + i, members, stride=own), :]
                        for q in range(blocks)
                        for m in range(count)
                    )
                )
            )
        return beside(*sides)

    def put_couple(c, value):
        for i, side in enumerate(split(value)):
            for q in range(blocks):
                for m in range(count):
                    first = (q * count + m) * members
                    s.stage_out[q, m, pl.ds(2 * c + i, members, stride=own), :] = side[first : first + members]

    def scalar_rows(i, p):
        return beside(s.scalars[i, pl.ds(2 * p, 1), :], s.scalars[i, pl.ds(2 * p + 1, 1), :])

    def by_block(value):
        return [split(value[q * half_rows : (q + 1) * half_rows]) for q in range(blocks)]

    def scan(flows, p, upward):
        block_step = power_of(7, p)
        flows = flows if upward else flows[::-1]
        total = flows[0]
        for flow in flows[1:]:
            total = plus(times(total, block_step), flow)

        def moved(value, reach):
            shift = reach if upward else half_rows - reach
            inside = place_of >= reach if upward else place_of < local - reach
            return tuple(jnp.where(inside, pltpu.roll(part, shift, 0), 0.0) for part in value)

        reach = 1
        while reach < local:
            total = plus(total, times(moved(total, reach), power_of(step_bit + reach.bit_length() - 1, p)))
            reach *= 2
        return moved(total, 1), total

    def carried(state, ref, scales, p, c, k, upward):
        scale = jnp.sum(jnp.where(carry_lane == c, scales[k], 0.0), axis=1, keepdims=True)
        lines = ref[p].astype(F32)
        lines = (lines[: count * groups] * scale, lines[count * groups :] * scale)
        for j in range(local):
            for i in range(2):
                s.widen[p, i, pl.ds(j, count * groups, stride=local), :] = lines[i]
        carry = (s.widen[p, 0, :half_rows], s.widen[p, 1, :half_rows])
        distance = place_of if upward else local - 1 - place_of
        for bit in range(local.bit_length() - 1):
            further = times(carry, power_of(step_bit + bit, p))
            carry = choose((distance >> bit) & 1 == 1, further, carry)
        return plus(state, carry)

    def through(state, flows, p, upward):
        block_step = power_of(7, p)
        listing = [state]
        flows = flows if upward else flows[::-1]
        for flow in flows[:-1]:
            state = plus(times(state, block_step), flow)
            listing.append(state)
        listing = listing if upward else listing[::-1]
        return over(*(beside(*state) for state in listing))

    def read_notes():
        wait_for(many(s.note_in), s.note_sem.at[1])
        notes = s.note_in[...].reshape(members, BLOCK)
        member_lane = lax.broadcasted_iota(jnp.int32, (members, BLOCK), 1)
        member_place = lax.rem(lax.broadcasted_iota(jnp.int32, (members, BLOCK), 0), local)
        start = (half * local + member_place) * span + member_lane
        for m in range(count):
            length = jnp.sum(jnp.where(member_lane == m, notes, 0.0), axis=1, keepdims=True)
            for q in range(blocks):
                first = (q * count + m) * members
                within = ((start + q * BLOCK).astype(F32) < length).astype(F32)
                s.mask[first : first + members] = beside(within, within)

    carry_lane = lax.broadcasted_iota(jnp.int32, (count * groups, BLOCK), 1)

    def pick_last(p, c, k, total, out, scales, first):
        lines = []
        for i in range(2):
            s.widen[p, i, :half_rows] = total[i]
            lines.append(s.widen[p, i, pl.ds(first, count * groups, stride=local), :])
        top = jnp.max(jnp.maximum(jnp.abs(lines[0]), jnp.abs(lines[1])), axis=1, keepdims=True)
        top = jnp.maximum(top, 1e-30)
        factor = STEPS / top
        out[p] = jnp.round(over(lines[0] * factor, lines[1] * factor)).astype(I16)
        scales[k] = jnp.where(carry_lane == c, top * (1.0 / STEPS), scales[k])

    def forward_first(k):
        for m in range(count):
            wait_for(many(s.x_in.at[k, m]), s.x_sem.at[k, m, 1])
        rows_in(s.x_in, k)

        def inflow(p, c):
            own_normed = gather_couple(c) * quantum
            drive = (own_normed * scalar_rows(0, p) + scalar_rows(1, p)) * s.mask[...]
            s.own_normed[p] = own_normed
            s.drive[p] = drive
            s.inflow[p] = product(two(drive), s.down[p])

        over_couples(k, inflow)

        s.carry_scale_out[k] = jnp.zeros((count * groups, BLOCK), F32)

        def scanned(p, c):
            state, total = scan(by_block(s.inflow[p]), p, True)
            s.entering[p, :half_rows] = beside(*state)
            pick_last(p, c, k, total, s.carry_out, s.carry_scale_out, local - 1)

        over_couples(k, scanned)
        rows = pl.ds(k * couples, couples)

        @pl.when(half == 0)
        def _():
            send(s.carry_out.at[rows], s.carry_in.at[rows], s.carry_sem.at[k, 0], partner)
            send(s.carry_scale_out.at[k], s.carry_scale_in.at[k], s.carry_sem.at[k, 1], partner)

    def forward_local(k):
        def nearby(p, c):
            drive = s.drive[p]
            s.response[p] = product(two(drive), s.toeplitz[p]) + scalar_rows(2, p) * drive

        over_couples(k, nearby)

    def share_below(response):
        return 0.5 * (1.0 + lax.erf(response * math.sqrt(0.5)))

    def slopes(p, c):
        response = s.response[p]
        density = jnp.exp(-0.5 * response * response) * (1.0 / math.sqrt(2.0 * math.pi))
        s.slope[p] = share_below(response) + response * density

    def forward_second(k):
        rows = pl.ds(k * couples, couples)

        @pl.when(half == 0)
        def _():
            s.carry_in[rows] = jnp.zeros((couples, 2 * count * groups, BLOCK), I16)
            s.carry_scale_in[k] = jnp.zeros((count * groups, BLOCK), F32)

        @pl.when(half == 1)
        def _():
            wait_for(s.carry_in.at[rows], s.carry_sem.at[k, 0, 1])
            wait_for(s.carry_scale_in.at[k], s.carry_sem.at[k, 1, 1])

        def complete(p, c):
            state = carried(
                split(s.entering[p, :half_rows]), s.carry_in, s.carry_scale_in, p, c, k, True
            )
            s.entering[p] = through(state, by_block(s.inflow[p]), p, True)

        over_couples(k, complete)

        def respond(p, c):
            response = s.response[p] + product(two(s.entering[p]), s.up[p], TURNED)
            s.response[p] = response
            put_couple(c, response * share_below(response))

        over_couples(k, respond)
        rows_out(s.a_out, k)
        for m in range(count):
            s.a_in[m, dp, k, pl.ds(here, 1)] = s.a_out[k, m, pl.ds(me, 1)]
            to_holders(s.a_out.at[k, m], s.a_in.at[m, :, k], s.a_sem.at[k, m])

    read_notes()
    over_couples(0, lambda p, c: tables_middle(p))
    weight_wait(0)
    weight_hop(1)
    forward_first(0)
    over_couples(1, lambda p, c: tables_middle(p))
    forward_first(1)
    for k in range(HALVES):
        forward_local(k)
    for k in range(HALVES):
        forward_second(k)
        if k == 0:
            weight_wait(1)
            weight_hop(2)
    for k in range(HALVES):
        over_couples(k, lambda p, c: tables_second(p))

    for m in range(count):
        s.upstream[m] = out_grad[m].T
    weight_wait(2)
    for j in range(tiles):
        rows = slice(j * BLOCK, (j + 1) * BLOCK)
        per = BLOCK // own
        flat = s.weight[...].reshape(-1, own, wide + BLOCK)[j * per : (j + 1) * per].reshape(BLOCK, -1)
        s.flat[rows] = flat[:, :wide]
        s.flipped[:, rows] = flat[:, :wide].T
        shifts = flat[:, wide:].astype(F32)
        shifts = shifts + pltpu.roll(shifts, BLOCK - 2, 1) + pltpu.roll(shifts, BLOCK - 4, 1)
        for i in range(2):
            column = jnp.broadcast_to(shifts[:, i : i + 1], (BLOCK, BLOCK)).reshape(per, own, BLOCK)
            for n in range(per):
                first = ((j * per + n) * 2 + i) * own
                s.shift[first : first + own] = column[n]

    def project(m):
        for k in range(HALVES):
            ref = s.a_out.at[k, m, pl.ds(0, members - 1)]
            wait_for(ref, s.a_sem.at[k, m, 1])
        activated = s.a_in[m].reshape(width, span)
        valid = s.valid[m : m + 1]
        lanes = slice(m * span, (m + 1) * span)
        s.pre[...] = dot(s.flipped[...], activated)
        for j in range(tiles):
            rows = slice(j * BLOCK, (j + 1) * BLOCK)
            gates = slice(width + j * BLOCK, width + (j + 1) * BLOCK)
            value = s.pre[rows] + beside(*[s.shift[rows]] * blocks)
            gate = jax.nn.sigmoid(s.pre[gates] + beside(*[s.shift[gates]] * blocks))
            gated = s.upstream[m, rows].astype(F32) * valid
            s.pre_grad[rows, lanes] = (gated * gate).astype(BF16)
            s.pre_grad[gates, lanes] = (gated * value * gate * (1.0 - gate)).astype(BF16)
            s.result[m, rows] = (s.tokens[m, rows].astype(F32) + value * gate * valid).astype(BF16)
        s.act_grad[...] = dot(s.flat[...], s.pre_grad[:, lanes])
        largest = jnp.zeros((1, 1), F32)
        for j in range(tiles):
            piece = s.act_grad[j * BLOCK : (j + 1) * BLOCK]
            largest = jnp.maximum(largest, jnp.max(jnp.abs(piece), axis=(0, 1), keepdims=True))
        largest = jnp.maximum(largest, 1e-30)
        s.scale_out[m] = jnp.broadcast_to(largest * (1.0 / STEPS), (1, BLOCK))
        s.scale_in[m, pl.ds(me, 1)] = s.scale_out[m][None]
        to_all(s.scale_out.at[m], s.scale_in.at[m], s.scale_sem.at[m])
        factor = STEPS / largest
        for j in range(tiles):
            coded = jnp.round(s.act_grad[j * BLOCK : (j + 1) * BLOCK] * factor).astype(I16)
            for rows, a, k, p in chunk_rows(j):
                s.g_out[k, m, a, p] = coded[rows]
        for k in range(HALVES):
            s.g_in[k, m, pl.ds(me, 1)] = s.g_out[k, m, dp, pl.ds(here, 1)]
            to_owners(s.g_out.at[k, m], s.g_in.at[k, m], s.g_sem.at[k, m])
    def weight_gradient():
        ones = jnp.ones((count * span, BLOCK), BF16)
        per = width // groups
        lane4 = lax.broadcasted_iota(jnp.int32, (zs, 2, own, BLOCK), 3)
        for j in range(groups):
            activated = beside(*(s.a_in[m, j].reshape(per, span) for m in range(count)))
            piece = dot(activated, s.pre_grad[...], TURNED).reshape(zs, 2, own, wide)
            sums = dot(s.pre_grad[2 * j * per : 2 * (j + 1) * per], ones).reshape(zs, 2, 2, own, BLOCK)
            sums = jnp.where(lane4 == 0, sums[:, :, 0], jnp.where(lane4 == 1, sums[:, :, 1], 0.0))
            s.total[j, :, :, :, :wide] = piece
            s.total[j, :, :, :, wide:] = sums

    for m in range(count):
        project(m)
    weight_gradient()

    def sum_hop(hop):
        sems = s.sum_sem
        if hop == 0:
            send(s.total.at[:, :, 1 - core], s.sum_core, sems.at[0], (dp, z * 2 + 1 - core))
        elif hop == "ready":
            wait_for(s.sum_core, sems.at[0, 0])
            wait_for(s.sum_core, sems.at[0, 1])
            for j in range(groups):
                part = s.total[j, :, pl.ds(core, 1)].reshape(zs, own, -1) + s.sum_core[j]
                s.sum_core[j] = part
                s.sum_dp_out[j] = part.astype(BF16)
        elif hop == 1:
            for k in range(1, groups):
                there = lax.rem(dp + k, groups)
                send(s.sum_dp_out.at[there], s.sum_dp_in.at[dp], sems.at[1], (there, seq))
        elif hop == 2:
            ref = s.sum_dp_in.at[pl.ds(0, groups - 1)]
            wait_for(ref, sems.at[1, 0])
            wait_for(ref, sems.at[1, 1])
            part = s.sum_core[dp]
            for k in range(1, groups):
                part += s.sum_dp_in[lax.rem(dp + k, groups)].astype(F32)
            s.sum_core[0] = part
            s.sum_z_out[...] = part.astype(BF16)
            for k in range(1, zs):
                there = lax.rem(z + k, zs)
                send(s.sum_z_out.at[there], s.sum_z_in.at[z], sems.at[2], (dp, there * 2 + core))
        else:
            ref = s.sum_z_in.at[pl.ds(0, zs - 1)]
            wait_for(ref, sems.at[2, 0])
            wait_for(ref, sems.at[2, 1])
            part = s.sum_core[0, pl.ds(z, 1)].reshape(own, -1)
            for k in range(1, zs):
                part += s.sum_z_in[lax.rem(z + k, zs)].astype(F32)
            rows_grad[...] = part[:, :wide]
            columns = part[:, wide:].T
            shift_grad[...] = beside(columns[:1], columns[1:2])

    sum_hop(0)
    for k in range(HALVES):
        over_couples(k, slopes)
    sum_hop("ready")
    for m in range(count):
        result[m] = s.result[m].T

    def backward_first(k):
        for m in range(count):
            wait_for(many(s.g_in.at[k, m]), s.g_sem.at[k, m, 1])
            if k == 0:
                wait_for(many(s.scale_in.at[m]), s.scale_sem.at[m, 1])
                scale = s.scale_in[m].reshape(members, BLOCK)
                for q in range(blocks):
                    first = (q * count + m) * members
                    s.scales[first : first + members] = beside(scale, scale)
        if k == 0:
            sum_hop(1)
        rows_in(s.g_in, k)

        def outflow(p, c):
            grad = gather_couple(c) * s.scales[...] * s.slope[p]
            s.grad[p] = grad
            s.outflow[p] = product(two(grad), s.base[p])

        over_couples(k, outflow)

        s.back_scale_out[k] = jnp.zeros((count * groups, BLOCK), F32)

        def scanned(p, c):
            state, total = scan(by_block(s.outflow[p]), p, False)
            s.leaving[p, full_rows - half_rows :] = beside(*state)
            pick_last(p, c, k, total, s.back_out, s.back_scale_out, 0)

        over_couples(k, scanned)
        rows = pl.ds(k * couples, couples)

        @pl.when(half == 1)
        def _():
            send(s.back_out.at[rows], s.back_in.at[rows], s.back_sem.at[k, 0], partner)
            send(s.back_scale_out.at[k], s.back_scale_in.at[k], s.back_sem.at[k, 1], partner)

    def backward_local(k):
        def nearby(p, c):
            grad = s.grad[p]
            s.response[p] = product(two(grad), s.toeplitz[p], TURNED) + scalar_rows(2, p) * grad

        over_couples(k, nearby)

    def backward_second(k):
        rows = pl.ds(k * couples, couples)

        @pl.when(half == 1)
        def _():
            s.back_in[rows] = jnp.zeros((couples, 2 * count * groups, BLOCK), I16)
            s.back_scale_in[k] = jnp.zeros((count * groups, BLOCK), F32)

        @pl.when(half == 0)
        def _():
            wait_for(s.back_in.at[rows], s.back_sem.at[k, 0, 1])
            wait_for(s.back_scale_in.at[k], s.back_sem.at[k, 1, 1])

        def complete(p, c):
            state = carried(
                split(s.leaving[p, full_rows - half_rows :]), s.back_in, s.back_scale_in, p, c, k, False
            )
            s.leaving[p] = through(state, by_block(s.outflow[p]), p, False)

        over_couples(k, complete)

        def respond(p, c):
            grad = s.grad[p]
            drive_grad = s.response[p] + product(two(s.leaving[p]), s.back[p], TURNED)
            norm_grad = drive_grad * s.mask[...]
            for i, value in enumerate((norm_grad * s.own_normed[p], norm_grad, grad * s.drive[p])):
                for side, line in enumerate(split(total_rows(value))):
                    s.part[k, pl.ds(5 * couples + i * own + 2 * c + side, 1), :] = line
            put_couple(c, norm_grad * scalar_rows(0, p))

        over_couples(k, respond)
        rows_out(s.d_out, k)
        for m in range(count):
            s.d_in[m, dp, k, pl.ds(here, 1)] = s.d_out[k, m, pl.ds(me, 1)]
            to_holders(s.d_out.at[k, m], s.d_in.at[m, :, k], s.d_sem.at[k, m])

    for k in range(HALVES):
        backward_first(k)
    for k in range(HALVES):
        backward_local(k)
    for k in range(HALVES):
        backward_second(k)
    sum_hop(2)

    def sum_of_products(first, second):
        (a, b), (c, d) = (split(first), split(second))
        return (total_rows(a * c - b * d), total_rows(a * d + b * c))

    def lag_sums(p, c):
        drive, grad = (two(s.drive[p]), two(s.grad[p]))
        lines = []
        for side in range(2):
            lanes = slice(side * BLOCK, (side + 1) * BLOCK)
            left = over(drive[0][:, lanes], drive[1][:, lanes], drive[0][:, lanes])
            right = over(grad[0][:, lanes], grad[0][:, lanes], grad[1][:, lanes])
            cross = jnp.where(lane_id >= row_id, dot(left, right, SIDEWAYS), 0.0)
            lags = cross[:8]
            for i in range(1, BLOCK // 8):
                lags = lags + pltpu.roll(cross[8 * i : 8 * i + 8], BLOCK - 8 * i, 1)
            for bit in range(3):
                moved = pltpu.roll(lags, BLOCK - (1 << bit), 1)
                lags = jnp.where((row_id[:8] >> bit) & 1 == 1, moved, lags)
            lines.append(total_rows(lags))
        later = [jnp.where(row_lane < BLOCK - 1, pltpu.roll(line, BLOCK - 1, 1), 0.0) for line in lines]
        eight = lax.broadcasted_iota(jnp.int32, (8, 2 * BLOCK), 0)
        near = jnp.where(eight == 0, beside(*(line * shrink for line in lines)), beside(*later))
        s.lags[p] = near

    def correlate(p, c):
        drive, grad, near = (two(s.drive[p]), two(s.grad[p]), two(s.lags[p]))
        entering, leaving = (s.entering[p], s.leaving[p])
        second = folded(over(*drive), s.down_ramp[p])
        third = dot(over(*grad, *near), s.base_ramp[p])
        near = third[2 * full_rows : 2 * full_rows + 8] + third[2 * full_rows + 8 :]
        third = third[:full_rows] + third[full_rows : 2 * full_rows]
        moment = times(sum_of_products(entering, s.outflow[p]), power_of(0, p))
        moment = plus(moment, split(near[:1]))
        paired = times(sum_of_products(leaving, entering), power_of(7, p))
        paired = (paired[0] * float(BLOCK), paired[1] * float(BLOCK))
        paired = plus(paired, plus(sum_of_products(leaving, second), sum_of_products(entering, third)))
        paired = plus(paired, split(near[1:2]))
        for i, line in enumerate(moment + paired):
            s.sums[i, pl.ds(p, 1), :] = line

    shrink = 1.0 / (row_lane.astype(F32) + 1.0)
    def parameters(k):
        over_couples(k, lag_sums)
        over_couples(k, correlate)
        rows = pl.ds(pl.multiple_of(k * couples, couples), couples)
        moment, paired = ((s.sums[0, rows], s.sums[1, rows]), (s.sums[2, rows], s.sums[3, rows]))
        paired = times(paired, (s.coeff[0, rows], s.coeff[1, rows]))
        _, pull = jax.vjp(coefficient_parts, *(s.raw[i, rows] for i in range(5)))
        for i, grad in enumerate(pull((paired[0], -paired[1], moment[0], -moment[1]))):
            s.part[pl.ds(k, 1), i * couples : (i + 1) * couples] = grad[None]

    parameters(other)
    send(s.part.at[other], s.part_in, s.part_sem, partner)
    parameters(half)

    def norm_backward(m):
        for k in range(HALVES):
            wait_for(s.d_out.at[k, m, pl.ds(0, members - 1)], s.d_sem.at[k, m, 1])
        inverse = s.inverse[m : m + 1]
        scaled = s.d_in[m].reshape(width, span)
        plain = jnp.zeros((1, span), F32)
        along = jnp.zeros((1, span), F32)
        for j in range(tiles):
            rows = slice(j * BLOCK, (j + 1) * BLOCK)
            piece = scaled[rows].astype(F32)
            plain += total_rows(piece)
            along += total_rows(piece * s.normed[m, rows])
        plain, along = (plain * (1.0 / width), along * (1.0 / width))
        for j in range(tiles):
            rows = slice(j * BLOCK, (j + 1) * BLOCK)
            piece = scaled[rows].astype(F32) - plain - s.normed[m, rows] * along
            piece = s.upstream[m, rows].astype(F32) + inverse * piece
            token_grad[m, :, rows] = piece.astype(BF16).T

    for m in range(count):
        norm_backward(m)

    wait_for(s.part_in, s.part_sem.at[0])
    wait_for(s.part_in, s.part_sem.at[1])
    mine = s.part[half] + s.part_in[...]
    grads = [mine[i * couples : (i + 1) * couples] for i in range(5)]

    def uncoupled(value):
        s.turn[pl.ds(0, couples, stride=2), :] = value
        s.turn[pl.ds(1, couples, stride=2), :] = pltpu.roll(value, states, 1)
        return s.turn[:own]

    rate_grad[...] = uncoupled(grads[0])[:, :states]
    turn_grad[...] = uncoupled(grads[1])[:, :states]
    mix_low = own_lane < states
    mix_re = uncoupled(grads[3])
    mixing_grad[...] = jnp.where(mix_low, mix_re, pltpu.roll(uncoupled(grads[4]), states, 1))
    lines = [jnp.where(mix_low, uncoupled(grads[2]), 0.0)]
    lines += [mine[5 * couples + i * own : 5 * couples + (i + 1) * own] for i in range(3)]
    ones = jnp.ones((8, BLOCK), F32)
    for rows, out in zip(lines, (spacing_grad, gain_grad, bias_grad, skip_grad), strict=True):
        line = lax.dot_general(ones, rows, (TURNED, ((), ())), preferred_element_type=F32, precision=HIGH)
        out[...] = line[:1]

    sum_hop(3)

    wait_for(many(s.note_in), s.note_sem.at[0])
    for m in range(count):
        wait_for(many(s.scale_in.at[m]), s.scale_sem.at[m, 0])
        for k in range(HALVES):
            wait_for(many(s.x_in.at[k, m]), s.x_sem.at[k, m, 0])
            wait_for(many(s.a_out.at[k, m]), s.a_sem.at[k, m, 0])
            wait_for(many(s.g_in.at[k, m]), s.g_sem.at[k, m, 0])
            wait_for(many(s.d_out.at[k, m]), s.d_sem.at[k, m, 0])
    for k in range(HALVES):
        rows = pl.ds(k * couples, couples)

        @pl.when(half == 0)
        def _():
            wait_for(s.carry_out.at[rows], s.carry_sem.at[k, 0, 0])
            wait_for(s.carry_scale_out.at[k], s.carry_sem.at[k, 1, 0])

        @pl.when(half == 1)
        def _():
            wait_for(s.back_out.at[rows], s.back_sem.at[k, 0, 0])
            wait_for(s.back_scale_out.at[k], s.back_sem.at[k, 1, 0])


class Scratch:
    def __init__(self, names, refs):
        for name, ref in zip(names, refs, strict=True):
            setattr(self, name, ref)


def scratch_of(size, states):
    groups, parts, own, width, span, count = size
    local, blocks, zs = (parts // HALVES, span // BLOCK, parts // 2)
    members, couples = (groups * local, own // 2)
    every = HALVES * couples
    rows = blocks * count * members
    bits = 7 + (blocks * local).bit_length()
    wide = 2 * width + BLOCK
    vmem, sems = (pltpu.VMEM, pltpu.SemaphoreType.DMA)
    by_holder = (HALVES, count, groups, local, own, span)
    by_owner = (HALVES, count, members, own, span)
    filed = (count, groups, HALVES, local, own, span)
    chunk_sems = sems((HALVES, count, 2))
    held = vmem((every, rows, 2 * BLOCK), F32)
    table, plain = (vmem((every, 2, 2 * BLOCK, 2 * BLOCK), BF16), vmem((every, 2 * BLOCK, 2 * BLOCK), BF16))
    kept = vmem((every, BLOCK, 2 * BLOCK), F32)
    carry, carry_sems = (vmem((every, 2 * count * groups, BLOCK), I16), sems((HALVES, 2, 2)))
    carry_scale = vmem((HALVES, count * groups, BLOCK), F32)
    part_rows = 5 * couples + 3 * own
    return {
        "tokens": vmem((count, width, span), BF16),
        "upstream": vmem((count, width, span), BF16),
        "result": vmem((count, width, span), BF16),
        "normed": vmem((count, width, span), F32),
        "inverse": vmem((count, span), F32),
        "valid": vmem((count, span), F32),
        "x_out": vmem(by_holder, I16), "x_in": vmem(by_owner, I16), "x_sem": chunk_sems,
        "a_out": vmem(by_owner, BF16), "a_in": vmem(filed, BF16), "a_sem": chunk_sems,
        "g_out": vmem(by_holder, I16), "g_in": vmem(by_owner, I16), "g_sem": chunk_sems,
        "d_out": vmem(by_owner, BF16), "d_in": vmem(filed, BF16), "d_sem": chunk_sems,
        "note_out": vmem((1, 1, BLOCK), F32), "note_in": vmem((members, 1, BLOCK), F32), "note_sem": sems((2,)),
        "scale_out": vmem((count, 1, BLOCK), F32), "scale_in": vmem((count, members, 1, BLOCK), F32),
        "scale_sem": sems((count, 2)),
        "scales": vmem((rows, 2 * BLOCK), F32),
        "params": vmem((HALVES, own, 3 * BLOCK), F32), "params_sem": sems((2,)),
        "weight_out": vmem((own, wide), BF16),
        "weight": vmem((groups, zs, 2, own, wide), BF16), "weight_sem": sems((3, 2)),
        "flat": vmem((width, 2 * width), BF16),
        "flipped": vmem((2 * width, width), BF16),
        "shift": vmem((2 * width, BLOCK), F32),
        "pre_grad": vmem((2 * width, count * span), BF16),
        "pre": vmem((2 * width, span), F32),
        "act_grad": vmem((width, span), F32),
        "total": vmem((groups, zs, 2, own, wide), F32),
        "sum_core": vmem((groups, zs, own, wide), F32),
        "sum_dp_out": vmem((groups, zs, own, wide), BF16),
        "sum_dp_in": vmem((groups, zs, own, wide), BF16),
        "sum_z_out": vmem((zs, own, wide), BF16),
        "sum_z_in": vmem((zs, own, wide), BF16),
        "sum_sem": sems((3, 2)),
        "turn": vmem((own + 8, BLOCK), F32),
        "scalars": vmem((3, HALVES * own, BLOCK), F32),
        "power": vmem((bits, 2, every, BLOCK), F32),
        "lead": vmem((2, every, BLOCK), F32),
        "coeff": vmem((2, every, BLOCK), F32),
        "base": table, "down": table, "up": table, "back": table, "toeplitz": table,
        "base_ramp": plain, "down_ramp": plain, "base_kept": kept, "down_kept": kept, "response": held,
        "stage_in": vmem((blocks, count, (members + 1) * own, BLOCK), F32),
        "stage_out": vmem((blocks, count, (members + 1) * own, BLOCK), F32),
        "mask": vmem((rows, 2 * BLOCK), F32),
        "own_normed": held, "drive": held, "entering": held, "slope": held, "inflow": held,
        "grad": held, "outflow": held, "leaving": held,
        "widen": vmem((every, 2, count * members + 8, BLOCK), F32),
        "carry_out": carry, "carry_in": carry, "carry_sem": carry_sems,
        "back_out": carry, "back_in": carry, "back_sem": carry_sems,
        "carry_scale_out": carry_scale, "carry_scale_in": carry_scale,
        "back_scale_out": carry_scale, "back_scale_in": carry_scale,
        "sums": vmem((4, every, BLOCK), F32),
        "raw": vmem((5, every, BLOCK), F32), "lags": vmem((every, 8, 2 * BLOCK), F32),
        "part": vmem((HALVES, part_rows, BLOCK), F32), "part_in": vmem((part_rows, BLOCK), F32),
        "part_sem": sems((2,)),
    }


def handed_over(values):
    def kernel(*refs):
        for given, out in zip(refs[: len(values)], refs[len(values) :], strict=True):
            out[...] = given[...].reshape(out.shape)

    shapes = [(value.size,) if value.shape[0] == 1 else value.shape for value in values]
    return pl.pallas_call(
        kernel,
        out_shape=[jax.ShapeDtypeStruct(shape, value.dtype) for shape, value in zip(shapes, values, strict=True)],
        in_specs=[pl.BlockSpec(memory_space=pltpu.VMEM)] * len(values),
        out_specs=[pl.BlockSpec(memory_space=pltpu.VMEM)] * len(values),
    )(*values)


def in_one_kernel(groups, parts, *args):
    inputs, lengths, ln_gain, ln_bias, lam_log, lam_im, log_dt, mix_weight, skip, glu_weight, glu_bias, out_grad = args
    count, span, width = inputs.shape
    own = ln_gain.shape[0]
    size = (groups, parts, own, width, span, count)
    scratch = scratch_of(size, lam_log.shape[1])

    def kernel(*refs):
        arguments, results, kept = (refs[:12], refs[12:23], refs[23:])
        whole_kernel(size, *arguments, *results, Scratch(scratch, kept))

    vmem, smem = (pl.BlockSpec(memory_space=pltpu.VMEM), pl.BlockSpec(memory_space=pltpu.SMEM))
    line = jax.ShapeDtypeStruct((1, own), F32)
    outs = pl.pallas_call(
        kernel,
        out_shape=(
            jax.ShapeDtypeStruct(inputs.shape, BF16),
            jax.ShapeDtypeStruct(inputs.shape, BF16),
            line,
            line,
            jax.ShapeDtypeStruct(lam_log.shape, F32),
            jax.ShapeDtypeStruct(lam_im.shape, F32),
            line,
            jax.ShapeDtypeStruct(mix_weight.shape, F32),
            line,
            jax.ShapeDtypeStruct(glu_weight.shape, F32),
            jax.ShapeDtypeStruct((1, 2 * own), F32),
        ),
        in_specs=[vmem, smem, smem, smem, vmem, vmem, smem, vmem, smem, vmem, smem, vmem],
        out_specs=[vmem] * 11,
        scratch_shapes=list(scratch.values()),
        compiler_params=pltpu.CompilerParams(
            collective_id=0, has_side_effects=True, vmem_limit_bytes=62 * 1024 * 1024
        ),
    )(*args)
    return tuple(handed_over(outs))


def solution(mesh):
    tokens, vector, matrix = (P("dp", "seq", None), P(BOTH), P(BOTH, None))
    groups, parts = (mesh.shape["dp"], mesh.shape["seq"])

    def step(*args):
        own = args[2].shape[0]
        if own % 16 == 0 and parts % 4 == 0:
            return in_one_kernel(groups, parts, *args)
        return per_device(*args)

    return jax.shard_map(
        step,
        mesh=mesh,
        in_specs=(
            tokens, P("dp"), vector, vector, matrix, matrix, vector, matrix, vector, matrix, vector, tokens,
        ),
        out_specs=(
            tokens, tokens, vector, vector, matrix, matrix, vector, matrix, vector, matrix, vector,
        ),
        check_vma=False,
    )
```
